512 devices in a mesh: dp: 32 (over z, core), section: 4 (over y), shard: 4 (over x).
Axes of the slice: x: 4, y: 4, z: 16, core: 2. Of those that a mesh axis runs over, the one named last changes fastest.
Arguments:
- boards: int32 [512, 361], P(('dp', 'shard')), may hold values from 0 to 2
- neighbours: int32 [512, 10], P(('dp', 'shard')), may hold values from 0 to 1023
- counts: int32 [512], P(('dp', 'shard')), may hold values from 0 to 10
- database: bfloat16 [1024, 1024], P('shard'), may hold values from -6 to 6
- w_first: bfloat16 [1024, 1024], replicated, may hold values from -0.1875 to 0.1875
- w_second: bfloat16 [1024, 256], replicated, may hold values from -0.1875 to 0.1875
- embed: bfloat16 [3, 256], replicated, may hold values from -4 to 4
- conv_weight: bfloat16 [4, 2304, 256], P('section', None, 'shard'), may hold values from -0.125 to 0.125
- cotangent: bfloat16 [512, 361, 256], P(('dp', 'shard')), may hold values from -6 to 6
Outputs:
- w1_grad: bfloat16 [1024, 1024], P(('section', 'shard'))
- w2_grad: bfloat16 [1024, 256], P(('section', 'shard'))
- embed_grad: bfloat16 [3, 256], replicated
- conv_grad: bfloat16 [4, 2304, 256], P('section', None, 'shard')
The draws below stay inside these ranges and needn't reach their ends.
Inputs may be any that keep to these rules, and one draw needn't show every extreme that they name: Slots from counts[i] on are unused. `neighbours`: rows of database.
All inputs are finite; a program needn't handle non-finite values.
Results may differ from the reference program's by a relative error of at most 0.023.
Values may be sent and summed in bfloat16 or wider, within the bound.
No kernel may reach another device: no remote copies, remote signals or barrier semaphores. Data moves between devices by JAX's collectives and lax.ppermute only.
A program may use at most 128 MiB of HBM per device.

```python
import math
import jax
import jax.numpy as jnp
import numpy as np
from jax import lax

BOARD = 19
C = 256
E = 1024
K = 10
CELLS = 361
BLOCKS = 4
STATES = 512
DB_ROWS = 1024


def plant(result, stream_key, low, top_value):
    place = [jax.random.randint(jax.random.fold_in(stream_key, axis), (), 0, length) for axis, length in enumerate(result.shape)]
    widest = result.shape.index(max(result.shape))
    beside = place[:widest] + [(place[widest] + 1) % result.shape[widest]] + place[widest + 1:]
    return result.at[tuple(place)].set(low).at[tuple(beside)].set(top_value)


def shard_levels(own_key, dims, cuts, least, high):
    def one(axis_at, parts):
        draws = jax.random.uniform(jax.random.fold_in(jax.random.fold_in(own_key, 6), axis_at), (parts,), jnp.float32, least / len(cuts), high / len(cuts))
        return jnp.repeat(jnp.exp(draws), dims[axis_at] // parts).reshape((-1,) + (1,) * (len(dims) - axis_at - 1))

    factor_of = one(*cuts[0])
    for cut in cuts[1:]:
        factor_of = factor_of * one(*cut)
    return factor_of


def rank_bounds(count, lean):
    loads = [(1 << 20) // math.isqrt(rank ** lean) + 1 for rank in range(1, count + 1)]
    scale = 1 + sum(loads) // (1 << 30)
    return np.cumsum(np.array([max(1, weight // scale) for weight in loads]))


def ranked_ids(key, dims, number_of, lean):
    table = rank_bounds(number_of, lean)
    lot = jax.random.randint(jax.random.fold_in(key, 1), dims, 0, int(table[number_of - 1]))
    standing = jnp.searchsorted(jnp.asarray(table, jnp.int32), lot, side="right")
    return jax.random.permutation(jax.random.fold_in(key, 2), number_of)[standing].astype(jnp.int32)


def gaussian(own_key, extent, deviation, reach, cuts=(), kind=jnp.bfloat16):
    gain = shard_levels(own_key, extent, cuts, -0.22, 0.18) if cuts else 1.0
    array = jax.random.normal(own_key, extent, jnp.float32) * deviation * gain
    return jnp.minimum(jnp.maximum(array, -reach), reach).astype(kind)


def setup_inputs(seed: int = 0) -> dict:
    key_list = jax.random.split(jax.random.key(seed), 10)
    boards = plant(jax.random.randint(key_list[0], (STATES, CELLS), 0, 3), jax.random.fold_in(key_list[0], 1), 0, 2).astype(jnp.int32)
    neighbours = plant(ranked_ids(key_list[1], (STATES, K), DB_ROWS, 2), jax.random.fold_in(key_list[1], 3), 0, DB_ROWS - 1).astype(jnp.int32)
    counts = plant(jax.random.randint(key_list[2], (STATES,), 0, K + 1), jax.random.fold_in(key_list[2], 1), 0, K).astype(jnp.int32)
    database = gaussian(key_list[3], (DB_ROWS, E), 1.0, 6.0, ((0, 4),))
    w_first = gaussian(key_list[4], (E, E), E ** -0.5, 0.1875)
    w_second = gaussian(key_list[5], (E, C), E ** -0.5, 0.1875)
    embed = gaussian(key_list[6], (3, C), 1.0, 4.0)
    conv_weight = gaussian(key_list[7], (BLOCKS, 9 * C, C), (9 * C) ** -0.5, 0.125, ((0, 4), (2, 4)))
    cotangent = gaussian(key_list[8], (STATES, CELLS, C), 1.0, 6.0, ((0, 128),))
    return dict(boards=boards, neighbours=neighbours, counts=counts, database=database, w_first=w_first, w_second=w_second, embed=embed, conv_weight=conv_weight, cotangent=cotangent)


NORM_EPS = 1e-05

def tap_patches(stream):
    grid = stream.reshape(BOARD, BOARD, -1)
    padded = jnp.pad(grid, ((1, 1), (1, 1), (0, 0)))
    taps = [padded[a:a + BOARD, b:b + BOARD] for a in range(3) for b in range(3)]
    return jnp.concatenate(taps, axis=-1).reshape(BOARD * BOARD, -1)

def fold_taps(spread, channels):
    grid = spread.reshape(BOARD, BOARD, 9, channels)
    folded = jnp.zeros((BOARD + 2, BOARD + 2, channels), jnp.float32)
    for a in range(3):
        for b in range(3):
            folded = folded.at[a:a + BOARD, b:b + BOARD].add(grid[:, :, 3 * a + b])
    return folded[1:BOARD + 1, 1:BOARD + 1].reshape(BOARD * BOARD, channels)

def gelu_slope(value):
    normal_cdf = 0.5 * (1.0 + jax.scipy.special.erf(value * 0.7071067811865476))
    density = jnp.exp(-0.5 * value * value) * 0.3989422804014327
    return normal_cdf + value * density

def silu_slope(value):
    sigma = jax.nn.sigmoid(value)
    return sigma * (1.0 + value * (1.0 - sigma))

def reference(boards, neighbours, counts, database, w_first, w_second, embed, conv_weight, cotangent):
    states = boards.shape[0]
    channels = embed.shape[1]
    live = jnp.arange(K, dtype=jnp.int32)[None, :] < counts[:, None]
    fetched = database[neighbours].astype(jnp.float32)
    summed = lax.optimization_barrier(jnp.sum(jnp.where(live[:, :, None], fetched, 0.0), axis=1))
    context = (summed / jnp.maximum(counts, 1).astype(jnp.float32)[:, None]).astype(jnp.bfloat16)
    preact = jnp.dot(context, w_first, preferred_element_type=jnp.float32)
    hidden = jax.nn.gelu(preact, approximate=False).astype(jnp.bfloat16)
    encoded = jnp.dot(hidden, w_second, preferred_element_type=jnp.float32)
    onehot = (boards[:, :, None] == jnp.arange(3, dtype=jnp.int32)).astype(jnp.float32)
    stones = jnp.einsum('scv,vd->scd', onehot, embed.astype(jnp.float32))
    start = (stones + encoded[:, None, :]).astype(jnp.bfloat16)

    def one_state(accumulated, item):
        stream, grad, planes = item
        saved = []
        for block in range(BLOCKS):
            patches = tap_patches(stream)
            zconv = jnp.dot(patches, conv_weight[block], preferred_element_type=jnp.float32)
            rscale = lax.rsqrt(lax.optimization_barrier(jnp.mean(zconv * zconv, axis=-1, keepdims=True)) + NORM_EPS)
            normed = zconv * rscale
            saved.append((patches, normed, rscale))
            stream = (stream.astype(jnp.float32) + jax.nn.silu(normed)).astype(jnp.bfloat16)
        pieces = [None] * BLOCKS
        for block in reversed(range(BLOCKS)):
            patches, normed, rscale = saved[block]
            dnorm = grad.astype(jnp.float32) * silu_slope(normed)
            dconv = (rscale * (dnorm - normed * lax.optimization_barrier(jnp.mean(dnorm * normed, axis=-1, keepdims=True)))).astype(jnp.bfloat16)
            pieces[block] = jnp.dot(patches.T, dconv, preferred_element_type=jnp.float32)
            spread = jnp.dot(dconv, conv_weight[block].T, preferred_element_type=jnp.float32)
            grad = (grad.astype(jnp.float32) + fold_taps(spread, channels)).astype(jnp.bfloat16)
        enc_part = lax.optimization_barrier(jnp.sum(grad.astype(jnp.float32), axis=0))
        stone_part = jnp.einsum('cv,cd->vd', planes, grad.astype(jnp.float32))
        return (accumulated + jnp.stack(pieces), (enc_part, stone_part))
    initial = jnp.zeros((BLOCKS, 9 * channels, channels), jnp.float32)
    conv_total, (enc_sum, stone_sum) = lax.scan(one_state, initial, (start, cotangent, onehot))
    enc_grad = enc_sum.astype(jnp.bfloat16)
    stone_grad = stone_sum.astype(jnp.bfloat16)
    hidden_grad = jnp.dot(enc_grad, w_second.T, preferred_element_type=jnp.float32)
    pre_grad = (hidden_grad * gelu_slope(preact)).astype(jnp.bfloat16)
    inverse_states = 1.0 / states
    conv_grad = (conv_total * inverse_states).astype(jnp.bfloat16)
    w1_grad = (jnp.dot(context.T, pre_grad, preferred_element_type=jnp.float32) * inverse_states).astype(jnp.bfloat16)
    w2_grad = (jnp.dot(hidden.T, enc_grad, preferred_element_type=jnp.float32) * inverse_states).astype(jnp.bfloat16)
    embed_grad = (lax.optimization_barrier(jnp.sum(stone_grad.astype(jnp.float32), axis=0)) * inverse_states).astype(jnp.bfloat16)
    return (w1_grad, w2_grad, embed_grad, conv_grad)
```

```python
import functools

import jax
import jax.numpy as jnp
from jax import lax
from jax.experimental import pallas as pl
from jax.experimental.pallas import tpu as pltpu
from jax.sharding import PartitionSpec as P

BOARD = 19
PITCH = 20
ROWS = 384
FRONT = 24
NORM_EPS = 1e-05
XOR = (0, 1, 3, 2)
TAP_SHIFTS = [(a - 1) * PITCH + (b - 1) for a in range(3) for b in range(3)]
VMEM_BYTES = 58 * 1024 * 1024
F32 = jnp.float32
BF16 = jnp.bfloat16


def swap(block, axis, bits):
    return lax.ppermute(block, axis, [(i, i ^ bits) for i in range(lax.axis_size(axis))])


def turned(block, axis, distance):
    size = lax.axis_size(axis)
    return lax.ppermute(block, axis, [(i, (i + distance) % size) for i in range(size)])


def nn(left, right):
    return lax.dot_general(left, right, (((1,), (0,)), ((), ())), preferred_element_type=F32)


def nt(left, right):
    return lax.dot_general(left, right, (((1,), (1,)), ((), ())), preferred_element_type=F32)


def tn(left, right):
    return lax.dot_general(left, right, (((0,), (0,)), ((), ())), preferred_element_type=F32)


def vmem_call(kernel, outs, scratch, name, flops, moved):
    spec = pl.BlockSpec(memory_space=pltpu.VMEM)

    def call(scalars, *arrays):
        return pl.pallas_call(
            kernel,
            out_shape=outs,
            in_specs=[pl.BlockSpec(memory_space=pltpu.SMEM)] + [spec] * len(arrays),
            out_specs=tuple(spec for _ in outs),
            scratch_shapes=scratch,
            compiler_params=pltpu.CompilerParams(vmem_limit_bytes=VMEM_BYTES),
            cost_estimate=pl.CostEstimate(flops=flops, bytes_accessed=moved, transcendentals=0),
            name=name,
        )(scalars, *arrays)

    return call


def trunk_kernel(
    where, context, w_first, w_second, embed, code_col, code_row, cotangent,
    a_near, a_far, a_near2, a_far2, b_near, b_far, b_near2, b_far2,
    own_a_hi, own_a_lo, own_b_hi, own_b_lo, oth_a_hi, oth_a_lo, oth_b_hi, oth_b_lo, vectors,
    wt, patches, gt, normed, rscales, buf, grad,
):
    s, h, c = where[0], where[1], where[2]

    def rows_of(jx, core, part):
        return pl.ds(pl.multiple_of((h ^ XOR[jx]) * 64 + core * 32 + part * 16, 16), 16)

    for core, near, far in ((c, a_near, a_far), (1 - c, a_near2, a_far2)):
        for jy in range(4):
            for jx in range(4):
                source = near if jy < 2 else far
                wt[s ^ XOR[jy], rows_of(jx, core, 0), :] = source[(jy % 2) * 4 + jx]
    for core, near, far in ((c, b_near, b_far), (1 - c, b_near2, b_far2)):
        for jx in range(4):
            for jy in range(4):
                source = near if jx < 2 else far
                wt[s ^ XOR[jy], rows_of(jx, core, 1), :] = source[(jx % 2) * 4 + jy]

    point = lax.broadcasted_iota(jnp.int32, (ROWS, 1), 0)
    column = point - ((point * 3277) >> 16) * PITCH
    mask = jnp.where((column < BOARD) & (point < BOARD * PITCH), 1.0, 0.0).astype(F32)

    preact = nn(context[...], w_first[...])
    cdf = 0.5 * (1.0 + lax.erf(preact * 0.7071067811865476))
    hidden = (preact * cdf).astype(BF16)
    encoded = nn(hidden, w_second[...])
    code = code_col[...]
    stone = embed[...].astype(F32)
    stones = jnp.where(code == 0, stone[0:1], jnp.where(code == 1, stone[1:2], stone[2:3]))
    start = (stones + encoded[0:1]).astype(BF16).astype(F32) * mask

    buf[0:FRONT, :] = jnp.zeros((FRONT, buf.shape[1]), F32)
    buf[FRONT + ROWS :, :] = jnp.zeros((FRONT, buf.shape[1]), F32)
    buf[FRONT : FRONT + ROWS, :] = start
    channels = start.shape[1]

    def forward(block, carry):
        for tap, shift in enumerate(TAP_SHIFTS):
            patches[block, :, tap * channels : (tap + 1) * channels] = buf[
                FRONT + shift : FRONT + shift + ROWS, :
            ].astype(BF16)
        zconv = nt(patches[block], wt[block])
        rscale = lax.rsqrt(jnp.mean(zconv * zconv, axis=-1, keepdims=True) + NORM_EPS)
        value = zconv * rscale
        normed[block] = value
        rscales[block] = rscale
        stream = buf[FRONT : FRONT + ROWS, :] + value * jax.nn.sigmoid(value)
        buf[FRONT : FRONT + ROWS, :] = stream.astype(BF16).astype(F32) * mask
        return carry

    lax.fori_loop(0, 4, forward, 0)
    grad[...] = cotangent[...].astype(F32)

    def backward(step, carry):
        block = 3 - step
        value = normed[block]
        upper = grad[...]
        sigma = jax.nn.sigmoid(value)
        dnorm = upper * (sigma * (1.0 + value * (1.0 - sigma)))
        inner = jnp.mean(dnorm * value, axis=-1, keepdims=True)
        dconv = rscales[block] * (dnorm - value * inner)
        gt[block] = nn(dconv.T.astype(BF16), patches[block]).astype(BF16)
        buf[FRONT : FRONT + ROWS, :] = dconv.astype(BF16).astype(F32)
        total = upper
        for tap, shift in enumerate(TAP_SHIFTS):
            total += nn(
                buf[FRONT - shift : FRONT - shift + ROWS, :].astype(BF16),
                wt[block, :, tap * channels : (tap + 1) * channels],
            )
        grad[...] = total.astype(BF16).astype(F32) * mask
        return carry

    lax.fori_loop(0, 4, backward, 0)

    kind = lax.broadcasted_iota(jnp.int32, (16, ROWS), 0)
    codes = code_row[...]
    picked = ((kind < 3) & (codes == kind)) | ((kind == 3) & (codes < 3))
    sums = nn(jnp.where(picked, 1.0, 0.0).astype(BF16), grad[...].astype(BF16))
    rounded = sums.astype(BF16)
    density = jnp.exp(-0.5 * preact * preact) * 0.3989422804014327
    pre_grad = (nt(rounded, w_second[...]) * (cdf + preact * density)).astype(BF16)
    vectors[...] = jnp.zeros(vectors.shape, F32)
    vectors[0:1, 0:1024] = context[...].astype(F32)[0:1]
    vectors[0:1, 1024:2048] = hidden.astype(F32)[0:1]
    vectors[0:1, 2048:3072] = pre_grad.astype(F32)[3:4]
    for place, row in enumerate((3, 0, 1, 2)):
        first = 3072 + place * channels
        vectors[0:1, first : first + channels] = rounded.astype(F32)[row : row + 1]

    for core, pieces in (
        (c, (own_a_lo, own_a_hi, own_b_lo, own_b_hi)),
        (1 - c, (oth_a_lo, oth_a_hi, oth_b_lo, oth_b_hi)),
    ):
        for jy in range(4):
            for jx in range(4):
                block = s ^ XOR[jy]
                pieces[jy // 2][jy % 2, jx] = gt[block, rows_of(jx, core, 0), :]
                pieces[2 + jx // 2][jx % 2, jy] = gt[block, rows_of(jx, core, 1), :]


def pack_kernel(where, a_own, a_come, b_own, b_come, near, far, *rest):
    outs, whole, product = rest[:4], rest[4], rest[5]
    first = where[0] * 256 + where[1] * 64 + where[2] * 32
    low = where[3]
    lanes = pl.multiple_of((first // 128) * 128, 128)
    rows = pl.ds(pl.multiple_of(first - lanes, 32), 32)
    whole[:, :, 896:1024] = jnp.zeros((4, 32, 128), F32)

    def spread(place, block):
        width = block.shape[1]
        done = 0
        while done < width:
            group, inside = divmod(place + done, 896)
            take = min(width - done, 896 - inside)
            whole[group, :, inside : inside + take] = block[:, done : done + take]
            done += take

    conv = jnp.concatenate(
        [a_own[...].astype(F32) + a_come[...], b_own[...].astype(F32) + b_come[...]], axis=0
    )
    spread(0, conv)
    product[:, 0:1024] = tn(near[:, pl.ds(lanes, 128)], near[:, 2048:3072]) + tn(
        far[:, pl.ds(lanes, 128)], far[:, 2048:3072]
    )
    lanes2 = pl.multiple_of(lanes + 1024, 128)
    product[:, 1024:1280] = tn(near[:, pl.ds(lanes2, 128)], near[:, 3072:3328]) + tn(
        far[:, pl.ds(lanes2, 128)], far[:, 3072:3328]
    )
    spread(2304, product[rows, :])
    stones = jnp.sum(
        near[:, 3328:4096].astype(F32) + far[:, 3328:4096].astype(F32), axis=0, keepdims=True
    )
    for piece in range(6):
        row = piece // 4
        whole[piece % 4, row : row + 1, 896:1024] = stones[:, piece * 128 : (piece + 1) * 128]
    for k in range(4):
        outs[k][...] = whole[low ^ k].astype(BF16)


def split_kernel(where, own, one, two, three, *rest):
    outs, total = rest[:4], rest[4]
    high = where[4]
    total[...] = own[...].astype(F32) + one[...] + two[...] + three[...]
    for k in range(4):
        place = high ^ k
        rows = pl.ds(pl.multiple_of((place // 2) * 16, 16), 16)
        lanes = pl.ds(pl.multiple_of((place % 2) * 512, 512), 512)
        outs[k][...] = total[rows, lanes].astype(BF16)


def join_kernel(where, own, one, two, three, out):
    high = where[4]
    for k, piece in enumerate((own, one, two, three)):
        place = high ^ k
        rows = pl.ds(pl.multiple_of((place // 2) * 16, 16), 16)
        lanes = pl.ds(pl.multiple_of((place % 2) * 512, 512), 512)
        out[rows, lanes] = piece[...]


def finish_kernel(where, *rest):
    own, other = rest[0:4], rest[4:8]
    conv, first, second, stones, whole, rows3 = rest[8:]
    c, low = where[2], where[3]
    for core, pieces in ((c, own), (1 - c, other)):
        rows = pl.ds(pl.multiple_of(core * 32, 32), 32)
        for k in range(4):
            whole[low ^ k, rows, :] = pieces[k][...].astype(F32) * (1.0 / 512.0)
    for group in range(4):
        for out, start, width in ((conv, 0, 2304), (first, 2304, 1024), (second, 3328, 256)):
            begin = max(start, group * 896)
            end = min(start + width, (group + 1) * 896)
            if begin < end:
                out[:, begin - start : end - start] = whole[
                    group, :, begin - group * 896 : end - group * 896
                ].astype(BF16)
    for piece in range(6):
        row = piece // 4
        v, half = divmod(piece, 2)
        rows3[v : v + 1, half * 128 : (half + 1) * 128] = whole[
            piece % 4, row : row + 1, 896:1024
        ]
    stones[...] = rows3[0:3, :].astype(BF16)


def body(boards, neighbours, counts, database, w_first, w_second, embed, conv_weight, cotangent):
    h = lax.axis_index("shard")
    s = lax.axis_index("section")
    dp = lax.axis_index("dp")
    c, z = dp % 2, dp // 2
    where = jnp.stack([s, h, c, z % 4, z // 4]).astype(jnp.int32)
    channels = embed.shape[1]
    taps = conv_weight.shape[1]

    mine = lax.dynamic_slice_in_dim(conv_weight[0].T, c * 32, 32, 0).reshape(2, 16, taps)

    def gather(unit, first, second):
        block = unit[None]
        block = jnp.concatenate([block, swap(block, first, 1)])
        block = jnp.concatenate([block, swap(block, first, 3)])
        block = jnp.concatenate([block, swap(block, second, 1)])
        return block, swap(block, second, 3)

    a_near, a_far = gather(mine[0], "shard", "section")
    b_near, b_far = gather(mine[1], "section", "shard")
    weights = (
        a_near, a_far, swap(a_near, "dp", 1), swap(a_far, "dp", 1),
        b_near, b_far, swap(b_near, "dp", 1), swap(b_far, "dp", 1),
    )

    ids = lax.dynamic_slice_in_dim(neighbours, s, 1, 0)
    count = lax.dynamic_slice_in_dim(counts, s, 1, 0)
    asked = jnp.concatenate([ids, count[:, None]], axis=1)
    asked = jnp.concatenate([asked] + [turned(asked, "shard", d) for d in (1, 2, 3)])
    slots = ids.shape[1]
    live = lax.broadcasted_iota(jnp.int32, (4, slots), 1) < asked[:, slots:]
    stored = database.shape[0]
    positions = lax.broadcasted_iota(jnp.int32, (1, 1, stored), 2) + h * stored
    hits = (asked[:, :slots, None] == positions) & live[:, :, None]
    picks = jnp.sum(hits.astype(F32), axis=1).astype(BF16)
    partial = jnp.dot(picks, database, preferred_element_type=F32)
    summed = partial[0:1]
    for d in (1, 2, 3):
        summed = summed + turned(partial[d : d + 1], "shard", -d)
    context = (summed / jnp.maximum(count, 1).astype(F32)[:, None]).astype(BF16)
    context = jnp.broadcast_to(context, (16, context.shape[1]))

    board = lax.dynamic_index_in_dim(boards, s, 0, keepdims=False).reshape(BOARD, BOARD)
    code = jnp.pad(board, ((0, 0), (0, 1)), constant_values=3).reshape(-1)
    code = jnp.pad(code, (0, ROWS - BOARD * PITCH), constant_values=3)
    upper = lax.dynamic_index_in_dim(cotangent, s, 0, keepdims=False)
    upper = jnp.pad(upper.reshape(BOARD, BOARD, channels), ((0, 0), (0, 1), (0, 0)))
    upper = jnp.pad(upper.reshape(-1, channels), ((0, ROWS - BOARD * PITCH), (0, 0)))

    part = jax.ShapeDtypeStruct((2, 4, 16, taps), BF16)
    own_a_hi, own_a_lo, own_b_hi, own_b_lo, oth_a_hi, oth_a_lo, oth_b_hi, oth_b_lo, vectors = vmem_call(
        trunk_kernel,
        (part,) * 8 + (jax.ShapeDtypeStruct((8, 4096), F32),),
        [
            pltpu.VMEM((4, channels, taps), BF16),
            pltpu.VMEM((4, ROWS, taps), BF16),
            pltpu.VMEM((4, channels, taps), BF16),
            pltpu.VMEM((4, ROWS, channels), F32),
            pltpu.VMEM((4, ROWS, 1), F32),
            pltpu.VMEM((2 * FRONT + ROWS, channels), F32),
            pltpu.VMEM((ROWS, channels), F32),
        ],
        "trunk",
        12 * 2 * ROWS * taps * channels,
        16 << 20,
    )(where, context, w_first, w_second, embed, code[:, None], code[None, :], upper, *weights)

    def plus(kept, come):
        return (kept.astype(F32) + come.astype(F32)).astype(BF16)

    a_hi = plus(own_a_hi, swap(oth_a_hi, "dp", 1))
    b_hi = plus(own_b_hi, swap(oth_b_hi, "dp", 1))
    a_lo = plus(own_a_lo, swap(oth_a_lo, "dp", 1))
    b_lo = plus(own_b_lo, swap(oth_b_lo, "dp", 1))

    def scatter(low, high, first, second):
        block = plus(low, swap(high, first, 3))
        block = plus(block[0], swap(block[1], first, 1))
        block = plus(block[0:2], swap(block[2:4], second, 3))
        return block[0], swap(block[1], second, 1)

    a_own, a_come = scatter(a_lo, a_hi, "section", "shard")
    b_own, b_come = scatter(b_lo, b_hi, "shard", "section")

    rows = vectors[0:1].astype(BF16)
    rows = jnp.concatenate([rows, swap(rows, "shard", 1)])
    rows = jnp.concatenate([rows, swap(rows, "shard", 3)])
    rows = jnp.concatenate([rows, swap(rows, "section", 1)])
    rows = jnp.concatenate([rows, swap(rows, "section", 3)])
    group = jax.ShapeDtypeStruct((32, 1024), BF16)
    groups = vmem_call(
        pack_kernel,
        (group,) * 4,
        [pltpu.VMEM((4, 32, 1024), F32), pltpu.VMEM((128, 1280), F32)],
        "pack",
        4 * 32 * 128 * 1280,
        1 << 20,
    )(where, a_own, a_come, b_own, b_come, rows, swap(rows, "dp", 1))

    come = [swap(groups[k], "dp", 2 * k) for k in (1, 2, 3)]
    chunk = jax.ShapeDtypeStruct((16, 512), BF16)
    chunks = vmem_call(
        split_kernel, (chunk,) * 4, [pltpu.VMEM((32, 1024), F32)], "split", 1 << 17, 1 << 19
    )(where, groups[0], *come)
    come = [swap(chunks[k], "dp", 8 * k) for k in (1, 2, 3)]
    total = plus(plus(chunks[0], come[0]).astype(F32), plus(come[1], come[2]).astype(F32))
    come = [swap(total, "dp", 8 * k) for k in (1, 2, 3)]
    (joined,) = vmem_call(join_kernel, (group,), [], "join", 1 << 10, 1 << 18)(where, total, *come)
    own = [joined] + [swap(joined, "dp", 2 * k) for k in (1, 2, 3)]
    other = [swap(piece, "dp", 1) for piece in own]
    conv, w1_grad, w2_grad, embed_grad = vmem_call(
        finish_kernel,
        (
            jax.ShapeDtypeStruct((64, taps), BF16),
            jax.ShapeDtypeStruct((64, 1024), BF16),
            jax.ShapeDtypeStruct((64, channels), BF16),
            jax.ShapeDtypeStruct((3, channels), BF16),
        ),
        [pltpu.VMEM((4, 64, 1024), F32), pltpu.VMEM((8, channels), F32)],
        "finish",
        1 << 18,
        1 << 20,
    )(where, *own, *other)
    return (w1_grad, w2_grad, embed_grad, conv.T[None])


def solution(mesh):
    placed = (
        P(("dp", "shard"), None),
        P(("dp", "shard"), None),
        P(("dp", "shard")),
        P("shard", None),
        P(),
        P(),
        P(),
        P("section", None, "shard"),
        P(("dp", "shard"), None, None),
    )
    return jax.shard_map(
        body,
        mesh=mesh,
        in_specs=placed,
        out_specs=(
            P(("section", "shard"), None),
            P(("section", "shard"), None),
            P(),
            P("section", None, "shard"),
        ),
        check_vma=False,
    )
```

```python
import jax
import jax.numpy as jnp
from jax import lax
from jax.experimental import pallas as pl
from jax.experimental.pallas import tpu as pltpu
from jax.sharding import PartitionSpec as P

BOARD = 19
PITCH = 20
ROWS = 384
FRONT = 24
NORM_EPS = 1e-05
TAP_SHIFTS = [(a - 1) * PITCH + (b - 1) for a in range(3) for b in range(3)]
VMEM_BYTES = 58 * 1024 * 1024
F32 = jnp.float32
BF16 = jnp.bfloat16


def swap(block, axis, bits):
    return lax.ppermute(block, axis, [(i, i ^ bits) for i in range(lax.axis_size(axis))])


def exchange(blocks, axis, groups=None):
    return lax.all_to_all(blocks, axis, 0, 0, axis_index_groups=groups, tiled=True)


def nn(left, right):
    return lax.dot_general(left, right, (((1,), (0,)), ((), ())), preferred_element_type=F32)


def nt(left, right):
    return lax.dot_general(left, right, (((1,), (1,)), ((), ())), preferred_element_type=F32)


def tn(left, right):
    return lax.dot_general(left, right, (((0,), (0,)), ((), ())), preferred_element_type=F32)


def vmem_call(kernel, outs, scratch, name, flops, moved):
    spec = pl.BlockSpec(memory_space=pltpu.VMEM)

    def call(scalars, *arrays):
        return pl.pallas_call(
            kernel,
            out_shape=outs,
            in_specs=[pl.BlockSpec(memory_space=pltpu.SMEM)] + [spec] * len(arrays),
            out_specs=tuple(spec for _ in outs),
            scratch_shapes=scratch,
            compiler_params=pltpu.CompilerParams(vmem_limit_bytes=VMEM_BYTES),
            cost_estimate=pl.CostEstimate(flops=flops, bytes_accessed=moved, transcendentals=0),
            name=name,
        )(scalars, *arrays)

    return call


def trunk_kernel(
    where, context, w_first, w_second, embed, code_col, code_row, cotangent, mine, theirs,
    own, other, vectors,
    wt, patches, gt, normed, rscales, buf, grad,
):
    c = where[2]

    def rows_of(shard, core):
        return pl.ds(pl.multiple_of(shard * 64 + core * 32, 32), 32)

    for core, pieces in ((c, mine), (1 - c, theirs)):
        for place in range(16):
            wt[place // 4, rows_of(place % 4, core), :] = pieces[place]

    point = lax.broadcasted_iota(jnp.int32, (ROWS, 1), 0)
    column = point - ((point * 3277) >> 16) * PITCH
    mask = jnp.where((column < BOARD) & (point < BOARD * PITCH), 1.0, 0.0).astype(F32)

    preact = nn(context[...], w_first[...])
    cdf = 0.5 * (1.0 + lax.erf(preact * 0.7071067811865476))
    hidden = (preact * cdf).astype(BF16)
    encoded = nn(hidden, w_second[...])
    code = code_col[...]
    stone = embed[...].astype(F32)
    stones = jnp.where(code == 0, stone[0:1], jnp.where(code == 1, stone[1:2], stone[2:3]))
    start = (stones + encoded[0:1]).astype(BF16).astype(F32) * mask

    buf[0:FRONT, :] = jnp.zeros((FRONT, buf.shape[1]), F32)
    buf[FRONT + ROWS :, :] = jnp.zeros((FRONT, buf.shape[1]), F32)
    buf[FRONT : FRONT + ROWS, :] = start
    channels = start.shape[1]

    def forward(block, carry):
        for tap, shift in enumerate(TAP_SHIFTS):
            patches[block, :, tap * channels : (tap + 1) * channels] = buf[
                FRONT + shift : FRONT + shift + ROWS, :
            ].astype(BF16)
        zconv = nt(patches[block], wt[block])
        rscale = lax.rsqrt(jnp.mean(zconv * zconv, axis=-1, keepdims=True) + NORM_EPS)
        value = zconv * rscale
        normed[block] = value
        rscales[block] = rscale
        stream = buf[FRONT : FRONT + ROWS, :] + value * jax.nn.sigmoid(value)
        buf[FRONT : FRONT + ROWS, :] = stream.astype(BF16).astype(F32) * mask
        return carry

    lax.fori_loop(0, 4, forward, 0)
    grad[...] = cotangent[...].astype(F32)

    def backward(step, carry):
        block = 3 - step
        value = normed[block]
        upper = grad[...]
        sigma = jax.nn.sigmoid(value)
        dnorm = upper * (sigma * (1.0 + value * (1.0 - sigma)))
        inner = jnp.mean(dnorm * value, axis=-1, keepdims=True)
        dconv = rscales[block] * (dnorm - value * inner)
        gt[block] = nn(dconv.T.astype(BF16), patches[block]).astype(BF16)
        buf[FRONT : FRONT + ROWS, :] = dconv.astype(BF16).astype(F32)
        total = upper
        for tap, shift in enumerate(TAP_SHIFTS):
            total += nn(
                buf[FRONT - shift : FRONT - shift + ROWS, :].astype(BF16),
                wt[block, :, tap * channels : (tap + 1) * channels],
            )
        grad[...] = total.astype(BF16).astype(F32) * mask
        return carry

    lax.fori_loop(0, 4, backward, 0)

    kind = lax.broadcasted_iota(jnp.int32, (16, ROWS), 0)
    codes = code_row[...]
    picked = ((kind < 3) & (codes == kind)) | ((kind == 3) & (codes < 3))
    sums = nn(jnp.where(picked, 1.0, 0.0).astype(BF16), grad[...].astype(BF16))
    rounded = sums.astype(BF16)
    density = jnp.exp(-0.5 * preact * preact) * 0.3989422804014327
    pre_grad = (nt(rounded, w_second[...]) * (cdf + preact * density)).astype(BF16)
    vectors[...] = jnp.zeros(vectors.shape, F32)
    vectors[0:1, 0:1024] = context[...].astype(F32)[0:1]
    vectors[0:1, 1024:2048] = hidden.astype(F32)[0:1]
    vectors[0:1, 2048:3072] = pre_grad.astype(F32)[3:4]
    for place, row in enumerate((3, 0, 1, 2)):
        first = 3072 + place * channels
        vectors[0:1, first : first + channels] = rounded.astype(F32)[row : row + 1]

    for core, pieces in ((c, own), (1 - c, other)):
        for place in range(16):
            pieces[place] = gt[place // 4, rows_of(place % 4, core), :]


def chunk_rows(piece):
    row = (piece % 4) // 2 * 16
    return slice(row, row + 16)


def chunk_lanes(piece):
    lane = piece % 2 * 512
    return slice(lane, lane + 512)


def pack_kernel(where, pieces, near, far, out, whole, product):
    first = where[0] * 256 + where[1] * 64 + where[2] * 32
    lanes = pl.multiple_of((first // 128) * 128, 128)
    rows = pl.ds(pl.multiple_of(first - lanes, 32), 32)
    whole[:, :, 896:1024] = jnp.zeros((4, 32, 128), F32)

    def spread(place, block):
        width = block.shape[1]
        done = 0
        while done < width:
            group, inside = divmod(place + done, 896)
            take = min(width - done, 896 - inside)
            whole[group, :, inside : inside + take] = block[:, done : done + take]
            done += take

    conv = pieces[0].astype(F32)
    for piece in range(1, 16):
        conv += pieces[piece].astype(F32)
    spread(0, conv)
    product[:, 0:1024] = tn(near[:, pl.ds(lanes, 128)], near[:, 2048:3072]) + tn(
        far[:, pl.ds(lanes, 128)], far[:, 2048:3072]
    )
    lanes2 = pl.multiple_of(lanes + 1024, 128)
    product[:, 1024:1280] = tn(near[:, pl.ds(lanes2, 128)], near[:, 3072:3328]) + tn(
        far[:, pl.ds(lanes2, 128)], far[:, 3072:3328]
    )
    spread(2304, product[rows, :])
    stones = jnp.sum(
        near[:, 3328:4096].astype(F32) + far[:, 3328:4096].astype(F32), axis=0, keepdims=True
    )
    for piece in range(6):
        row = piece // 4
        whole[piece % 4, row : row + 1, 896:1024] = stones[:, piece * 128 : (piece + 1) * 128]
    for piece in range(16):
        out[piece] = whole[piece // 4, chunk_rows(piece), chunk_lanes(piece)].astype(BF16)


def finish_kernel(where, mine, theirs, conv, first, second, stones, whole, rows3):
    c = where[2]
    for core, pieces in ((c, mine), (1 - c, theirs)):
        for piece in range(16):
            rows = pl.ds(pl.multiple_of(core * 32 + chunk_rows(piece).start, 16), 16)
            whole[piece // 4, rows, chunk_lanes(piece)] = pieces[piece].astype(F32) * (1.0 / 512.0)
    for group in range(4):
        for out, start, width in ((conv, 0, 2304), (first, 2304, 1024), (second, 3328, 256)):
            begin = max(start, group * 896)
            end = min(start + width, (group + 1) * 896)
            if begin < end:
                out[:, begin - start : end - start] = whole[
                    group, :, begin - group * 896 : end - group * 896
                ].astype(BF16)
    for piece in range(6):
        row = piece // 4
        v, half = divmod(piece, 2)
        rows3[v : v + 1, half * 128 : (half + 1) * 128] = whole[
            piece % 4, row : row + 1, 896:1024
        ]
    stones[...] = rows3[0:3, :].astype(BF16)


def body(boards, neighbours, counts, database, w_first, w_second, embed, conv_weight, cotangent):
    h = lax.axis_index("shard")
    s = lax.axis_index("section")
    dp = lax.axis_index("dp")
    c = dp % 2
    where = jnp.stack([s, h, c]).astype(jnp.int32)
    channels = embed.shape[1]
    taps = conv_weight.shape[1]
    plane = ("section", "shard")

    unit = lax.dynamic_slice_in_dim(conv_weight[0].T, c * 32, 32, 0)[None]
    mine = lax.all_gather(unit, plane, axis=0, tiled=True)
    theirs = swap(mine, "dp", 1)

    ids = lax.dynamic_slice_in_dim(neighbours, s, 1, 0)
    count = lax.dynamic_slice_in_dim(counts, s, 1, 0)
    asked = jnp.concatenate([ids, count[:, None]], axis=1)
    asked = exchange(jnp.broadcast_to(asked, (4, asked.shape[1])), "shard")
    slots = ids.shape[1]
    live = lax.broadcasted_iota(jnp.int32, (4, slots), 1) < asked[:, slots:]
    stored = database.shape[0]
    positions = lax.broadcasted_iota(jnp.int32, (1, 1, stored), 2) + h * stored
    hits = (asked[:, :slots, None] == positions) & live[:, :, None]
    picks = jnp.sum(hits.astype(F32), axis=1).astype(BF16)
    partial = jnp.dot(picks, database, preferred_element_type=F32)
    summed = jnp.sum(exchange(partial, "shard"), axis=0, keepdims=True)
    context = (summed / jnp.maximum(count, 1).astype(F32)[:, None]).astype(BF16)
    context = jnp.broadcast_to(context, (16, context.shape[1]))

    board = lax.dynamic_index_in_dim(boards, s, 0, keepdims=False).reshape(BOARD, BOARD)
    code = jnp.pad(board, ((0, 0), (0, 1)), constant_values=3).reshape(-1)
    code = jnp.pad(code, (0, ROWS - BOARD * PITCH), constant_values=3)
    upper = lax.dynamic_index_in_dim(cotangent, s, 0, keepdims=False)
    upper = jnp.pad(upper.reshape(BOARD, BOARD, channels), ((0, 0), (0, 1), (0, 0)))
    upper = jnp.pad(upper.reshape(-1, channels), ((0, ROWS - BOARD * PITCH), (0, 0)))

    part = jax.ShapeDtypeStruct((16, 32, taps), BF16)
    own, other, vectors = vmem_call(
        trunk_kernel,
        (part, part, jax.ShapeDtypeStruct((8, 4096), F32)),
        [
            pltpu.VMEM((4, channels, taps), BF16),
            pltpu.VMEM((4, ROWS, taps), BF16),
            pltpu.VMEM((4, channels, taps), BF16),
            pltpu.VMEM((4, ROWS, channels), F32),
            pltpu.VMEM((4, ROWS, 1), F32),
            pltpu.VMEM((2 * FRONT + ROWS, channels), F32),
            pltpu.VMEM((ROWS, channels), F32),
        ],
        "trunk",
        12 * 2 * ROWS * taps * channels,
        16 << 20,
    )(where, context, w_first, w_second, embed, code[:, None], code[None, :], upper, mine, theirs)

    pieces = (own.astype(F32) + swap(other, "dp", 1).astype(F32)).astype(BF16)
    pieces = exchange(pieces, plane)

    rows = lax.all_gather(vectors[0:1].astype(BF16), plane, axis=0, tiled=True)
    (chunks,) = vmem_call(
        pack_kernel,
        (jax.ShapeDtypeStruct((16, 16, 512), BF16),),
        [pltpu.VMEM((4, 32, 1024), F32), pltpu.VMEM((128, 1280), F32)],
        "pack",
        4 * 32 * 128 * 1280,
        3 << 20,
    )(where, pieces, rows, swap(rows, "dp", 1))

    line = [[2 * i + core for i in range(lax.axis_size("dp") // 2)] for core in (0, 1)]
    total = jnp.sum(exchange(chunks, "dp", line).astype(F32), axis=0, keepdims=True).astype(BF16)
    mine = exchange(jnp.broadcast_to(total, chunks.shape), "dp", line)
    conv, w1_grad, w2_grad, embed_grad = vmem_call(
        finish_kernel,
        (
            jax.ShapeDtypeStruct((64, taps), BF16),
            jax.ShapeDtypeStruct((64, 1024), BF16),
            jax.ShapeDtypeStruct((64, channels), BF16),
            jax.ShapeDtypeStruct((3, channels), BF16),
        ),
        [pltpu.VMEM((4, 64, 1024), F32), pltpu.VMEM((8, channels), F32)],
        "finish",
        1 << 18,
        1 << 20,
    )(where, mine, swap(mine, "dp", 1))
    return (w1_grad, w2_grad, embed_grad, conv.T[None])


def solution(mesh):
    placed = (
        P(("dp", "shard"), None),
        P(("dp", "shard"), None),
        P(("dp", "shard")),
        P("shard", None),
        P(),
        P(),
        P(),
        P("section", None, "shard"),
        P(("dp", "shard"), None, None),
    )
    return jax.shard_map(
        body,
        mesh=mesh,
        in_specs=placed,
        out_specs=(
            P(("section", "shard"), None),
            P(("section", "shard"), None),
            P(),
            P("section", None, "shard"),
        ),
        check_vma=False,
    )
```

```python
import jax
import jax.numpy as jnp
from jax import lax
from jax.experimental import pallas as pl
from jax.experimental.pallas import tpu as pltpu
from jax.sharding import PartitionSpec as P

BOARD = 19
PITCH = 20
ROWS = 384
FRONT = 24
NORM_EPS = 1e-05
TAP_SHIFTS = [(a - 1) * PITCH + (b - 1) for a in range(3) for b in range(3)]
VMEM_BYTES = 58 * 1024 * 1024
F32 = jnp.float32
BF16 = jnp.bfloat16


def swap(block, axis, bits):
    return lax.ppermute(block, axis, [(i, i ^ bits) for i in range(lax.axis_size(axis))])


def exchange(blocks, axis):
    return lax.all_to_all(blocks, axis, 0, 0, tiled=True)


def nn(left, right):
    return lax.dot_general(left, right, (((1,), (0,)), ((), ())), preferred_element_type=F32)


def nt(left, right):
    return lax.dot_general(left, right, (((1,), (1,)), ((), ())), preferred_element_type=F32)


def tn(left, right):
    return lax.dot_general(left, right, (((0,), (0,)), ((), ())), preferred_element_type=F32)


def vmem_call(kernel, outs, scratch, name, flops, moved):
    spec = pl.BlockSpec(memory_space=pltpu.VMEM)

    def call(scalars, *arrays):
        return pl.pallas_call(
            kernel,
            out_shape=outs,
            in_specs=[pl.BlockSpec(memory_space=pltpu.SMEM)] + [spec] * len(arrays),
            out_specs=tuple(spec for _ in outs),
            scratch_shapes=scratch,
            compiler_params=pltpu.CompilerParams(vmem_limit_bytes=VMEM_BYTES),
            cost_estimate=pl.CostEstimate(flops=flops, bytes_accessed=moved, transcendentals=0),
            name=name,
        )(scalars, *arrays)

    return call


def trunk_kernel(
    where, context, w_first, w_second, embed, code_col, code_row, cotangent, mine, theirs,
    own, other,
    wt, patches, gt, normed, rscales, buf, grad, vectors,
):
    c = where[2]

    def rows_of(shard, core):
        return pl.ds(pl.multiple_of(shard * 64 + core * 32, 32), 32)

    for core, pieces in ((c, mine), (1 - c, theirs)):
        for place in range(16):
            wt[place // 4, rows_of(place % 4, core), :] = pieces[place]

    point = lax.broadcasted_iota(jnp.int32, (ROWS, 1), 0)
    column = point - ((point * 3277) >> 16) * PITCH
    mask = jnp.where((column < BOARD) & (point < BOARD * PITCH), 1.0, 0.0).astype(F32)

    preact = nn(context[...], w_first[...])
    cdf = 0.5 * (1.0 + lax.erf(preact * 0.7071067811865476))
    hidden = (preact * cdf).astype(BF16)
    encoded = nn(hidden, w_second[...])
    code = code_col[...]
    stone = embed[...].astype(F32)
    stones = jnp.where(code == 0, stone[0:1], jnp.where(code == 1, stone[1:2], stone[2:3]))
    start = (stones + encoded[0:1]).astype(BF16).astype(F32) * mask

    buf[0:FRONT, :] = jnp.zeros((FRONT, buf.shape[1]), F32)
    buf[FRONT + ROWS :, :] = jnp.zeros((FRONT, buf.shape[1]), F32)
    buf[FRONT : FRONT + ROWS, :] = start
    channels = start.shape[1]

    def forward(block, carry):
        for tap, shift in enumerate(TAP_SHIFTS):
            patches[block, :, tap * channels : (tap + 1) * channels] = buf[
                FRONT + shift : FRONT + shift + ROWS, :
            ].astype(BF16)
        zconv = nt(patches[block], wt[block])
        rscale = lax.rsqrt(jnp.mean(zconv * zconv, axis=-1, keepdims=True) + NORM_EPS)
        value = zconv * rscale
        normed[block] = value
        rscales[block] = rscale
        stream = buf[FRONT : FRONT + ROWS, :] + value * jax.nn.sigmoid(value)
        buf[FRONT : FRONT + ROWS, :] = stream.astype(BF16).astype(F32) * mask
        return carry

    lax.fori_loop(0, 4, forward, 0)
    grad[...] = cotangent[...].astype(F32)

    def backward(step, carry):
        block = 3 - step
        value = normed[block]
        upper = grad[...]
        sigma = jax.nn.sigmoid(value)
        dnorm = upper * (sigma * (1.0 + value * (1.0 - sigma)))
        inner = jnp.mean(dnorm * value, axis=-1, keepdims=True)
        dconv = rscales[block] * (dnorm - value * inner)
        gt[block] = nn(dconv.T.astype(BF16), patches[block]).astype(BF16)
        buf[FRONT : FRONT + ROWS, :] = dconv.astype(BF16).astype(F32)
        total = upper
        for tap, shift in enumerate(TAP_SHIFTS):
            total += nn(
                buf[FRONT - shift : FRONT - shift + ROWS, :].astype(BF16),
                wt[block, :, tap * channels : (tap + 1) * channels],
            )
        grad[...] = total.astype(BF16).astype(F32) * mask
        return carry

    lax.fori_loop(0, 4, backward, 0)

    kind = lax.broadcasted_iota(jnp.int32, (16, ROWS), 0)
    codes = code_row[...]
    picked = ((kind < 3) & (codes == kind)) | ((kind == 3) & (codes < 3))
    sums = nn(jnp.where(picked, 1.0, 0.0).astype(BF16), grad[...].astype(BF16))
    rounded = sums.astype(BF16)
    density = jnp.exp(-0.5 * preact * preact) * 0.3989422804014327
    pre_grad = (nt(rounded, w_second[...]) * (cdf + preact * density)).astype(BF16)
    parts = ((context[...], 0, 8), (hidden, 0, 8), (pre_grad, 3, 8))
    parts += tuple((rounded, row, 2) for row in (3, 0, 1, 2))
    place = 0
    for array, row, count in parts:
        for piece in range(count):
            vectors[place : place + 1, :] = array.astype(F32)[
                row : row + 1, piece * 128 : (piece + 1) * 128
            ]
            place += 1
    tail = vectors[...].astype(BF16)
    taps = gt.shape[2]
    for core, pieces in ((c, own), (1 - c, other)):
        for place in range(16):
            pieces[place, :, 0:taps] = gt[place // 4, rows_of(place % 4, core), :]
            pieces[place, :, taps:] = tail


def merge_kernel(own, come, out):
    taps = own.shape[2] - 128
    out[:, :, 0:taps] = (own[:, :, 0:taps].astype(F32) + come[:, :, 0:taps].astype(F32)).astype(BF16)
    out[:, :, taps : taps + 128] = own[:, :, taps:]
    out[:, :, taps + 128 :] = come[:, :, taps:]


def merge(own, come):
    count, rows, width = own.shape
    spec = pl.BlockSpec((2, rows, width), lambda i: (i, 0, 0))
    return pl.pallas_call(
        merge_kernel,
        grid=(count // 2,),
        in_specs=[spec, spec],
        out_specs=pl.BlockSpec((2, rows, width + 128), lambda i: (i, 0, 0)),
        out_shape=jax.ShapeDtypeStruct((count, rows, width + 128), BF16),
        compiler_params=pltpu.CompilerParams(vmem_limit_bytes=VMEM_BYTES),
        cost_estimate=pl.CostEstimate(
            flops=own.size, bytes_accessed=6 * own.size, transcendentals=0
        ),
        name="merge",
    )(own, come)


def pack_kernel(where, pieces, out, vectors, product, stones):
    first = where[0] * 256 + where[1] * 64 + where[2] * 32
    row = first // 128
    rows = pl.ds(pl.multiple_of(first - row * 128, 32), 32)
    taps = pieces.shape[2] - 256
    for piece in range(16):
        for core in (0, 1):
            state = piece * 2 + core
            lane = taps + core * 128
            vectors[state * 32 : (state + 1) * 32, :] = pieces[piece, :, lane : lane + 128].astype(F32)

    def of_states(place):
        return vectors[pl.ds(place, 32, stride=32), :]

    context = of_states(row).astype(BF16)
    hidden = of_states(row + 8).astype(BF16)
    for piece in range(8):
        lanes = slice(piece * 128, (piece + 1) * 128)
        product[:, lanes] = tn(context, of_states(16 + piece).astype(BF16))
    for piece in range(2):
        lanes = slice(1024 + piece * 128, 1024 + (piece + 1) * 128)
        product[:, lanes] = tn(hidden, of_states(24 + piece).astype(BF16))
    stones[...] = jnp.zeros(stones.shape, F32)
    for piece in range(6):
        v, half = divmod(piece, 2)
        stones[v : v + 1, half * 128 : (half + 1) * 128] = jnp.sum(
            of_states(26 + piece), axis=0, keepdims=True
        )
    for column in range(taps // 256):
        lanes = slice(column * 256, (column + 1) * 256)
        block = pieces[0, :, lanes].astype(F32)
        for piece in range(1, 16):
            block += pieces[piece, :, lanes].astype(F32)
        out[2 * column] = block[0:16].astype(BF16)
        out[2 * column + 1] = block[16:32].astype(BF16)
    for column in range(5):
        block = product[rows, column * 256 : (column + 1) * 256]
        place = 2 * (taps // 256 + column)
        out[place] = block[0:16].astype(BF16)
        out[place + 1] = block[16:32].astype(BF16)
    out[28] = stones[...].astype(BF16)
    for place in (29, 30, 31):
        out[place] = jnp.zeros(out.shape[1:], BF16)


def finish_kernel(where, pieces, conv, first, second, stones):
    for out, start in ((conv, 0), (first, conv.shape[1]), (second, conv.shape[1] + first.shape[1])):
        for column in range(out.shape[1] // 256):
            for half in range(2):
                for core in range(2):
                    row = core * 32 + half * 16
                    out[row : row + 16, column * 256 : (column + 1) * 256] = (
                        pieces[2 * (start // 256 + column) + half, core].astype(F32) * (1.0 / 512.0)
                    ).astype(BF16)
    stones[...] = (pieces[28, 0].astype(F32) * (1.0 / 512.0))[0:3].astype(BF16)


def body(boards, neighbours, counts, database, w_first, w_second, embed, conv_weight, cotangent):
    h = lax.axis_index("shard")
    s = lax.axis_index("section")
    dp = lax.axis_index("dp")
    c = dp % 2
    where = jnp.stack([s, h, c]).astype(jnp.int32)
    channels = embed.shape[1]
    taps = conv_weight.shape[1]
    plane = ("section", "shard")

    unit = lax.dynamic_slice_in_dim(conv_weight[0].T, c * 32, 32, 0)[None]
    mine = exchange(jnp.broadcast_to(unit, (16,) + unit.shape[1:]), plane)
    theirs = swap(mine, "dp", 1)

    ids = lax.dynamic_slice_in_dim(neighbours, s, 1, 0)
    count = lax.dynamic_slice_in_dim(counts, s, 1, 0)
    asked = jnp.concatenate([ids, count[:, None]], axis=1)
    asked = exchange(jnp.broadcast_to(asked, (4, asked.shape[1])), "shard")
    slots = ids.shape[1]
    live = lax.broadcasted_iota(jnp.int32, (4, slots), 1) < asked[:, slots:]
    stored = database.shape[0]
    positions = lax.broadcasted_iota(jnp.int32, (1, 1, stored), 2) + h * stored
    hits = (asked[:, :slots, None] == positions) & live[:, :, None]
    picks = jnp.sum(hits.astype(F32), axis=1).astype(BF16)
    partial = jnp.dot(picks, database, preferred_element_type=F32)
    summed = jnp.sum(exchange(partial, "shard"), axis=0, keepdims=True)
    context = (summed / jnp.maximum(count, 1).astype(F32)[:, None]).astype(BF16)
    context = jnp.broadcast_to(context, (16, context.shape[1]))

    board = lax.dynamic_index_in_dim(boards, s, 0, keepdims=False).reshape(BOARD, BOARD)
    code = jnp.pad(board, ((0, 0), (0, 1)), constant_values=3).reshape(-1)
    code = jnp.pad(code, (0, ROWS - BOARD * PITCH), constant_values=3)
    upper = lax.dynamic_index_in_dim(cotangent, s, 0, keepdims=False)
    upper = jnp.pad(upper.reshape(BOARD, BOARD, channels), ((0, 0), (0, 1), (0, 0)))
    upper = jnp.pad(upper.reshape(-1, channels), ((0, ROWS - BOARD * PITCH), (0, 0)))

    part = jax.ShapeDtypeStruct((16, 32, taps + 128), BF16)
    own, other = vmem_call(
        trunk_kernel,
        (part, part),
        [
            pltpu.VMEM((4, channels, taps), BF16),
            pltpu.VMEM((4, ROWS, taps), BF16),
            pltpu.VMEM((4, channels, taps), BF16),
            pltpu.VMEM((4, ROWS, channels), F32),
            pltpu.VMEM((4, ROWS, 1), F32),
            pltpu.VMEM((2 * FRONT + ROWS, channels), F32),
            pltpu.VMEM((ROWS, channels), F32),
            pltpu.VMEM((32, 128), F32),
        ],
        "trunk",
        12 * 2 * ROWS * taps * channels,
        16 << 20,
    )(where, context, w_first, w_second, embed, code[:, None], code[None, :], upper, mine, theirs)

    pieces = exchange(merge(own, swap(other, "dp", 1)), plane)
    (chunks,) = vmem_call(
        pack_kernel,
        (jax.ShapeDtypeStruct((32, 16, 256), BF16),),
        [
            pltpu.VMEM((1024, 128), F32),
            pltpu.VMEM((128, 1280), F32),
            pltpu.VMEM((16, 256), F32),
        ],
        "pack",
        4 * 32 * 128 * 1280,
        3 << 20,
    )(where, pieces)

    total = exchange(chunks, "dp").astype(F32).reshape(-1, 2, 16, 256)
    total = jnp.sum(total, axis=0, keepdims=True).astype(BF16)
    chunks = exchange(jnp.broadcast_to(total, (lax.axis_size("dp"),) + total.shape[1:]), "dp")
    conv, w1_grad, w2_grad, embed_grad = vmem_call(
        finish_kernel,
        (
            jax.ShapeDtypeStruct((64, taps), BF16),
            jax.ShapeDtypeStruct((64, 1024), BF16),
            jax.ShapeDtypeStruct((64, channels), BF16),
            jax.ShapeDtypeStruct((3, channels), BF16),
        ),
        [],
        "finish",
        1 << 18,
        1 << 20,
    )(where, chunks)
    return (w1_grad, w2_grad, embed_grad, conv.T[None])


def solution(mesh):
    placed = (
        P(("dp", "shard"), None),
        P(("dp", "shard"), None),
        P(("dp", "shard")),
        P("shard", None),
        P(),
        P(),
        P(),
        P("section", None, "shard"),
        P(("dp", "shard"), None, None),
    )
    return jax.shard_map(
        body,
        mesh=mesh,
        in_specs=placed,
        out_specs=(
            P(("section", "shard"), None),
            P(("section", "shard"), None),
            P(),
            P("section", None, "shard"),
        ),
        check_vma=False,
    )
```

```python
import jax
import jax.numpy as jnp
from jax import lax
from jax.experimental import pallas as pl
from jax.experimental.pallas import tpu as pltpu
from jax.sharding import PartitionSpec as P

BOARD = 19
PITCH = 20
ROWS = 384
FRONT = 24
NORM_EPS = 1e-05
TAP_SHIFTS = [(a - 1) * PITCH + (b - 1) for a in range(3) for b in range(3)]
VMEM_BYTES = 40 * 1024 * 1024
F32 = jnp.float32
BF16 = jnp.bfloat16


def swap(block, axis, bits):
    return lax.ppermute(block, axis, [(i, i ^ bits) for i in range(lax.axis_size(axis))])


def turned(block, axis, distance):
    size = lax.axis_size(axis)
    return lax.ppermute(block, axis, [(i, (i + distance) % size) for i in range(size)])


def exchange(blocks, axis):
    return lax.all_to_all(blocks, axis, 0, 0, tiled=True)


def nn(left, right):
    return lax.dot_general(left, right, (((1,), (0,)), ((), ())), preferred_element_type=F32)


def nt(left, right):
    return lax.dot_general(left, right, (((1,), (1,)), ((), ())), preferred_element_type=F32)


def tn(left, right):
    return lax.dot_general(left, right, (((0,), (0,)), ((), ())), preferred_element_type=F32)


def vmem_call(kernel, outs, scratch, name, flops, moved):
    spec = pl.BlockSpec(memory_space=pltpu.VMEM)

    def call(scalars, *arrays):
        return pl.pallas_call(
            kernel,
            out_shape=outs,
            in_specs=[pl.BlockSpec(memory_space=pltpu.SMEM)] + [spec] * len(arrays),
            out_specs=tuple(spec for _ in outs),
            scratch_shapes=scratch,
            compiler_params=pltpu.CompilerParams(vmem_limit_bytes=VMEM_BYTES),
            cost_estimate=pl.CostEstimate(flops=flops, bytes_accessed=moved, transcendentals=0),
            name=name,
        )(scalars, *arrays)

    return call


def trunk_kernel(
    where, context, w_first, w_second, embed, code_col, code_row, cotangent, mine, theirs,
    own, other, tail,
    wt, patches, gt, normed, rscales, buf, grad, vectors,
):
    c = where[2]

    def rows_of(shard, core):
        return pl.ds(pl.multiple_of(shard * 64 + core * 32, 32), 32)

    for core, pieces in ((c, mine), (1 - c, theirs)):
        for place in range(16):
            wt[place // 4, rows_of(place % 4, core), :] = pieces[place]

    point = lax.broadcasted_iota(jnp.int32, (ROWS, 1), 0)
    column = point - ((point * 3277) >> 16) * PITCH
    mask = jnp.where((column < BOARD) & (point < BOARD * PITCH), 1.0, 0.0).astype(F32)

    preact = nn(context[...], w_first[...])
    cdf = 0.5 * (1.0 + lax.erf(preact * 0.7071067811865476))
    hidden = (preact * cdf).astype(BF16)
    encoded = nn(hidden, w_second[...])
    code = code_col[...]
    stone = embed[...].astype(F32)
    stones = jnp.where(code == 0, stone[0:1], jnp.where(code == 1, stone[1:2], stone[2:3]))
    start = (stones + encoded[0:1]).astype(BF16).astype(F32) * mask

    buf[0:FRONT, :] = jnp.zeros((FRONT, buf.shape[1]), F32)
    buf[FRONT + ROWS :, :] = jnp.zeros((FRONT, buf.shape[1]), F32)
    buf[FRONT : FRONT + ROWS, :] = start
    channels = start.shape[1]

    def forward(block, carry):
        for tap, shift in enumerate(TAP_SHIFTS):
            patches[block, :, tap * channels : (tap + 1) * channels] = buf[
                FRONT + shift : FRONT + shift + ROWS, :
            ].astype(BF16)
        zconv = nt(patches[block], wt[block])
        rscale = lax.rsqrt(jnp.mean(zconv * zconv, axis=-1, keepdims=True) + NORM_EPS)
        value = zconv * rscale
        normed[block] = value
        rscales[block] = rscale
        stream = buf[FRONT : FRONT + ROWS, :] + value * jax.nn.sigmoid(value)
        buf[FRONT : FRONT + ROWS, :] = stream.astype(BF16).astype(F32) * mask
        return carry

    lax.fori_loop(0, 4, forward, 0)
    grad[...] = cotangent[...].astype(F32)

    def backward(step, carry):
        block = 3 - step
        value = normed[block]
        upper = grad[...]
        sigma = jax.nn.sigmoid(value)
        dnorm = upper * (sigma * (1.0 + value * (1.0 - sigma)))
        inner = jnp.mean(dnorm * value, axis=-1, keepdims=True)
        dconv = rscales[block] * (dnorm - value * inner)
        gt[block] = nn(dconv.T.astype(BF16), patches[block]).astype(BF16)
        buf[FRONT : FRONT + ROWS, :] = dconv.astype(BF16).astype(F32)
        total = upper
        for tap, shift in enumerate(TAP_SHIFTS):
            total += nn(
                buf[FRONT - shift : FRONT - shift + ROWS, :].astype(BF16),
                wt[block, :, tap * channels : (tap + 1) * channels],
            )
        grad[...] = total.astype(BF16).astype(F32) * mask
        return carry

    lax.fori_loop(0, 4, backward, 0)

    kind = lax.broadcasted_iota(jnp.int32, (16, ROWS), 0)
    codes = code_row[...]
    picked = ((kind < 3) & (codes == kind)) | ((kind == 3) & (codes < 3))
    sums = nn(jnp.where(picked, 1.0, 0.0).astype(BF16), grad[...].astype(BF16))
    rounded = sums.astype(BF16)
    density = jnp.exp(-0.5 * preact * preact) * 0.3989422804014327
    pre_grad = (nt(rounded, w_second[...]) * (cdf + preact * density)).astype(BF16)
    parts = ((context[...], 0, 8), (hidden, 0, 8), (pre_grad, 3, 8))
    parts += tuple((rounded, row, 2) for row in (3, 0, 1, 2))
    place = 0
    for array, row, count in parts:
        for piece in range(count):
            vectors[place : place + 1, :] = array.astype(F32)[
                row : row + 1, piece * 128 : (piece + 1) * 128
            ]
            place += 1
    tail[...] = vectors[...].astype(BF16)
    for core, pieces in ((c, own), (1 - c, other)):
        for place in range(16):
            pieces[place] = gt[place // 4, rows_of(place % 4, core), :]


def pack_kernel(where, pieces, near, far, out, vectors, product, stones):
    first = where[0] * 256 + where[1] * 64 + where[2] * 32
    row = first // 128
    rows = pl.ds(pl.multiple_of(first - row * 128, 32), 32)
    taps = pieces.shape[2]
    for piece in range(16):
        vectors[piece * 32 : (piece + 1) * 32, :] = near[piece].astype(F32)
        vectors[(16 + piece) * 32 : (17 + piece) * 32, :] = far[piece].astype(F32)

    def of_states(place):
        return vectors[pl.ds(place, 32, stride=32), :]

    context = of_states(row).astype(BF16)
    hidden = of_states(row + 8).astype(BF16)
    for piece in range(8):
        lanes = slice(piece * 128, (piece + 1) * 128)
        product[:, lanes] = tn(context, of_states(16 + piece).astype(BF16))
    for piece in range(2):
        lanes = slice(1024 + piece * 128, 1024 + (piece + 1) * 128)
        product[:, lanes] = tn(hidden, of_states(24 + piece).astype(BF16))
    stones[...] = jnp.zeros(stones.shape, F32)
    for piece in range(6):
        v, half = divmod(piece, 2)
        stones[v : v + 1, half * 128 : (half + 1) * 128] = jnp.sum(
            of_states(26 + piece), axis=0, keepdims=True
        )
    for column in range(taps // 256):
        lanes = slice(column * 256, (column + 1) * 256)
        block = pieces[0, :, lanes].astype(F32)
        for piece in range(1, 16):
            block += pieces[piece, :, lanes].astype(F32)
        out[2 * column] = block[0:16].astype(BF16)
        out[2 * column + 1] = block[16:32].astype(BF16)
    for column in range(5):
        block = product[rows, column * 256 : (column + 1) * 256]
        place = 2 * (taps // 256 + column)
        out[place] = block[0:16].astype(BF16)
        out[place + 1] = block[16:32].astype(BF16)
    out[28] = stones[...].astype(BF16)
    for place in (29, 30, 31):
        out[place] = jnp.zeros(out.shape[1:], BF16)


def finish_kernel(where, mine, theirs, conv, first, second, stones):
    c = where[2]
    for out, start in ((conv, 0), (first, conv.shape[1]), (second, conv.shape[1] + first.shape[1])):
        for column in range(out.shape[1] // 256):
            for half in range(2):
                for core, pieces in ((c, mine), (1 - c, theirs)):
                    rows = pl.ds(pl.multiple_of(core * 32 + half * 16, 16), 16)
                    out[rows, column * 256 : (column + 1) * 256] = (
                        pieces[2 * (start // 256 + column) + half].astype(F32) * (1.0 / 512.0)
                    ).astype(BF16)
    stones[...] = (mine[28].astype(F32) * (1.0 / 512.0))[0:3].astype(BF16)


def body(boards, neighbours, counts, database, w_first, w_second, embed, conv_weight, cotangent):
    h = lax.axis_index("shard")
    s = lax.axis_index("section")
    dp = lax.axis_index("dp")
    c = dp % 2
    where = jnp.stack([s, h, c]).astype(jnp.int32)
    channels = embed.shape[1]
    taps = conv_weight.shape[1]
    plane = ("section", "shard")

    unit = lax.dynamic_slice_in_dim(conv_weight[0].T, c * 32, 32, 0)[None]
    mine = exchange(jnp.broadcast_to(unit, (16,) + unit.shape[1:]), plane)
    theirs = swap(mine, "dp", 1)

    ids = lax.dynamic_slice_in_dim(neighbours, s, 1, 0)
    count = lax.dynamic_slice_in_dim(counts, s, 1, 0)
    asked = jnp.concatenate([ids, count[:, None]], axis=1)
    asked = jnp.concatenate([asked] + [turned(asked, "shard", d) for d in (1, 2, 3)])
    slots = ids.shape[1]
    live = lax.broadcasted_iota(jnp.int32, (4, slots), 1) < asked[:, slots:]
    stored = database.shape[0]
    positions = lax.broadcasted_iota(jnp.int32, (1, 1, stored), 2) + h * stored
    hits = (asked[:, :slots, None] == positions) & live[:, :, None]
    picks = jnp.sum(hits.astype(F32), axis=1).astype(BF16)
    partial = jnp.dot(picks, database, preferred_element_type=F32)
    summed = partial[0:1]
    for d in (1, 2, 3):
        summed = summed + turned(partial[d : d + 1], "shard", -d)
    context = (summed / jnp.maximum(count, 1).astype(F32)[:, None]).astype(BF16)
    context = jnp.broadcast_to(context, (16, context.shape[1]))

    board = lax.dynamic_index_in_dim(boards, s, 0, keepdims=False).reshape(BOARD, BOARD)
    code = jnp.pad(board, ((0, 0), (0, 1)), constant_values=3).reshape(-1)
    code = jnp.pad(code, (0, ROWS - BOARD * PITCH), constant_values=3)
    upper = lax.dynamic_index_in_dim(cotangent, s, 0, keepdims=False)
    upper = jnp.pad(upper.reshape(BOARD, BOARD, channels), ((0, 0), (0, 1), (0, 0)))
    upper = jnp.pad(upper.reshape(-1, channels), ((0, ROWS - BOARD * PITCH), (0, 0)))

    part = jax.ShapeDtypeStruct((16, 32, taps), BF16)
    own, other, rows = vmem_call(
        trunk_kernel,
        (part, part, jax.ShapeDtypeStruct((32, 128), BF16)),
        [
            pltpu.VMEM((4, channels, taps), BF16),
            pltpu.VMEM((4, ROWS, taps), BF16),
            pltpu.VMEM((4, channels, taps), BF16),
            pltpu.VMEM((4, ROWS, channels), F32),
            pltpu.VMEM((4, ROWS, 1), F32),
            pltpu.VMEM((2 * FRONT + ROWS, channels), F32),
            pltpu.VMEM((ROWS, channels), F32),
            pltpu.VMEM((32, 128), F32),
        ],
        "trunk",
        12 * 2 * ROWS * taps * channels,
        16 << 20,
    )(where, context, w_first, w_second, embed, code[:, None], code[None, :], upper, mine, theirs)

    pieces = exchange((own.astype(F32) + swap(other, "dp", 1).astype(F32)).astype(BF16), plane)

    rows = rows[None]
    for axis, bits in (("shard", 1), ("shard", 3), ("section", 1), ("section", 3)):
        rows = jnp.concatenate([rows, swap(rows, axis, bits)])
    (chunks,) = vmem_call(
        pack_kernel,
        (jax.ShapeDtypeStruct((32, 16, 256), BF16),),
        [
            pltpu.VMEM((1024, 128), F32),
            pltpu.VMEM((128, 1280), F32),
            pltpu.VMEM((16, 256), F32),
        ],
        "pack",
        4 * 32 * 128 * 1280,
        3 << 20,
    )(where, pieces, rows, swap(rows, "dp", 1))

    def along_z(blocks, groups, step):
        return lax.all_to_all(
            blocks.reshape((4, step) + blocks.shape[-2:]), "dp", 0, 0,
            axis_index_groups=groups, tiled=True,
        )

    fours = range(lax.axis_size("dp") // 8)
    low = [[8 * i + 2 * j + core for j in range(4)] for i in fours for core in (0, 1)]
    high = [[8 * i + 2 * j + core for i in fours] for j in range(4) for core in (0, 1)]
    chunks = jnp.sum(along_z(chunks, low, 8).astype(F32), axis=0).astype(BF16)
    chunks = jnp.sum(along_z(chunks, high, 2).astype(F32), axis=0).astype(BF16)
    chunks = along_z(jnp.broadcast_to(chunks, (4,) + chunks.shape), high, 2)
    chunks = chunks.reshape((8,) + chunks.shape[-2:])
    chunks = along_z(jnp.broadcast_to(chunks, (4,) + chunks.shape), low, 8)
    chunks = chunks.reshape((32,) + chunks.shape[-2:])
    conv, w1_grad, w2_grad, embed_grad = vmem_call(
        finish_kernel,
        (
            jax.ShapeDtypeStruct((64, taps), BF16),
            jax.ShapeDtypeStruct((64, 1024), BF16),
            jax.ShapeDtypeStruct((64, channels), BF16),
            jax.ShapeDtypeStruct((3, channels), BF16),
        ),
        [],
        "finish",
        1 << 18,
        1 << 20,
    )(where, chunks, swap(chunks, "dp", 1))
    return (w1_grad, w2_grad, embed_grad, conv.T[None])


def solution(mesh):
    placed = (
        P(("dp", "shard"), None),
        P(("dp", "shard"), None),
        P(("dp", "shard")),
        P("shard", None),
        P(),
        P(),
        P(),
        P("section", None, "shard"),
        P(("dp", "shard"), None, None),
    )
    return jax.shard_map(
        body,
        mesh=mesh,
        in_specs=placed,
        out_specs=(
            P(("section", "shard"), None),
            P(("section", "shard"), None),
            P(),
            P("section", None, "shard"),
        ),
        check_vma=False,
    )
```

```python
import jax
import jax.numpy as jnp
from jax import lax
from jax.experimental import pallas as pl
from jax.experimental.pallas import tpu as pltpu
from jax.sharding import PartitionSpec as P

BOARD = 19
PITCH = 20
ROWS = 384
FRONT = 24
NORM_EPS = 1e-05
TAP_SHIFTS = [(a - 1) * PITCH + (b - 1) for a in range(3) for b in range(3)]
VMEM_BYTES = 40 * 1024 * 1024
F32 = jnp.float32
BF16 = jnp.bfloat16


def swap(block, axis, bits):
    return lax.ppermute(block, axis, [(i, i ^ bits) for i in range(lax.axis_size(axis))])


def turned(block, axis, distance):
    size = lax.axis_size(axis)
    return lax.ppermute(block, axis, [(i, (i + distance) % size) for i in range(size)])


def exchange(blocks, axis):
    return lax.all_to_all(blocks, axis, 0, 0, tiled=True)


def nn(left, right):
    return lax.dot_general(left, right, (((1,), (0,)), ((), ())), preferred_element_type=F32)


def nt(left, right):
    return lax.dot_general(left, right, (((1,), (1,)), ((), ())), preferred_element_type=F32)


def tn(left, right):
    return lax.dot_general(left, right, (((0,), (0,)), ((), ())), preferred_element_type=F32)


def vmem_call(kernel, outs, scratch, name, flops, moved):
    spec = pl.BlockSpec(memory_space=pltpu.VMEM)

    def call(scalars, *arrays):
        return pl.pallas_call(
            kernel,
            out_shape=outs,
            in_specs=[pl.BlockSpec(memory_space=pltpu.SMEM)] + [spec] * len(arrays),
            out_specs=tuple(spec for _ in outs),
            scratch_shapes=scratch,
            compiler_params=pltpu.CompilerParams(vmem_limit_bytes=VMEM_BYTES),
            cost_estimate=pl.CostEstimate(flops=flops, bytes_accessed=moved, transcendentals=0),
            name=name,
        )(scalars, *arrays)

    return call


def encoder_kernel(where, context, w_first, w_second, preact, hidden, encoded):
    value = nn(context[...], w_first[...])
    preact[...] = value
    rounded = (value * (0.5 * (1.0 + lax.erf(value * 0.7071067811865476)))).astype(BF16)
    hidden[...] = rounded
    encoded[...] = nn(rounded, w_second[...])


def trunk_kernel(
    where, context, preact_in, hidden_in, encoded_in, w_second, embed, code_col, code_row, cotangent,
    mine, theirs,
    own, other,
    wt, patches, gt, normed, rscales, buf, grad, vectors,
):
    c = where[2]

    def rows_of(shard, core):
        return pl.ds(pl.multiple_of(shard * 64 + core * 32, 32), 32)

    for core, pieces in ((c, mine), (1 - c, theirs)):
        for place in range(16):
            wt[place // 4, rows_of(place % 4, core), :] = pieces[place]

    point = lax.broadcasted_iota(jnp.int32, (ROWS, 1), 0)
    column = point - ((point * 3277) >> 16) * PITCH
    mask = jnp.where((column < BOARD) & (point < BOARD * PITCH), 1.0, 0.0).astype(F32)

    preact, hidden, encoded = preact_in[...], hidden_in[...], encoded_in[...]
    code = code_col[...]
    stone = embed[...].astype(F32)
    stones = jnp.where(code == 0, stone[0:1], jnp.where(code == 1, stone[1:2], stone[2:3]))
    start = (stones + encoded[0:1]).astype(BF16).astype(F32) * mask

    buf[0:FRONT, :] = jnp.zeros((FRONT, buf.shape[1]), F32)
    buf[FRONT + ROWS :, :] = jnp.zeros((FRONT, buf.shape[1]), F32)
    buf[FRONT : FRONT + ROWS, :] = start
    channels = start.shape[1]

    def forward(block, carry):
        for tap, shift in enumerate(TAP_SHIFTS):
            patches[block, :, tap * channels : (tap + 1) * channels] = buf[
                FRONT + shift : FRONT + shift + ROWS, :
            ].astype(BF16)
        zconv = nt(patches[block], wt[block])
        rscale = lax.rsqrt(jnp.mean(zconv * zconv, axis=-1, keepdims=True) + NORM_EPS)
        value = zconv * rscale
        normed[block] = value
        rscales[block] = rscale
        stream = buf[FRONT : FRONT + ROWS, :] + value * jax.nn.sigmoid(value)
        buf[FRONT : FRONT + ROWS, :] = stream.astype(BF16).astype(F32) * mask
        return carry

    lax.fori_loop(0, 4, forward, 0)
    grad[...] = cotangent[...].astype(F32)

    def backward(step, carry):
        block = 3 - step
        value = normed[block]
        upper = grad[...]
        sigma = jax.nn.sigmoid(value)
        dnorm = upper * (sigma * (1.0 + value * (1.0 - sigma)))
        inner = jnp.mean(dnorm * value, axis=-1, keepdims=True)
        dconv = rscales[block] * (dnorm - value * inner)
        gt[block] = nn(dconv.T.astype(BF16), patches[block]).astype(BF16)
        buf[FRONT : FRONT + ROWS, :] = dconv.astype(BF16).astype(F32)
        total = upper
        for tap, shift in enumerate(TAP_SHIFTS):
            total += nn(
                buf[FRONT - shift : FRONT - shift + ROWS, :].astype(BF16),
                wt[block, :, tap * channels : (tap + 1) * channels],
            )
        grad[...] = total.astype(BF16).astype(F32) * mask
        return carry

    lax.fori_loop(0, 4, backward, 0)

    kind = lax.broadcasted_iota(jnp.int32, (16, ROWS), 0)
    codes = code_row[...]
    picked = ((kind < 3) & (codes == kind)) | ((kind == 3) & (codes < 3))
    sums = nn(jnp.where(picked, 1.0, 0.0).astype(BF16), grad[...].astype(BF16))
    rounded = sums.astype(BF16)
    cdf = 0.5 * (1.0 + lax.erf(preact * 0.7071067811865476))
    density = jnp.exp(-0.5 * preact * preact) * 0.3989422804014327
    pre_grad = (nt(rounded, w_second[...]) * (cdf + preact * density)).astype(BF16)
    parts = ((context[...], 0, 8), (hidden, 0, 8), (pre_grad, 3, 8))
    parts += tuple((rounded, row, 2) for row in (3, 0, 1, 2))
    place = 0
    for array, row, count in parts:
        for piece in range(count):
            vectors[place : place + 1, :] = array.astype(F32)[
                row : row + 1, piece * 128 : (piece + 1) * 128
            ]
            place += 1
    tail = vectors[...].astype(BF16)
    empty = jnp.zeros(tail.shape, BF16)
    taps = gt.shape[2]
    for core, pieces, first, second in ((c, own, tail, empty), (1 - c, other, empty, tail)):
        for place in range(16):
            pieces[place, :, 0:taps] = gt[place // 4, rows_of(place % 4, core), :]
            pieces[place, :, taps : taps + 128] = first
            pieces[place, :, taps + 128 :] = second


def pack_kernel(where, pieces, out, vectors, product, stones):
    first = where[0] * 256 + where[1] * 64 + where[2] * 32
    row = first // 128
    rows = pl.ds(pl.multiple_of(first - row * 128, 32), 32)
    taps = pieces.shape[2] - 256
    for piece in range(16):
        for core in (0, 1):
            state = piece * 2 + core
            lane = taps + core * 128
            vectors[state * 32 : (state + 1) * 32, :] = pieces[piece, :, lane : lane + 128].astype(F32)

    def of_states(place):
        return vectors[pl.ds(place, 32, stride=32), :]

    context = of_states(row).astype(BF16)
    hidden = of_states(row + 8).astype(BF16)
    for piece in range(8):
        lanes = slice(piece * 128, (piece + 1) * 128)
        product[:, lanes] = tn(context, of_states(16 + piece).astype(BF16))
    for piece in range(2):
        lanes = slice(1024 + piece * 128, 1024 + (piece + 1) * 128)
        product[:, lanes] = tn(hidden, of_states(24 + piece).astype(BF16))
    stones[...] = jnp.zeros(stones.shape, F32)
    for piece in range(6):
        v, half = divmod(piece, 2)
        stones[v : v + 1, half * 128 : (half + 1) * 128] = jnp.sum(
            of_states(26 + piece), axis=0, keepdims=True
        )
    for column in range(taps // 256):
        lanes = slice(column * 256, (column + 1) * 256)
        block = pieces[0, :, lanes].astype(F32)
        for piece in range(1, 16):
            block += pieces[piece, :, lanes].astype(F32)
        out[2 * column] = block[0:16].astype(BF16)
        out[2 * column + 1] = block[16:32].astype(BF16)
    for column in range(5):
        block = product[rows, column * 256 : (column + 1) * 256]
        place = 2 * (taps // 256 + column)
        out[place] = block[0:16].astype(BF16)
        out[place + 1] = block[16:32].astype(BF16)
    out[28] = stones[...].astype(BF16)
    for place in (29, 30, 31):
        out[place] = jnp.zeros(out.shape[1:], BF16)


def finish_kernel(where, mine, theirs, conv, first, second, stones):
    c = where[2]
    for out, start in ((conv, 0), (first, conv.shape[1]), (second, conv.shape[1] + first.shape[1])):
        for column in range(out.shape[1] // 256):
            for half in range(2):
                for core, pieces in ((c, mine), (1 - c, theirs)):
                    rows = pl.ds(pl.multiple_of(core * 32 + half * 16, 16), 16)
                    out[rows, column * 256 : (column + 1) * 256] = (
                        pieces[2 * (start // 256 + column) + half].astype(F32) * (1.0 / 512.0)
                    ).astype(BF16)
    stones[...] = (mine[28].astype(F32) * (1.0 / 512.0))[0:3].astype(BF16)


def body(boards, neighbours, counts, database, w_first, w_second, embed, conv_weight, cotangent):
    h = lax.axis_index("shard")
    s = lax.axis_index("section")
    dp = lax.axis_index("dp")
    c = dp % 2
    where = jnp.stack([s, h, c]).astype(jnp.int32)
    channels = embed.shape[1]
    taps = conv_weight.shape[1]
    plane = ("section", "shard")

    ids = lax.dynamic_slice_in_dim(neighbours, s, 1, 0)
    count = lax.dynamic_slice_in_dim(counts, s, 1, 0)
    asked = jnp.concatenate([ids, count[:, None]], axis=1)
    asked = exchange(jnp.broadcast_to(asked, (4, asked.shape[1])), "shard")

    unit = lax.dynamic_slice_in_dim(conv_weight[0].T, c * 32, 32, 0)[None]
    asked, unit = lax.optimization_barrier((asked, unit))
    mine = exchange(jnp.broadcast_to(unit, (16,) + unit.shape[1:]), plane)

    slots = ids.shape[1]
    live = lax.broadcasted_iota(jnp.int32, (4, slots), 1) < asked[:, slots:]
    stored = database.shape[0]
    positions = lax.broadcasted_iota(jnp.int32, (1, 1, stored), 2) + h * stored
    hits = (asked[:, :slots, None] == positions) & live[:, :, None]
    picks = jnp.sum(hits.astype(F32), axis=1).astype(BF16)
    partial = jnp.dot(picks, database, preferred_element_type=F32)
    summed = lax.dynamic_slice_in_dim(partial, h, 1, 0)
    for d in (1, 2, 3):
        piece = lax.dynamic_slice_in_dim(partial, (h + 4 - d) % 4, 1, 0)
        summed = summed + turned(piece, "shard", -d)
    context = (summed / jnp.maximum(count, 1).astype(F32)[:, None]).astype(BF16)
    context = jnp.broadcast_to(context, (16, context.shape[1]))

    board = lax.dynamic_index_in_dim(boards, s, 0, keepdims=False).reshape(BOARD, BOARD)
    code = jnp.pad(board, ((0, 0), (0, 1)), constant_values=3).reshape(-1)
    code = jnp.pad(code, (0, ROWS - BOARD * PITCH), constant_values=3)
    upper = lax.dynamic_index_in_dim(cotangent, s, 0, keepdims=False)
    upper = jnp.pad(upper.reshape(BOARD, BOARD, channels), ((0, 0), (0, 1), (0, 0)))
    upper = jnp.pad(upper.reshape(-1, channels), ((0, ROWS - BOARD * PITCH), (0, 0)))

    mine, context, upper = lax.optimization_barrier((mine, context, upper))
    theirs = swap(mine, "dp", 1)
    width = context.shape[1]
    preact, hidden, encoded = vmem_call(
        encoder_kernel,
        (
            jax.ShapeDtypeStruct((16, width), F32),
            jax.ShapeDtypeStruct((16, width), BF16),
            jax.ShapeDtypeStruct((16, channels), F32),
        ),
        [],
        "encoder",
        2 * 16 * width * (width + channels),
        3 << 20,
    )(where, context, w_first, w_second)
    part = jax.ShapeDtypeStruct((16, 32, taps + 256), BF16)
    own, other = vmem_call(
        trunk_kernel,
        (part, part),
        [
            pltpu.VMEM((4, channels, taps), BF16),
            pltpu.VMEM((4, ROWS, taps), BF16),
            pltpu.VMEM((4, channels, taps), BF16),
            pltpu.VMEM((4, ROWS, channels), F32),
            pltpu.VMEM((4, ROWS, 1), F32),
            pltpu.VMEM((2 * FRONT + ROWS, channels), F32),
            pltpu.VMEM((ROWS, channels), F32),
            pltpu.VMEM((32, 128), F32),
        ],
        "trunk",
        12 * 2 * ROWS * taps * channels,
        16 << 20,
    )(
        where, context, preact, hidden, encoded, w_second, embed,
        code[:, None], code[None, :], upper, mine, theirs,
    )

    pieces = exchange((own.astype(F32) + swap(other, "dp", 1).astype(F32)).astype(BF16), plane)

    (chunks,) = vmem_call(
        pack_kernel,
        (jax.ShapeDtypeStruct((32, 16, 256), BF16),),
        [
            pltpu.VMEM((1024, 128), F32),
            pltpu.VMEM((128, 1280), F32),
            pltpu.VMEM((16, 256), F32),
        ],
        "pack",
        4 * 32 * 128 * 1280,
        3 << 20,
    )(where, pieces)

    line = [[2 * i + core for i in range(lax.axis_size("dp") // 2)] for core in (0, 1)]

    def along_z(blocks):
        return lax.all_to_all(blocks, "dp", 0, 0, axis_index_groups=line, tiled=True)

    total = along_z(chunks.reshape(16, 2, 16, 256))
    total = jnp.sum(total.astype(F32), axis=0, keepdims=True).astype(BF16)
    chunks = along_z(jnp.broadcast_to(total, (16,) + total.shape[1:])).reshape(32, 16, 256)
    conv, w1_grad, w2_grad, embed_grad = vmem_call(
        finish_kernel,
        (
            jax.ShapeDtypeStruct((64, taps), BF16),
            jax.ShapeDtypeStruct((64, 1024), BF16),
            jax.ShapeDtypeStruct((64, channels), BF16),
            jax.ShapeDtypeStruct((3, channels), BF16),
        ),
        [],
        "finish",
        1 << 18,
        1 << 20,
    )(where, chunks, swap(chunks, "dp", 1))
    return (w1_grad, w2_grad, embed_grad, conv.T[None])


def solution(mesh):
    placed = (
        P(("dp", "shard"), None),
        P(("dp", "shard"), None),
        P(("dp", "shard")),
        P("shard", None),
        P(),
        P(),
        P(),
        P("section", None, "shard"),
        P(("dp", "shard"), None, None),
    )
    return jax.shard_map(
        body,
        mesh=mesh,
        in_specs=placed,
        out_specs=(
            P(("section", "shard"), None),
            P(("section", "shard"), None),
            P(),
            P("section", None, "shard"),
        ),
        check_vma=False,
    )
```

```python
import jax
import jax.numpy as jnp
from jax import lax
from jax.experimental import pallas as pl
from jax.experimental.pallas import tpu as pltpu
from jax.sharding import PartitionSpec as P

BOARD = 19
PITCH = 20
ROWS = 384
FRONT = 24
NORM_EPS = 1e-05
TAP_SHIFTS = [(a - 1) * PITCH + (b - 1) for a in range(3) for b in range(3)]
VMEM_BYTES = 40 * 1024 * 1024
F32 = jnp.float32
BF16 = jnp.bfloat16


def swap(block, axis, bits):
    return lax.ppermute(block, axis, [(i, i ^ bits) for i in range(lax.axis_size(axis))])


def turned(block, axis, distance):
    size = lax.axis_size(axis)
    return lax.ppermute(block, axis, [(i, (i + distance) % size) for i in range(size)])


def exchange(blocks, axis):
    return lax.all_to_all(blocks, axis, 0, 0, tiled=True)


def nn(left, right):
    return lax.dot_general(left, right, (((1,), (0,)), ((), ())), preferred_element_type=F32)


def nt(left, right):
    return lax.dot_general(left, right, (((1,), (1,)), ((), ())), preferred_element_type=F32)


def tn(left, right):
    return lax.dot_general(left, right, (((0,), (0,)), ((), ())), preferred_element_type=F32)


def vmem_call(kernel, outs, scratch, name, flops, moved):
    spec = pl.BlockSpec(memory_space=pltpu.VMEM)

    def call(scalars, *arrays):
        return pl.pallas_call(
            kernel,
            out_shape=outs,
            in_specs=[pl.BlockSpec(memory_space=pltpu.SMEM)] + [spec] * len(arrays),
            out_specs=tuple(spec for _ in outs),
            scratch_shapes=scratch,
            compiler_params=pltpu.CompilerParams(vmem_limit_bytes=VMEM_BYTES),
            cost_estimate=pl.CostEstimate(flops=flops, bytes_accessed=moved, transcendentals=0),
            name=name,
        )(scalars, *arrays)

    return call


def encoder_kernel(where, context, w_first, w_second, preact, hidden, encoded):
    value = nn(context[...], w_first[...])
    preact[...] = value
    rounded = (value * (0.5 * (1.0 + lax.erf(value * 0.7071067811865476)))).astype(BF16)
    hidden[...] = rounded
    encoded[...] = nn(rounded, w_second[...])


def trunk_kernel(
    where, context, preact_in, hidden_in, encoded_in, w_second, embed, code_col, code_row, cotangent,
    mine, theirs,
    own, other,
    wt, patches, gt, normed, rscales, buf, grad, vectors,
):
    c = where[2]

    def block_rows(outer, inner, core):
        block = jnp.where(core == 0, inner, outer)
        shard = jnp.where(core == 0, outer, inner)
        return block, pl.ds(pl.multiple_of(shard * 64 + core * 32, 32), 32)

    for core, pieces in ((c, mine), (1 - c, theirs)):
        for outer in range(4):
            for inner in range(4):
                block, rows = block_rows(inner, outer, core)
                wt[block, rows, :] = pieces[outer, inner]

    point = lax.broadcasted_iota(jnp.int32, (ROWS, 1), 0)
    column = point - ((point * 3277) >> 16) * PITCH
    mask = jnp.where((column < BOARD) & (point < BOARD * PITCH), 1.0, 0.0).astype(F32)

    preact, hidden, encoded = preact_in[...], hidden_in[...], encoded_in[...]
    code = code_col[...]
    stone = embed[...].astype(F32)
    stones = jnp.where(code == 0, stone[0:1], jnp.where(code == 1, stone[1:2], stone[2:3]))
    start = (stones + encoded[0:1]).astype(BF16).astype(F32) * mask

    buf[0:FRONT, :] = jnp.zeros((FRONT, buf.shape[1]), F32)
    buf[FRONT + ROWS :, :] = jnp.zeros((FRONT, buf.shape[1]), F32)
    buf[FRONT : FRONT + ROWS, :] = start
    channels = start.shape[1]

    def forward(block, carry):
        for tap, shift in enumerate(TAP_SHIFTS):
            patches[block, :, tap * channels : (tap + 1) * channels] = buf[
                FRONT + shift : FRONT + shift + ROWS, :
            ].astype(BF16)
        zconv = nt(patches[block], wt[block])
        rscale = lax.rsqrt(jnp.mean(zconv * zconv, axis=-1, keepdims=True) + NORM_EPS)
        value = zconv * rscale
        normed[block] = value
        rscales[block] = rscale
        stream = buf[FRONT : FRONT + ROWS, :] + value * jax.nn.sigmoid(value)
        buf[FRONT : FRONT + ROWS, :] = stream.astype(BF16).astype(F32) * mask
        return carry

    lax.fori_loop(0, 4, forward, 0)
    grad[...] = cotangent[...].astype(F32)

    def backward(step, carry):
        block = 3 - step
        value = normed[block]
        upper = grad[...]
        sigma = jax.nn.sigmoid(value)
        dnorm = upper * (sigma * (1.0 + value * (1.0 - sigma)))
        inner = jnp.mean(dnorm * value, axis=-1, keepdims=True)
        dconv = rscales[block] * (dnorm - value * inner)
        gt[block] = nn(dconv.T.astype(BF16), patches[block]).astype(BF16)
        buf[FRONT : FRONT + ROWS, :] = dconv.astype(BF16).astype(F32)
        total = upper
        for tap, shift in enumerate(TAP_SHIFTS):
            total += nn(
                buf[FRONT - shift : FRONT - shift + ROWS, :].astype(BF16),
                wt[block, :, tap * channels : (tap + 1) * channels],
            )
        grad[...] = total.astype(BF16).astype(F32) * mask
        return carry

    lax.fori_loop(0, 4, backward, 0)

    kind = lax.broadcasted_iota(jnp.int32, (16, ROWS), 0)
    codes = code_row[...]
    picked = ((kind < 3) & (codes == kind)) | ((kind == 3) & (codes < 3))
    sums = nn(jnp.where(picked, 1.0, 0.0).astype(BF16), grad[...].astype(BF16))
    rounded = sums.astype(BF16)
    cdf = 0.5 * (1.0 + lax.erf(preact * 0.7071067811865476))
    density = jnp.exp(-0.5 * preact * preact) * 0.3989422804014327
    pre_grad = (nt(rounded, w_second[...]) * (cdf + preact * density)).astype(BF16)
    parts = ((context[...], 0, 8), (hidden, 0, 8), (pre_grad, 3, 8))
    parts += tuple((rounded, row, 2) for row in (3, 0, 1, 2))
    place = 0
    for array, row, count in parts:
        for piece in range(count):
            vectors[place : place + 1, :] = array.astype(F32)[
                row : row + 1, piece * 128 : (piece + 1) * 128
            ]
            place += 1
    tail = vectors[...].astype(BF16)
    empty = jnp.zeros(tail.shape, BF16)
    taps = gt.shape[2]
    for core, pieces, first, second in ((c, own, tail, empty), (1 - c, other, empty, tail)):
        for outer in range(4):
            for inner in range(4):
                block, rows = block_rows(outer, inner, core)
                pieces[outer, inner, :, 0:taps] = gt[block, rows, :]
                pieces[outer, inner, :, taps : taps + 128] = first
                pieces[outer, inner, :, taps + 128 :] = second


def fold_kernel(where, pieces, out):
    taps = pieces.shape[3] - 256
    for inner in range(4):
        total = pieces[0, inner, :, 0:taps].astype(F32)
        for source in range(1, 4):
            total += pieces[source, inner, :, 0:taps].astype(F32)
        out[inner, :, 0:taps] = total.astype(BF16)
        for source in range(4):
            lane = taps + source * 256
            out[inner, :, lane : lane + 256] = pieces[source, inner, :, taps:]


def pack_kernel(where, pieces, out, vectors, product, stones):
    first = where[0] * 256 + where[1] * 64 + where[2] * 32
    row = first // 128
    rows = pl.ds(pl.multiple_of(first - row * 128, 32), 32)
    taps = pieces.shape[2] - 1024
    for state in range(32):
        lane = taps + state % 8 * 128
        vectors[state * 32 : (state + 1) * 32, :] = pieces[state // 8, :, lane : lane + 128].astype(F32)

    def of_states(place):
        return vectors[pl.ds(place, 32, stride=32), :]

    context = of_states(row).astype(BF16)
    hidden = of_states(row + 8).astype(BF16)
    for piece in range(8):
        lanes = slice(piece * 128, (piece + 1) * 128)
        product[:, lanes] = tn(context, of_states(16 + piece).astype(BF16))
    for piece in range(2):
        lanes = slice(1024 + piece * 128, 1024 + (piece + 1) * 128)
        product[:, lanes] = tn(hidden, of_states(24 + piece).astype(BF16))
    stones[...] = jnp.zeros(stones.shape, F32)
    for piece in range(6):
        v, half = divmod(piece, 2)
        stones[v : v + 1, half * 128 : (half + 1) * 128] = jnp.sum(
            of_states(26 + piece), axis=0, keepdims=True
        )
    for column in range(taps // 256):
        lanes = slice(column * 256, (column + 1) * 256)
        block = pieces[0, :, lanes].astype(F32)
        for piece in range(1, 4):
            block += pieces[piece, :, lanes].astype(F32)
        out[2 * column] = block[0:16].astype(BF16)
        out[2 * column + 1] = block[16:32].astype(BF16)
    for column in range(5):
        block = product[rows, column * 256 : (column + 1) * 256]
        place = 2 * (taps // 256 + column)
        out[place] = block[0:16].astype(BF16)
        out[place + 1] = block[16:32].astype(BF16)
    out[28] = stones[...].astype(BF16)
    for place in (29, 30, 31):
        out[place] = jnp.zeros(out.shape[1:], BF16)


def finish_kernel(where, mine, theirs, conv, first, second, stones):
    c = where[2]
    for out, start in ((conv, 0), (first, conv.shape[1]), (second, conv.shape[1] + first.shape[1])):
        for column in range(out.shape[1] // 256):
            for half in range(2):
                for core, pieces in ((c, mine), (1 - c, theirs)):
                    rows = pl.ds(pl.multiple_of(core * 32 + half * 16, 16), 16)
                    out[rows, column * 256 : (column + 1) * 256] = (
                        pieces[2 * (start // 256 + column) + half].astype(F32) * (1.0 / 512.0)
                    ).astype(BF16)
    stones[...] = (mine[28].astype(F32) * (1.0 / 512.0))[0:3].astype(BF16)


def body(boards, neighbours, counts, database, w_first, w_second, embed, conv_weight, cotangent):
    h = lax.axis_index("shard")
    s = lax.axis_index("section")
    dp = lax.axis_index("dp")
    c = dp % 2
    where = jnp.stack([s, h, c]).astype(jnp.int32)
    channels = embed.shape[1]
    taps = conv_weight.shape[1]

    along_x, along_y = [], []
    for place in range(lax.axis_size("dp")):
        lines = ([[place * 16 + i * 4 + j for j in range(4)] for i in range(4)],
                 [[place * 16 + i * 4 + j for i in range(4)] for j in range(4)])
        along_x += lines[place % 2]
        along_y += lines[1 - place % 2]

    def ring(blocks, groups):
        return lax.all_to_all(
            blocks, ("dp", "section", "shard"), 0, 0, axis_index_groups=groups, tiled=True
        )

    slots = neighbours.shape[1]
    asked = jnp.concatenate([neighbours, counts[:, None]], axis=1)
    state = lax.broadcasted_iota(jnp.int32, asked.shape, 0)
    asked = jnp.sum(jnp.where(state == s, asked, 0), axis=0, keepdims=True)
    count = asked[:, slots]
    asked = exchange(jnp.broadcast_to(asked, (4, slots + 1)), "shard")

    unit = lax.dynamic_slice_in_dim(conv_weight[0].T, c * 32, 32, 0)
    unit = jnp.broadcast_to(unit[None], (4,) + unit.shape)
    asked, unit = lax.optimization_barrier((asked, unit))
    mine = ring(unit, along_x)
    mine = ring(jnp.broadcast_to(mine[None], (4,) + mine.shape), along_y)

    live = lax.broadcasted_iota(jnp.int32, (4, slots), 1) < asked[:, slots:]
    stored = database.shape[0]
    positions = lax.broadcasted_iota(jnp.int32, (1, 1, stored), 2) + h * stored
    hits = (asked[:, :slots, None] == positions) & live[:, :, None]
    picks = jnp.sum(hits.astype(F32), axis=1).astype(BF16)
    partial = jnp.dot(picks, database, preferred_element_type=F32)
    summed = lax.dynamic_slice_in_dim(partial, h, 1, 0)
    for d in (1, 2, 3):
        piece = lax.dynamic_slice_in_dim(partial, (h + 4 - d) % 4, 1, 0)
        summed = summed + turned(piece, "shard", -d)
    context = (summed / jnp.maximum(count, 1).astype(F32)[:, None]).astype(BF16)
    context = jnp.broadcast_to(context, (16, context.shape[1]))

    board = lax.dynamic_index_in_dim(boards, s, 0, keepdims=False).reshape(BOARD, BOARD)
    code = jnp.pad(board, ((0, 0), (0, 1)), constant_values=3).reshape(-1)
    code = jnp.pad(code, (0, ROWS - BOARD * PITCH), constant_values=3)
    upper = lax.dynamic_index_in_dim(cotangent, s, 0, keepdims=False)
    upper = jnp.pad(upper.reshape(BOARD, BOARD, channels), ((0, 0), (0, 1), (0, 0)))
    upper = jnp.pad(upper.reshape(-1, channels), ((0, ROWS - BOARD * PITCH), (0, 0)))

    mine, context, upper = lax.optimization_barrier((mine, context, upper))
    theirs = swap(mine, "dp", 1)
    width = context.shape[1]
    preact, hidden, encoded = vmem_call(
        encoder_kernel,
        (
            jax.ShapeDtypeStruct((16, width), F32),
            jax.ShapeDtypeStruct((16, width), BF16),
            jax.ShapeDtypeStruct((16, channels), F32),
        ),
        [],
        "encoder",
        2 * 16 * width * (width + channels),
        3 << 20,
    )(where, context, w_first, w_second)
    part = jax.ShapeDtypeStruct((4, 4, 32, taps + 256), BF16)
    own, other = vmem_call(
        trunk_kernel,
        (part, part),
        [
            pltpu.VMEM((4, channels, taps), BF16),
            pltpu.VMEM((4, ROWS, taps), BF16),
            pltpu.VMEM((4, channels, taps), BF16),
            pltpu.VMEM((4, ROWS, channels), F32),
            pltpu.VMEM((4, ROWS, 1), F32),
            pltpu.VMEM((2 * FRONT + ROWS, channels), F32),
            pltpu.VMEM((ROWS, channels), F32),
            pltpu.VMEM((32, 128), F32),
        ],
        "trunk",
        12 * 2 * ROWS * taps * channels,
        16 << 20,
    )(
        where, context, preact, hidden, encoded, w_second, embed,
        code[:, None], code[None, :], upper, mine, theirs,
    )

    pieces = ring((own.astype(F32) + swap(other, "dp", 1).astype(F32)).astype(BF16), along_x)
    (pieces,) = vmem_call(
        fold_kernel,
        (jax.ShapeDtypeStruct((4, 32, taps + 1024), BF16),),
        [],
        "fold",
        pieces.size,
        3 << 20,
    )(where, pieces)
    pieces = ring(pieces, along_y)
    (chunks,) = vmem_call(
        pack_kernel,
        (jax.ShapeDtypeStruct((32, 16, 256), BF16),),
        [
            pltpu.VMEM((1024, 128), F32),
            pltpu.VMEM((128, 1280), F32),
            pltpu.VMEM((16, 256), F32),
        ],
        "pack",
        4 * 32 * 128 * 1280,
        3 << 20,
    )(where, pieces)

    line = [[2 * i + core for i in range(lax.axis_size("dp") // 2)] for core in (0, 1)]

    def along_z(blocks):
        return lax.all_to_all(blocks, "dp", 0, 0, axis_index_groups=line, tiled=True)

    total = along_z(chunks.reshape(16, 2, 16, 256))
    total = jnp.sum(total.astype(F32), axis=0, keepdims=True).astype(BF16)
    chunks = along_z(jnp.broadcast_to(total, (16,) + total.shape[1:])).reshape(32, 16, 256)
    conv, w1_grad, w2_grad, embed_grad = vmem_call(
        finish_kernel,
        (
            jax.ShapeDtypeStruct((64, taps), BF16),
            jax.ShapeDtypeStruct((64, 1024), BF16),
            jax.ShapeDtypeStruct((64, channels), BF16),
            jax.ShapeDtypeStruct((3, channels), BF16),
        ),
        [],
        "finish",
        1 << 18,
        1 << 20,
    )(where, chunks, swap(chunks, "dp", 1))
    return (w1_grad, w2_grad, embed_grad, conv.T[None])


def solution(mesh):
    placed = (
        P(("dp", "shard"), None),
        P(("dp", "shard"), None),
        P(("dp", "shard")),
        P("shard", None),
        P(),
        P(),
        P(),
        P("section", None, "shard"),
        P(("dp", "shard"), None, None),
    )
    return jax.shard_map(
        body,
        mesh=mesh,
        in_specs=placed,
        out_specs=(
            P(("section", "shard"), None),
            P(("section", "shard"), None),
            P(),
            P("section", None, "shard"),
        ),
        check_vma=False,
    )
```

```python
import jax
import jax.numpy as jnp
from jax import lax
from jax.experimental import pallas as pl
from jax.experimental.pallas import tpu as pltpu
from jax.sharding import PartitionSpec as P

BOARD = 19
PITCH = 20
ROWS = 384
FRONT = 24
NORM_EPS = 1e-05
TAP_SHIFTS = [(a - 1) * PITCH + (b - 1) for a in range(3) for b in range(3)]
VMEM_BYTES = 40 * 1024 * 1024
F32 = jnp.float32
BF16 = jnp.bfloat16


def swap(block, axis, bits):
    return lax.ppermute(block, axis, [(i, i ^ bits) for i in range(lax.axis_size(axis))])


def turned(block, axis, distance):
    size = lax.axis_size(axis)
    return lax.ppermute(block, axis, [(i, (i + distance) % size) for i in range(size)])


def turned(block, axis, distance):
    size = lax.axis_size(axis)
    return lax.ppermute(block, axis, [(i, (i + distance) % size) for i in range(size)])


def exchange(blocks, axis):
    return lax.all_to_all(blocks, axis, 0, 0, tiled=True)


def nn(left, right):
    return lax.dot_general(left, right, (((1,), (0,)), ((), ())), preferred_element_type=F32)


def nt(left, right):
    return lax.dot_general(left, right, (((1,), (1,)), ((), ())), preferred_element_type=F32)


def tn(left, right):
    return lax.dot_general(left, right, (((0,), (0,)), ((), ())), preferred_element_type=F32)


def vmem_call(kernel, outs, scratch, name, flops, moved, far=0):
    spec = pl.BlockSpec(memory_space=pltpu.VMEM)

    def call(scalars, *arrays):
        return pl.pallas_call(
            kernel,
            out_shape=outs,
            in_specs=[pl.BlockSpec(memory_space=pltpu.SMEM)]
            + [spec] * (len(arrays) - far)
            + [pl.BlockSpec(memory_space=pltpu.HBM)] * far,
            out_specs=tuple(spec for _ in outs),
            scratch_shapes=scratch,
            compiler_params=pltpu.CompilerParams(vmem_limit_bytes=VMEM_BYTES),
            cost_estimate=pl.CostEstimate(flops=flops, bytes_accessed=moved, transcendentals=0),
            name=name,
        )(scalars, *arrays)

    return call


def encoder_kernel(where, context, w_first, w_second, preact, hidden, encoded):
    value = nn(context[...], w_first[...])
    preact[...] = value
    rounded = (value * (0.5 * (1.0 + lax.erf(value * 0.7071067811865476)))).astype(BF16)
    hidden[...] = rounded
    encoded[...] = nn(rounded, w_second[...])


def trunk_kernel(
    where, context, preact_in, hidden_in, encoded_in, w_second, embed, code_col, code_row, cotangent,
    mine, theirs,
    own, other,
    wt, patches, normed, rscales, buf, grad, vectors, arrived,
):
    c = where[2]

    def block_rows(outer, inner, core):
        block = jnp.where(core == 0, inner, outer)
        shard = jnp.where(core == 0, outer, inner)
        return block, pl.ds(pl.multiple_of(shard * 64 + core * 32, 32), 32)

    copies = []
    for place in range(16):
        outer, inner = divmod(place, 4)
        block, rows = block_rows(inner, outer, 1 - c)
        copies.append(
            pltpu.make_async_copy(
                theirs.at[outer, inner], wt.at[block, rows, :], arrived.at[place]
            )
        )
        copies[-1].start()
    for place in range(16):
        outer, inner = divmod(place, 4)
        block, rows = block_rows(inner, outer, c)
        wt[block, rows, :] = mine[outer, inner]

    point = lax.broadcasted_iota(jnp.int32, (ROWS, 1), 0)
    column = point - ((point * 3277) >> 16) * PITCH
    mask = jnp.where((column < BOARD) & (point < BOARD * PITCH), 1.0, 0.0).astype(F32)

    preact, hidden, encoded = preact_in[...], hidden_in[...], encoded_in[...]
    code = code_col[...]
    stone = embed[...].astype(F32)
    stones = jnp.where(code == 0, stone[0:1], jnp.where(code == 1, stone[1:2], stone[2:3]))
    start = (stones + encoded[0:1]).astype(BF16).astype(F32) * mask

    buf[0:FRONT, :] = jnp.zeros((FRONT, buf.shape[1]), F32)
    buf[FRONT + ROWS :, :] = jnp.zeros((FRONT, buf.shape[1]), F32)
    buf[FRONT : FRONT + ROWS, :] = start
    channels = start.shape[1]
    taps = wt.shape[2]

    def forward(block, carry):
        for tap, shift in enumerate(TAP_SHIFTS):
            patches[block, :, tap * channels : (tap + 1) * channels] = buf[
                FRONT + shift : FRONT + shift + ROWS, :
            ].astype(BF16)
        zconv = nt(patches[block], wt[block])
        rscale = lax.rsqrt(jnp.mean(zconv * zconv, axis=-1, keepdims=True) + NORM_EPS)
        value = zconv * rscale
        normed[block] = value
        rscales[block] = rscale
        stream = buf[FRONT : FRONT + ROWS, :] + value * jax.nn.sigmoid(value)
        buf[FRONT : FRONT + ROWS, :] = stream.astype(BF16).astype(F32) * mask
        return carry

    for copy in copies:
        copy.wait()
    lax.fori_loop(0, 4, forward, 0)
    grad[...] = cotangent[...].astype(F32)

    def backward(step, carry):
        block = 3 - step
        value = normed[block]
        upper = grad[...]
        sigma = jax.nn.sigmoid(value)
        dnorm = upper * (sigma * (1.0 + value * (1.0 - sigma)))
        inner = jnp.mean(dnorm * value, axis=-1, keepdims=True)
        dconv = rscales[block] * (dnorm - value * inner)
        product = nn(dconv.T.astype(BF16), patches[block]).astype(BF16)
        for half in range(2):
            for pieces, core in ((own, half), (other, 1 - half)):

                @pl.when(c == core)
                def _():
                    for shard in range(4):
                        outer = shard if half == 0 else block
                        inner = block if half == 0 else shard
                        first = shard * 64 + half * 32
                        pieces[outer, inner, :, 0:taps] = product[first : first + 32]

        buf[FRONT : FRONT + ROWS, :] = dconv.astype(BF16).astype(F32)
        total = upper
        for tap, shift in enumerate(TAP_SHIFTS):
            total += nn(
                buf[FRONT - shift : FRONT - shift + ROWS, :].astype(BF16),
                wt[block, :, tap * channels : (tap + 1) * channels],
            )
        grad[...] = total.astype(BF16).astype(F32) * mask
        return carry

    lax.fori_loop(0, 4, backward, 0)

    kind = lax.broadcasted_iota(jnp.int32, (16, ROWS), 0)
    codes = code_row[...]
    picked = ((kind < 3) & (codes == kind)) | ((kind == 3) & (codes < 3))
    sums = nn(jnp.where(picked, 1.0, 0.0).astype(BF16), grad[...].astype(BF16))
    rounded = sums.astype(BF16)
    cdf = 0.5 * (1.0 + lax.erf(preact * 0.7071067811865476))
    density = jnp.exp(-0.5 * preact * preact) * 0.3989422804014327
    pre_grad = (nt(rounded, w_second[...]) * (cdf + preact * density)).astype(BF16)
    parts = ((context[...], 0, 8), (hidden, 0, 8), (pre_grad, 3, 8))
    parts += tuple((rounded, row, 2) for row in (3, 0, 1, 2))
    place = 0
    for array, row, count in parts:
        for piece in range(count):
            vectors[place : place + 1, :] = array.astype(F32)[
                row : row + 1, piece * 128 : (piece + 1) * 128
            ]
            place += 1
    tail = vectors[...].astype(BF16)
    empty = jnp.zeros(tail.shape, BF16)
    for pieces, first, second in ((own, tail, empty), (other, empty, tail)):
        for outer in range(4):
            for inner in range(4):
                pieces[outer, inner, :, taps : taps + 128] = first
                pieces[outer, inner, :, taps + 128 :] = second


def fold_kernel(where, pieces, out):
    taps = pieces.shape[3] - 256
    for inner in range(4):
        total = pieces[0, inner, :, 0:taps].astype(F32)
        for source in range(1, 4):
            total += pieces[source, inner, :, 0:taps].astype(F32)
        out[inner, :, 0:taps] = total.astype(BF16)
        for source in range(4):
            lane = taps + source * 256
            out[inner, :, lane : lane + 256] = pieces[source, inner, :, taps:]


def pack_kernel(where, pieces, out, vectors, product, stones):
    first = where[0] * 256 + where[1] * 64 + where[2] * 32
    row = first // 128
    rows = pl.ds(pl.multiple_of(first - row * 128, 32), 32)
    taps = pieces.shape[2] - 1024
    for state in range(32):
        lane = taps + state % 8 * 128
        vectors[state * 32 : (state + 1) * 32, :] = pieces[state // 8, :, lane : lane + 128].astype(F32)

    def of_states(place):
        return vectors[pl.ds(place, 32, stride=32), :]

    context = of_states(row).astype(BF16)
    hidden = of_states(row + 8).astype(BF16)
    for piece in range(8):
        lanes = slice(piece * 128, (piece + 1) * 128)
        product[:, lanes] = tn(context, of_states(16 + piece).astype(BF16))
    for piece in range(2):
        lanes = slice(1024 + piece * 128, 1024 + (piece + 1) * 128)
        product[:, lanes] = tn(hidden, of_states(24 + piece).astype(BF16))
    stones[...] = jnp.zeros(stones.shape, F32)
    for piece in range(6):
        v, half = divmod(piece, 2)
        stones[v : v + 1, half * 128 : (half + 1) * 128] = jnp.sum(
            of_states(26 + piece), axis=0, keepdims=True
        )
    for column in range(taps // 256):
        lanes = slice(column * 256, (column + 1) * 256)
        block = pieces[0, :, lanes].astype(F32)
        for piece in range(1, 4):
            block += pieces[piece, :, lanes].astype(F32)
        out[2 * column] = block[0:16].astype(BF16)
        out[2 * column + 1] = block[16:32].astype(BF16)
    for column in range(5):
        block = product[rows, column * 256 : (column + 1) * 256]
        place = 2 * (taps // 256 + column)
        out[place] = block[0:16].astype(BF16)
        out[place + 1] = block[16:32].astype(BF16)
    out[28] = stones[...].astype(BF16)
    for place in (29, 30, 31):
        out[place] = jnp.zeros(out.shape[1:], BF16)


def finish_kernel(where, mine, theirs, conv, first, second, stones):
    c = where[2]
    for out, start in ((conv, 0), (first, conv.shape[1]), (second, conv.shape[1] + first.shape[1])):
        for column in range(out.shape[1] // 256):
            for half in range(2):
                for core, pieces in ((c, mine), (1 - c, theirs)):
                    rows = pl.ds(pl.multiple_of(core * 32 + half * 16, 16), 16)
                    out[rows, column * 256 : (column + 1) * 256] = (
                        pieces[2 * (start // 256 + column) + half].astype(F32) * (1.0 / 512.0)
                    ).astype(BF16)
    stones[...] = (mine[28].astype(F32) * (1.0 / 512.0))[0:3].astype(BF16)


def body(boards, neighbours, counts, database, w_first, w_second, embed, conv_weight, cotangent):
    h = lax.axis_index("shard")
    s = lax.axis_index("section")
    dp = lax.axis_index("dp")
    c = dp % 2
    where = jnp.stack([s, h, c]).astype(jnp.int32)
    channels = embed.shape[1]
    taps = conv_weight.shape[1]

    along_x, along_y = [], []
    for place in range(lax.axis_size("dp")):
        lines = ([[place * 16 + i * 4 + j for j in range(4)] for i in range(4)],
                 [[place * 16 + i * 4 + j for i in range(4)] for j in range(4)])
        along_x += lines[place % 2]
        along_y += lines[1 - place % 2]

    def ring(blocks, groups):
        return lax.all_to_all(
            blocks, ("dp", "section", "shard"), 0, 0, axis_index_groups=groups, tiled=True
        )

    slots = neighbours.shape[1]
    asked = jnp.concatenate([neighbours, counts[:, None]], axis=1)
    state = lax.broadcasted_iota(jnp.int32, asked.shape, 0)
    asked = jnp.sum(jnp.where(state == s, asked, 0), axis=0, keepdims=True)
    count = asked[:, slots]
    asked = jnp.concatenate([asked] + [turned(asked, "shard", d) for d in (1, 2, 3)])

    unit = lax.dynamic_slice_in_dim(conv_weight[0].T, c * 32, 32, 0)
    unit = jnp.broadcast_to(unit[None], (4,) + unit.shape)
    mine = ring(unit, along_x)
    asked, mine = lax.optimization_barrier((asked, mine))
    mine = ring(jnp.broadcast_to(mine[None], (4,) + mine.shape), along_y)

    live = lax.broadcasted_iota(jnp.int32, (4, slots), 1) < asked[:, slots:]
    stored = database.shape[0]
    positions = lax.broadcasted_iota(jnp.int32, (1, 1, stored), 2) + h * stored
    hits = (asked[:, :slots, None] == positions) & live[:, :, None]
    picks = jnp.sum(hits.astype(F32), axis=1).astype(BF16)
    partial = jnp.dot(picks, database, preferred_element_type=F32)
    summed = partial[0:1]
    for d in (1, 2, 3):
        summed = summed + turned(partial[d : d + 1], "shard", -d)
    context = (summed / jnp.maximum(count, 1).astype(F32)[:, None]).astype(BF16)
    context = jnp.broadcast_to(context, (16, context.shape[1]))

    board = lax.dynamic_index_in_dim(boards, s, 0, keepdims=False).reshape(BOARD, BOARD)
    code = jnp.pad(board, ((0, 0), (0, 1)), constant_values=3).reshape(-1)
    code = jnp.pad(code, (0, ROWS - BOARD * PITCH), constant_values=3)
    upper = lax.dynamic_index_in_dim(cotangent, s, 0, keepdims=False)
    upper = jnp.pad(upper.reshape(BOARD, BOARD, channels), ((0, 0), (0, 1), (0, 0)))
    upper = jnp.pad(upper.reshape(-1, channels), ((0, ROWS - BOARD * PITCH), (0, 0)))

    mine, context, upper = lax.optimization_barrier((mine, context, upper))
    theirs = swap(mine, "dp", 1)
    width = context.shape[1]
    preact, hidden, encoded = vmem_call(
        encoder_kernel,
        (
            jax.ShapeDtypeStruct((16, width), F32),
            jax.ShapeDtypeStruct((16, width), BF16),
            jax.ShapeDtypeStruct((16, channels), F32),
        ),
        [],
        "encoder",
        2 * 16 * width * (width + channels),
        3 << 20,
    )(where, context, w_first, w_second)
    part = jax.ShapeDtypeStruct((4, 4, 32, taps + 256), BF16)
    own, other = vmem_call(
        trunk_kernel,
        (part, part),
        [
            pltpu.VMEM((4, channels, taps), BF16),
            pltpu.VMEM((4, ROWS, taps), BF16),
            pltpu.VMEM((4, ROWS, channels), F32),
            pltpu.VMEM((4, ROWS, 1), F32),
            pltpu.VMEM((2 * FRONT + ROWS, channels), F32),
            pltpu.VMEM((ROWS, channels), F32),
            pltpu.VMEM((32, 128), F32),
            pltpu.SemaphoreType.DMA((16,)),
        ],
        "trunk",
        12 * 2 * ROWS * taps * channels,
        16 << 20,
        far=1,
    )(
        where, context, preact, hidden, encoded, w_second, embed,
        code[:, None], code[None, :], upper, mine, theirs,
    )

    pieces = ring((own.astype(F32) + swap(other, "dp", 1).astype(F32)).astype(BF16), along_x)
    (pieces,) = vmem_call(
        fold_kernel,
        (jax.ShapeDtypeStruct((4, 32, taps + 1024), BF16),),
        [],
        "fold",
        pieces.size,
        3 << 20,
    )(where, pieces)
    pieces = ring(pieces, along_y)
    (chunks,) = vmem_call(
        pack_kernel,
        (jax.ShapeDtypeStruct((32, 16, 256), BF16),),
        [
            pltpu.VMEM((1024, 128), F32),
            pltpu.VMEM((128, 1280), F32),
            pltpu.VMEM((16, 256), F32),
        ],
        "pack",
        4 * 32 * 128 * 1280,
        3 << 20,
    )(where, pieces)

    line = [[2 * i + core for i in range(lax.axis_size("dp") // 2)] for core in (0, 1)]

    def along_z(blocks):
        return lax.all_to_all(blocks, "dp", 0, 0, axis_index_groups=line, tiled=True)

    total = along_z(chunks.reshape(16, 2, 16, 256))
    total = jnp.sum(total.astype(F32), axis=0, keepdims=True).astype(BF16)
    chunks = along_z(jnp.broadcast_to(total, (16,) + total.shape[1:])).reshape(32, 16, 256)
    conv, w1_grad, w2_grad, embed_grad = vmem_call(
        finish_kernel,
        (
            jax.ShapeDtypeStruct((64, taps), BF16),
            jax.ShapeDtypeStruct((64, 1024), BF16),
            jax.ShapeDtypeStruct((64, channels), BF16),
            jax.ShapeDtypeStruct((3, channels), BF16),
        ),
        [],
        "finish",
        1 << 18,
        1 << 20,
    )(where, chunks, swap(chunks, "dp", 1))
    return (w1_grad, w2_grad, embed_grad, conv.T[None])


def solution(mesh):
    placed = (
        P(("dp", "shard"), None),
        P(("dp", "shard"), None),
        P(("dp", "shard")),
        P("shard", None),
        P(),
        P(),
        P(),
        P("section", None, "shard"),
        P(("dp", "shard"), None, None),
    )
    return jax.shard_map(
        body,
        mesh=mesh,
        in_specs=placed,
        out_specs=(
            P(("section", "shard"), None),
            P(("section", "shard"), None),
            P(),
            P("section", None, "shard"),
        ),
        check_vma=False,
    )
```

```python
import jax
import jax.numpy as jnp
from jax import lax
from jax.experimental import pallas as pl
from jax.experimental.pallas import tpu as pltpu
from jax.sharding import PartitionSpec as P

BOARD = 19
PITCH = 20
ROWS = 384
FRONT = 24
NORM_EPS = 1e-05
TAP_SHIFTS = [(a - 1) * PITCH + (b - 1) for a in range(3) for b in range(3)]
VMEM_BYTES = 40 * 1024 * 1024
F32 = jnp.float32
BF16 = jnp.bfloat16


def swap(block, axis, bits):
    return lax.ppermute(block, axis, [(i, i ^ bits) for i in range(lax.axis_size(axis))])


def exchange(blocks, axis):
    return lax.all_to_all(blocks, axis, 0, 0, tiled=True)


def turned(block, axis, distance):
    size = lax.axis_size(axis)
    return lax.ppermute(block, axis, [(i, (i + distance) % size) for i in range(size)])


def turned(block, axis, distance):
    size = lax.axis_size(axis)
    return lax.ppermute(block, axis, [(i, (i + distance) % size) for i in range(size)])


def exchange(blocks, axis):
    return lax.all_to_all(blocks, axis, 0, 0, tiled=True)


def nn(left, right):
    return lax.dot_general(left, right, (((1,), (0,)), ((), ())), preferred_element_type=F32)


def nt(left, right):
    return lax.dot_general(left, right, (((1,), (1,)), ((), ())), preferred_element_type=F32)


def tn(left, right):
    return lax.dot_general(left, right, (((0,), (0,)), ((), ())), preferred_element_type=F32)


def vmem_call(kernel, outs, scratch, name, flops, moved, far=0):
    spec = pl.BlockSpec(memory_space=pltpu.VMEM)

    def call(scalars, *arrays):
        return pl.pallas_call(
            kernel,
            out_shape=outs,
            in_specs=[pl.BlockSpec(memory_space=pltpu.SMEM)]
            + [spec] * (len(arrays) - far)
            + [pl.BlockSpec(memory_space=pltpu.HBM)] * far,
            out_specs=tuple(spec for _ in outs),
            scratch_shapes=scratch,
            compiler_params=pltpu.CompilerParams(vmem_limit_bytes=VMEM_BYTES),
            cost_estimate=pl.CostEstimate(flops=flops, bytes_accessed=moved, transcendentals=0),
            name=name,
        )(scalars, *arrays)

    return call


def encoder_kernel(where, context, w_first, w_second, preact, hidden, encoded):
    value = nn(context[...], w_first[...])
    preact[...] = value
    rounded = (value * (0.5 * (1.0 + lax.erf(value * 0.7071067811865476)))).astype(BF16)
    hidden[...] = rounded
    encoded[...] = nn(rounded, w_second[...])


def trunk_kernel(
    where, context, preact_in, hidden_in, encoded_in, w_second, embed, code_col, code_row, cotangent,
    mine, theirs,
    own, other,
    wt, patches, gt, normed, rscales, buf, grad, vectors, arrived,
):
    c = where[2]

    def block_rows(outer, inner, core):
        block = jnp.where(core == 0, inner, outer)
        shard = jnp.where(core == 0, outer, inner)
        return block, pl.ds(pl.multiple_of(shard * 64 + core * 32, 32), 32)

    copies = []
    for place in range(16):
        outer, inner = divmod(place, 4)
        block, rows = block_rows(inner, outer, 1 - c)
        copies.append(
            pltpu.make_async_copy(
                theirs.at[outer, inner], wt.at[block, rows, :], arrived.at[place]
            )
        )
        copies[-1].start()
    for place in range(16):
        outer, inner = divmod(place, 4)
        block, rows = block_rows(inner, outer, c)
        wt[block, rows, :] = mine[outer, inner]

    point = lax.broadcasted_iota(jnp.int32, (ROWS, 1), 0)
    column = point - ((point * 3277) >> 16) * PITCH
    mask = jnp.where((column < BOARD) & (point < BOARD * PITCH), 1.0, 0.0).astype(F32)

    preact, hidden, encoded = preact_in[...], hidden_in[...], encoded_in[...]
    code = code_col[...]
    stone = embed[...].astype(F32)
    stones = jnp.where(code == 0, stone[0:1], jnp.where(code == 1, stone[1:2], stone[2:3]))
    start = (stones + encoded[0:1]).astype(BF16).astype(F32) * mask

    buf[0:FRONT, :] = jnp.zeros((FRONT, buf.shape[1]), F32)
    buf[FRONT + ROWS :, :] = jnp.zeros((FRONT, buf.shape[1]), F32)
    buf[FRONT : FRONT + ROWS, :] = start
    channels = start.shape[1]
    taps = wt.shape[2]

    def forward(block, carry):
        for tap, shift in enumerate(TAP_SHIFTS):
            patches[block, :, tap * channels : (tap + 1) * channels] = buf[
                FRONT + shift : FRONT + shift + ROWS, :
            ].astype(BF16)
        zconv = nt(patches[block], wt[block])
        rscale = lax.rsqrt(jnp.mean(zconv * zconv, axis=-1, keepdims=True) + NORM_EPS)
        value = zconv * rscale
        normed[block] = value
        rscales[block] = rscale
        stream = buf[FRONT : FRONT + ROWS, :] + value * jax.nn.sigmoid(value)
        buf[FRONT : FRONT + ROWS, :] = stream.astype(BF16).astype(F32) * mask
        return carry

    for copy in copies:
        copy.wait()
    lax.fori_loop(0, 4, forward, 0)
    grad[...] = cotangent[...].astype(F32)

    def backward(step, carry):
        block = 3 - step
        value = normed[block]
        upper = grad[...]
        sigma = jax.nn.sigmoid(value)
        dnorm = upper * (sigma * (1.0 + value * (1.0 - sigma)))
        inner = jnp.mean(dnorm * value, axis=-1, keepdims=True)
        dconv = rscales[block] * (dnorm - value * inner)
        gt[block] = nn(dconv.T.astype(BF16), patches[block]).astype(BF16)
        buf[FRONT : FRONT + ROWS, :] = dconv.astype(BF16).astype(F32)
        moved = [
            buf[FRONT - shift : FRONT - shift + ROWS, :].astype(BF16) for shift in TAP_SHIFTS
        ]
        weights = [wt[block, :, tap * channels : (tap + 1) * channels] for tap in range(9)]
        total = upper + nn(jnp.concatenate(moved, axis=1), jnp.concatenate(weights, axis=0))
        grad[...] = total.astype(BF16).astype(F32) * mask
        return carry

    lax.fori_loop(0, 4, backward, 0)

    kind = lax.broadcasted_iota(jnp.int32, (16, ROWS), 0)
    codes = code_row[...]
    picked = ((kind < 3) & (codes == kind)) | ((kind == 3) & (codes < 3))
    sums = nn(jnp.where(picked, 1.0, 0.0).astype(BF16), grad[...].astype(BF16))
    rounded = sums.astype(BF16)
    cdf = 0.5 * (1.0 + lax.erf(preact * 0.7071067811865476))
    density = jnp.exp(-0.5 * preact * preact) * 0.3989422804014327
    pre_grad = (nt(rounded, w_second[...]) * (cdf + preact * density)).astype(BF16)
    parts = ((context[...], 0, 8), (hidden, 0, 8), (pre_grad, 3, 8))
    parts += tuple((rounded, row, 2) for row in (3, 0, 1, 2))
    place = 0
    for array, row, count in parts:
        for piece in range(count):
            vectors[place : place + 1, :] = array.astype(F32)[
                row : row + 1, piece * 128 : (piece + 1) * 128
            ]
            place += 1
    tail = vectors[...].astype(BF16)
    empty = jnp.zeros(tail.shape, BF16)
    for core, pieces, first, second in ((c, own, tail, empty), (1 - c, other, empty, tail)):
        for outer in range(4):
            for inner in range(4):
                block, rows = block_rows(outer, inner, core)
                pieces[outer, inner, :, 0:taps] = gt[block, rows, :]
                pieces[outer, inner, :, taps : taps + 128] = first
                pieces[outer, inner, :, taps + 128 :] = second


def fold_kernel(where, pieces, out):
    taps = pieces.shape[3] - 256
    for inner in range(4):
        total = pieces[0, inner, :, 0:taps].astype(F32)
        for source in range(1, 4):
            total += pieces[source, inner, :, 0:taps].astype(F32)
        out[inner, :, 0:taps] = total.astype(BF16)
        for source in range(4):
            lane = taps + source * 256
            out[inner, :, lane : lane + 256] = pieces[source, inner, :, taps:]


def pack_kernel(where, pieces, out, vectors, product, stones):
    first = where[0] * 256 + where[1] * 64 + where[2] * 32
    row = first // 128
    rows = pl.ds(pl.multiple_of(first - row * 128, 32), 32)
    taps = pieces.shape[2] - 1024
    for state in range(32):
        lane = taps + state % 8 * 128
        vectors[state * 32 : (state + 1) * 32, :] = pieces[state // 8, :, lane : lane + 128].astype(F32)

    def of_states(place):
        return vectors[pl.ds(place, 32, stride=32), :]

    context = of_states(row).astype(BF16)
    hidden = of_states(row + 8).astype(BF16)
    for piece in range(8):
        lanes = slice(piece * 128, (piece + 1) * 128)
        product[:, lanes] = tn(context, of_states(16 + piece).astype(BF16))
    for piece in range(2):
        lanes = slice(1024 + piece * 128, 1024 + (piece + 1) * 128)
        product[:, lanes] = tn(hidden, of_states(24 + piece).astype(BF16))
    stones[...] = jnp.zeros(stones.shape, F32)
    for piece in range(6):
        v, half = divmod(piece, 2)
        stones[v : v + 1, half * 128 : (half + 1) * 128] = jnp.sum(
            of_states(26 + piece), axis=0, keepdims=True
        )
    for column in range(taps // 256):
        lanes = slice(column * 256, (column + 1) * 256)
        block = pieces[0, :, lanes].astype(F32)
        for piece in range(1, 4):
            block += pieces[piece, :, lanes].astype(F32)
        out[2 * column] = block[0:16].astype(BF16)
        out[2 * column + 1] = block[16:32].astype(BF16)
    for column in range(5):
        block = product[rows, column * 256 : (column + 1) * 256]
        place = 2 * (taps // 256 + column)
        out[place] = block[0:16].astype(BF16)
        out[place + 1] = block[16:32].astype(BF16)
    out[28] = stones[...].astype(BF16)
    for place in (29, 30, 31):
        out[place] = jnp.zeros(out.shape[1:], BF16)


def finish_kernel(where, mine, theirs, conv, first, second, stones):
    c = where[2]
    for out, start in ((conv, 0), (first, conv.shape[1]), (second, conv.shape[1] + first.shape[1])):
        for column in range(out.shape[1] // 256):
            for half in range(2):
                for core, pieces in ((c, mine), (1 - c, theirs)):
                    rows = pl.ds(pl.multiple_of(core * 32 + half * 16, 16), 16)
                    out[rows, column * 256 : (column + 1) * 256] = (
                        pieces[2 * (start // 256 + column) + half].astype(F32) * (1.0 / 512.0)
                    ).astype(BF16)
    stones[...] = (mine[28].astype(F32) * (1.0 / 512.0))[0:3].astype(BF16)


def body(boards, neighbours, counts, database, w_first, w_second, embed, conv_weight, cotangent):
    h = lax.axis_index("shard")
    s = lax.axis_index("section")
    dp = lax.axis_index("dp")
    c = dp % 2
    where = jnp.stack([s, h, c]).astype(jnp.int32)
    channels = embed.shape[1]
    taps = conv_weight.shape[1]

    along_x, along_y = [], []
    for place in range(lax.axis_size("dp")):
        lines = ([[place * 16 + i * 4 + j for j in range(4)] for i in range(4)],
                 [[place * 16 + i * 4 + j for i in range(4)] for j in range(4)])
        along_x += lines[place % 2]
        along_y += lines[1 - place % 2]

    def ring(blocks, groups):
        return lax.all_to_all(
            blocks, ("dp", "section", "shard"), 0, 0, axis_index_groups=groups, tiled=True
        )

    slots = neighbours.shape[1]
    asked = jnp.concatenate([neighbours, counts[:, None]], axis=1)
    state = lax.broadcasted_iota(jnp.int32, asked.shape, 0)
    asked = jnp.sum(jnp.where(state == s, asked, 0), axis=0, keepdims=True)
    count = asked[:, slots]
    asked = exchange(jnp.broadcast_to(asked, (4, slots + 1)), "shard")

    unit = lax.dynamic_slice_in_dim(conv_weight[0].T, c * 32, 32, 0)
    unit = jnp.broadcast_to(unit[None], (4,) + unit.shape)
    mine = ring(unit, along_x)
    asked, mine = lax.optimization_barrier((asked, mine))
    mine = ring(jnp.broadcast_to(mine[None], (4,) + mine.shape), along_y)

    live = lax.broadcasted_iota(jnp.int32, (4, slots), 1) < asked[:, slots:]
    stored = database.shape[0]
    positions = lax.broadcasted_iota(jnp.int32, (1, 1, stored), 2) + h * stored
    hits = (asked[:, :slots, None] == positions) & live[:, :, None]
    picks = jnp.sum(hits.astype(F32), axis=1).astype(BF16)
    partial = jnp.dot(picks, database, preferred_element_type=F32)
    summed = lax.dynamic_slice_in_dim(partial, h, 1, 0)
    for d in (1, 2, 3):
        piece = lax.dynamic_slice_in_dim(partial, (h + 4 - d) % 4, 1, 0)
        summed = summed + turned(piece, "shard", -d)
    context = (summed / jnp.maximum(count, 1).astype(F32)[:, None]).astype(BF16)
    context = jnp.broadcast_to(context, (16, context.shape[1]))

    board = lax.dynamic_index_in_dim(boards, s, 0, keepdims=False).reshape(BOARD, BOARD)
    code = jnp.pad(board, ((0, 0), (0, 1)), constant_values=3).reshape(-1)
    code = jnp.pad(code, (0, ROWS - BOARD * PITCH), constant_values=3)
    upper = lax.dynamic_index_in_dim(cotangent, s, 0, keepdims=False)
    upper = jnp.pad(upper.reshape(BOARD, BOARD, channels), ((0, 0), (0, 1), (0, 0)))
    upper = jnp.pad(upper.reshape(-1, channels), ((0, ROWS - BOARD * PITCH), (0, 0)))

    mine, context, upper = lax.optimization_barrier((mine, context, upper))
    theirs = swap(mine, "dp", 1)
    width = context.shape[1]
    preact, hidden, encoded = vmem_call(
        encoder_kernel,
        (
            jax.ShapeDtypeStruct((16, width), F32),
            jax.ShapeDtypeStruct((16, width), BF16),
            jax.ShapeDtypeStruct((16, channels), F32),
        ),
        [],
        "encoder",
        2 * 16 * width * (width + channels),
        3 << 20,
    )(where, context, w_first, w_second)
    part = jax.ShapeDtypeStruct((4, 4, 32, taps + 256), BF16)
    own, other = vmem_call(
        trunk_kernel,
        (part, part),
        [
            pltpu.VMEM((4, channels, taps), BF16),
            pltpu.VMEM((4, ROWS, taps), BF16),
            pltpu.VMEM((4, channels, taps), BF16),
            pltpu.VMEM((4, ROWS, channels), F32),
            pltpu.VMEM((4, ROWS, 1), F32),
            pltpu.VMEM((2 * FRONT + ROWS, channels), F32),
            pltpu.VMEM((ROWS, channels), F32),
            pltpu.VMEM((32, 128), F32),
            pltpu.SemaphoreType.DMA((16,)),
        ],
        "trunk",
        12 * 2 * ROWS * taps * channels,
        16 << 20,
        far=1,
    )(
        where, context, preact, hidden, encoded, w_second, embed,
        code[:, None], code[None, :], upper, mine, theirs,
    )

    pieces = ring((own.astype(F32) + swap(other, "dp", 1).astype(F32)).astype(BF16), along_x)
    (pieces,) = vmem_call(
        fold_kernel,
        (jax.ShapeDtypeStruct((4, 32, taps + 1024), BF16),),
        [],
        "fold",
        pieces.size,
        3 << 20,
    )(where, pieces)
    pieces = ring(pieces, along_y)
    (chunks,) = vmem_call(
        pack_kernel,
        (jax.ShapeDtypeStruct((32, 16, 256), BF16),),
        [
            pltpu.VMEM((1024, 128), F32),
            pltpu.VMEM((128, 1280), F32),
            pltpu.VMEM((16, 256), F32),
        ],
        "pack",
        4 * 32 * 128 * 1280,
        3 << 20,
    )(where, pieces)

    line = [[2 * i + core for i in range(lax.axis_size("dp") // 2)] for core in (0, 1)]

    def along_z(blocks):
        return lax.all_to_all(blocks, "dp", 0, 0, axis_index_groups=line, tiled=True)

    total = along_z(chunks.reshape(16, 2, 16, 256))
    total = jnp.sum(total.astype(F32), axis=0, keepdims=True).astype(BF16)
    chunks = along_z(jnp.broadcast_to(total, (16,) + total.shape[1:])).reshape(32, 16, 256)
    conv, w1_grad, w2_grad, embed_grad = vmem_call(
        finish_kernel,
        (
            jax.ShapeDtypeStruct((64, taps), BF16),
            jax.ShapeDtypeStruct((64, 1024), BF16),
            jax.ShapeDtypeStruct((64, channels), BF16),
            jax.ShapeDtypeStruct((3, channels), BF16),
        ),
        [],
        "finish",
        1 << 18,
        1 << 20,
    )(where, chunks, swap(chunks, "dp", 1))
    return (w1_grad, w2_grad, embed_grad, conv.T[None])


def solution(mesh):
    placed = (
        P(("dp", "shard"), None),
        P(("dp", "shard"), None),
        P(("dp", "shard")),
        P("shard", None),
        P(),
        P(),
        P(),
        P("section", None, "shard"),
        P(("dp", "shard"), None, None),
    )
    return jax.shard_map(
        body,
        mesh=mesh,
        in_specs=placed,
        out_specs=(
            P(("section", "shard"), None),
            P(("section", "shard"), None),
            P(),
            P("section", None, "shard"),
        ),
        check_vma=False,
    )
```

```python
import jax
import jax.numpy as jnp
from jax import lax
from jax.experimental import pallas as pl
from jax.experimental.pallas import tpu as pltpu
from jax.sharding import PartitionSpec as P

BOARD = 19
PITCH = 20
ROWS = 384
FRONT = 24
NORM_EPS = 1e-05
TAP_SHIFTS = [(a - 1) * PITCH + (b - 1) for a in range(3) for b in range(3)]
VMEM_BYTES = 40 * 1024 * 1024
F32 = jnp.float32
BF16 = jnp.bfloat16


def swap(block, axis, bits):
    return lax.ppermute(block, axis, [(i, i ^ bits) for i in range(lax.axis_size(axis))])


def turned(block, axis, distance):
    size = lax.axis_size(axis)
    return lax.ppermute(block, axis, [(i, (i + distance) % size) for i in range(size)])


def turned(block, axis, distance):
    size = lax.axis_size(axis)
    return lax.ppermute(block, axis, [(i, (i + distance) % size) for i in range(size)])


def exchange(blocks, axis):
    return lax.all_to_all(blocks, axis, 0, 0, tiled=True)


def nn(left, right):
    return lax.dot_general(left, right, (((1,), (0,)), ((), ())), preferred_element_type=F32)


def nt(left, right):
    return lax.dot_general(left, right, (((1,), (1,)), ((), ())), preferred_element_type=F32)


def tn(left, right):
    return lax.dot_general(left, right, (((0,), (0,)), ((), ())), preferred_element_type=F32)


def vmem_call(kernel, outs, scratch, name, flops, moved, far=0):
    spec = pl.BlockSpec(memory_space=pltpu.VMEM)

    def call(scalars, *arrays):
        return pl.pallas_call(
            kernel,
            out_shape=outs,
            in_specs=[pl.BlockSpec(memory_space=pltpu.SMEM)]
            + [spec] * (len(arrays) - far)
            + [pl.BlockSpec(memory_space=pltpu.HBM)] * far,
            out_specs=tuple(spec for _ in outs),
            scratch_shapes=scratch,
            compiler_params=pltpu.CompilerParams(vmem_limit_bytes=VMEM_BYTES),
            cost_estimate=pl.CostEstimate(flops=flops, bytes_accessed=moved, transcendentals=0),
            name=name,
        )(scalars, *arrays)

    return call


def encoder_kernel(where, context, w_first, w_second, preact, hidden, encoded):
    value = nn(context[...], w_first[...])
    preact[...] = value
    rounded = (value * (0.5 * (1.0 + lax.erf(value * 0.7071067811865476)))).astype(BF16)
    hidden[...] = rounded
    encoded[...] = nn(rounded, w_second[...])


def trunk_kernel(
    where, context, preact_in, hidden_in, encoded_in, w_second, embed, code_col, code_row, cotangent,
    mine, theirs,
    own, other,
    wt, patches, gt, normed, rscales, buf, grad, vectors, arrived,
):
    c = where[2]

    def block_rows(outer, inner, core):
        block = jnp.where(core == 0, inner, outer)
        shard = jnp.where(core == 0, outer, inner)
        return block, pl.ds(pl.multiple_of(shard * 64 + core * 32, 32), 32)

    copies = []
    for place in range(16):
        outer, inner = divmod(place, 4)
        block, rows = block_rows(inner, outer, 1 - c)
        copies.append(
            pltpu.make_async_copy(
                theirs.at[outer, inner], wt.at[block, rows, :], arrived.at[place]
            )
        )
        copies[-1].start()
    for place in range(16):
        outer, inner = divmod(place, 4)
        block, rows = block_rows(inner, outer, c)
        wt[block, rows, :] = mine[outer, inner]

    point = lax.broadcasted_iota(jnp.int32, (ROWS, 1), 0)
    column = point - ((point * 3277) >> 16) * PITCH
    mask = jnp.where((column < BOARD) & (point < BOARD * PITCH), 1.0, 0.0).astype(F32)

    preact, hidden, encoded = preact_in[...], hidden_in[...], encoded_in[...]
    code = code_col[...]
    stone = embed[...].astype(F32)
    stones = jnp.where(code == 0, stone[0:1], jnp.where(code == 1, stone[1:2], stone[2:3]))
    start = (stones + encoded[0:1]).astype(BF16).astype(F32) * mask

    buf[0:FRONT, :] = jnp.zeros((FRONT, buf.shape[1]), F32)
    buf[FRONT + ROWS :, :] = jnp.zeros((FRONT, buf.shape[1]), F32)
    buf[FRONT : FRONT + ROWS, :] = start
    channels = start.shape[1]
    taps = wt.shape[2]

    def forward(block, carry):
        for tap, shift in enumerate(TAP_SHIFTS):
            patches[block, :, tap * channels : (tap + 1) * channels] = buf[
                FRONT + shift : FRONT + shift + ROWS, :
            ].astype(BF16)
        zconv = nt(patches[block], wt[block])
        rscale = lax.rsqrt(jnp.mean(zconv * zconv, axis=-1, keepdims=True) + NORM_EPS)
        value = zconv * rscale
        normed[block] = value
        rscales[block] = rscale
        stream = buf[FRONT : FRONT + ROWS, :] + value * jax.nn.sigmoid(value)
        buf[FRONT : FRONT + ROWS, :] = stream.astype(BF16).astype(F32) * mask
        return carry

    for copy in copies:
        copy.wait()
    lax.fori_loop(0, 4, forward, 0)
    grad[...] = cotangent[...].astype(F32)

    def backward(step, carry):
        block = 3 - step
        value = normed[block]
        upper = grad[...]
        sigma = jax.nn.sigmoid(value)
        dnorm = upper * (sigma * (1.0 + value * (1.0 - sigma)))
        inner = jnp.mean(dnorm * value, axis=-1, keepdims=True)
        dconv = rscales[block] * (dnorm - value * inner)
        gt[block] = nn(dconv.T.astype(BF16), patches[block]).astype(BF16)
        buf[FRONT : FRONT + ROWS, :] = dconv.astype(BF16).astype(F32)
        total = upper
        for tap, shift in enumerate(TAP_SHIFTS):
            total += nn(
                buf[FRONT - shift : FRONT - shift + ROWS, :].astype(BF16),
                wt[block, :, tap * channels : (tap + 1) * channels],
            )
        grad[...] = total.astype(BF16).astype(F32) * mask
        return carry

    lax.fori_loop(0, 4, backward, 0)

    kind = lax.broadcasted_iota(jnp.int32, (16, ROWS), 0)
    codes = code_row[...]
    picked = ((kind < 3) & (codes == kind)) | ((kind == 3) & (codes < 3))
    sums = nn(jnp.where(picked, 1.0, 0.0).astype(BF16), grad[...].astype(BF16))
    rounded = sums.astype(BF16)
    cdf = 0.5 * (1.0 + lax.erf(preact * 0.7071067811865476))
    density = jnp.exp(-0.5 * preact * preact) * 0.3989422804014327
    pre_grad = (nt(rounded, w_second[...]) * (cdf + preact * density)).astype(BF16)
    parts = ((context[...], 0, 8), (hidden, 0, 8), (pre_grad, 3, 8))
    parts += tuple((rounded, row, 2) for row in (3, 0, 1, 2))
    place = 0
    for array, row, count in parts:
        for piece in range(count):
            vectors[place : place + 1, :] = array.astype(F32)[
                row : row + 1, piece * 128 : (piece + 1) * 128
            ]
            place += 1
    tail = vectors[...].astype(BF16)
    empty = jnp.zeros(tail.shape, BF16)
    for core, pieces, first, second in ((c, own, tail, empty), (1 - c, other, empty, tail)):
        for outer in range(4):
            for inner in range(4):
                block, rows = block_rows(outer, inner, core)
                pieces[outer, inner, :, 0:taps] = gt[block, rows, :]
                pieces[outer, inner, :, taps : taps + 128] = first
                pieces[outer, inner, :, taps + 128 :] = second


def fold_kernel(where, pieces, out):
    taps = pieces.shape[3] - 256
    for inner in range(4):
        total = pieces[0, inner, :, 0:taps].astype(F32)
        for source in range(1, 4):
            total += pieces[source, inner, :, 0:taps].astype(F32)
        out[inner, :, 0:taps] = total.astype(BF16)
        for source in range(4):
            lane = taps + source * 256
            out[inner, :, lane : lane + 256] = pieces[source, inner, :, taps:]


def pack_kernel(where, pieces, out, vectors, product, stones):
    first = where[0] * 256 + where[1] * 64 + where[2] * 32
    row = first // 128
    rows = pl.ds(pl.multiple_of(first - row * 128, 32), 32)
    taps = pieces.shape[2] - 1024
    for state in range(32):
        lane = taps + state % 8 * 128
        vectors[state * 32 : (state + 1) * 32, :] = pieces[state // 8, :, lane : lane + 128].astype(F32)

    def of_states(place):
        return vectors[pl.ds(place, 32, stride=32), :]

    context = of_states(row).astype(BF16)
    hidden = of_states(row + 8).astype(BF16)
    for piece in range(8):
        lanes = slice(piece * 128, (piece + 1) * 128)
        product[:, lanes] = tn(context, of_states(16 + piece).astype(BF16))
    for piece in range(2):
        lanes = slice(1024 + piece * 128, 1024 + (piece + 1) * 128)
        product[:, lanes] = tn(hidden, of_states(24 + piece).astype(BF16))
    stones[...] = jnp.zeros(stones.shape, F32)
    for piece in range(6):
        v, half = divmod(piece, 2)
        stones[v : v + 1, half * 128 : (half + 1) * 128] = jnp.sum(
            of_states(26 + piece), axis=0, keepdims=True
        )
    for column in range(taps // 256):
        lanes = slice(column * 256, (column + 1) * 256)
        block = pieces[0, :, lanes].astype(F32)
        for piece in range(1, 4):
            block += pieces[piece, :, lanes].astype(F32)
        out[2 * column] = block[0:16].astype(BF16)
        out[2 * column + 1] = block[16:32].astype(BF16)
    for column in range(5):
        block = product[rows, column * 256 : (column + 1) * 256]
        place = 2 * (taps // 256 + column)
        out[place] = block[0:16].astype(BF16)
        out[place + 1] = block[16:32].astype(BF16)
    out[28] = stones[...].astype(BF16)
    for place in (29, 30, 31):
        out[place] = jnp.zeros(out.shape[1:], BF16)


def finish_kernel(where, mine, theirs, conv, first, second, stones):
    c = where[2]
    for out, start in ((conv, 0), (first, conv.shape[1]), (second, conv.shape[1] + first.shape[1])):
        for column in range(out.shape[1] // 256):
            for half in range(2):
                for core, pieces in ((c, mine), (1 - c, theirs)):
                    rows = pl.ds(pl.multiple_of(core * 32 + half * 16, 16), 16)
                    out[rows, column * 256 : (column + 1) * 256] = (
                        pieces[2 * (start // 256 + column) + half].astype(F32) * (1.0 / 512.0)
                    ).astype(BF16)
    stones[...] = (mine[28].astype(F32) * (1.0 / 512.0))[0:3].astype(BF16)


def body(boards, neighbours, counts, database, w_first, w_second, embed, conv_weight, cotangent):
    h = lax.axis_index("shard")
    s = lax.axis_index("section")
    dp = lax.axis_index("dp")
    c = dp % 2
    where = jnp.stack([s, h, c]).astype(jnp.int32)
    channels = embed.shape[1]
    taps = conv_weight.shape[1]

    along_x, along_y = [], []
    for place in range(lax.axis_size("dp")):
        lines = ([[place * 16 + i * 4 + j for j in range(4)] for i in range(4)],
                 [[place * 16 + i * 4 + j for i in range(4)] for j in range(4)])
        along_x += lines[place % 2]
        along_y += lines[1 - place % 2]

    def ring(blocks, groups):
        return lax.all_to_all(
            blocks, ("dp", "section", "shard"), 0, 0, axis_index_groups=groups, tiled=True
        )

    slots = neighbours.shape[1]
    asked = jnp.concatenate([neighbours, counts[:, None]], axis=1)
    state = lax.broadcasted_iota(jnp.int32, asked.shape, 0)
    asked = jnp.sum(jnp.where(state == s, asked, 0), axis=0, keepdims=True)
    count = asked[:, slots]
    asked = jnp.broadcast_to(jnp.pad(asked, ((0, 0), (0, 127 - slots))), (8, 128))
    asked = lax.all_gather(asked[None], "shard", axis=0, tiled=True)[:, 0, : slots + 1]

    unit = lax.dynamic_slice_in_dim(conv_weight[0].T, c * 32, 32, 0)
    unit = jnp.broadcast_to(unit[None], (4,) + unit.shape)
    mine = ring(unit, along_x)
    asked, mine = lax.optimization_barrier((asked, mine))
    mine = ring(jnp.broadcast_to(mine[None], (4,) + mine.shape), along_y)

    live = lax.broadcasted_iota(jnp.int32, (4, slots), 1) < asked[:, slots:]
    stored = database.shape[0]
    positions = lax.broadcasted_iota(jnp.int32, (1, 1, stored), 2) + h * stored
    hits = (asked[:, :slots, None] == positions) & live[:, :, None]
    picks = jnp.sum(hits.astype(F32), axis=1).astype(BF16)
    partial = jnp.dot(picks, database, preferred_element_type=F32)
    summed = lax.dynamic_slice_in_dim(partial, h, 1, 0)
    for d in (1, 2, 3):
        piece = lax.dynamic_slice_in_dim(partial, (h + 4 - d) % 4, 1, 0)
        summed = summed + turned(piece, "shard", -d)
    context = (summed / jnp.maximum(count, 1).astype(F32)[:, None]).astype(BF16)
    context = jnp.broadcast_to(context, (16, context.shape[1]))

    board = lax.dynamic_index_in_dim(boards, s, 0, keepdims=False).reshape(BOARD, BOARD)
    code = jnp.pad(board, ((0, 0), (0, 1)), constant_values=3).reshape(-1)
    code = jnp.pad(code, (0, ROWS - BOARD * PITCH), constant_values=3)
    upper = lax.dynamic_index_in_dim(cotangent, s, 0, keepdims=False)
    upper = jnp.pad(upper.reshape(BOARD, BOARD, channels), ((0, 0), (0, 1), (0, 0)))
    upper = jnp.pad(upper.reshape(-1, channels), ((0, ROWS - BOARD * PITCH), (0, 0)))

    mine, context, upper = lax.optimization_barrier((mine, context, upper))
    theirs = swap(mine, "dp", 1)
    width = context.shape[1]
    preact, hidden, encoded = vmem_call(
        encoder_kernel,
        (
            jax.ShapeDtypeStruct((16, width), F32),
            jax.ShapeDtypeStruct((16, width), BF16),
            jax.ShapeDtypeStruct((16, channels), F32),
        ),
        [],
        "encoder",
        2 * 16 * width * (width + channels),
        3 << 20,
    )(where, context, w_first, w_second)
    part = jax.ShapeDtypeStruct((4, 4, 32, taps + 256), BF16)
    own, other = vmem_call(
        trunk_kernel,
        (part, part),
        [
            pltpu.VMEM((4, channels, taps), BF16),
            pltpu.VMEM((4, ROWS, taps), BF16),
            pltpu.VMEM((4, channels, taps), BF16),
            pltpu.VMEM((4, ROWS, channels), F32),
            pltpu.VMEM((4, ROWS, 1), F32),
            pltpu.VMEM((2 * FRONT + ROWS, channels), F32),
            pltpu.VMEM((ROWS, channels), F32),
            pltpu.VMEM((32, 128), F32),
            pltpu.SemaphoreType.DMA((16,)),
        ],
        "trunk",
        12 * 2 * ROWS * taps * channels,
        16 << 20,
        far=1,
    )(
        where, context, preact, hidden, encoded, w_second, embed,
        code[:, None], code[None, :], upper, mine, theirs,
    )

    pieces = ring((own.astype(F32) + swap(other, "dp", 1).astype(F32)).astype(BF16), along_x)
    (pieces,) = vmem_call(
        fold_kernel,
        (jax.ShapeDtypeStruct((4, 32, taps + 1024), BF16),),
        [],
        "fold",
        pieces.size,
        3 << 20,
    )(where, pieces)
    pieces = ring(pieces, along_y)
    (chunks,) = vmem_call(
        pack_kernel,
        (jax.ShapeDtypeStruct((32, 16, 256), BF16),),
        [
            pltpu.VMEM((1024, 128), F32),
            pltpu.VMEM((128, 1280), F32),
            pltpu.VMEM((16, 256), F32),
        ],
        "pack",
        4 * 32 * 128 * 1280,
        3 << 20,
    )(where, pieces)

    line = [[2 * i + core for i in range(lax.axis_size("dp") // 2)] for core in (0, 1)]

    def along_z(blocks):
        return lax.all_to_all(blocks, "dp", 0, 0, axis_index_groups=line, tiled=True)

    total = along_z(chunks.reshape(16, 2, 16, 256))
    total = jnp.sum(total.astype(F32), axis=0, keepdims=True).astype(BF16)
    chunks = along_z(jnp.broadcast_to(total, (16,) + total.shape[1:])).reshape(32, 16, 256)
    conv, w1_grad, w2_grad, embed_grad = vmem_call(
        finish_kernel,
        (
            jax.ShapeDtypeStruct((64, taps), BF16),
            jax.ShapeDtypeStruct((64, 1024), BF16),
            jax.ShapeDtypeStruct((64, channels), BF16),
            jax.ShapeDtypeStruct((3, channels), BF16),
        ),
        [],
        "finish",
        1 << 18,
        1 << 20,
    )(where, chunks, swap(chunks, "dp", 1))
    return (w1_grad, w2_grad, embed_grad, conv.T[None])


def solution(mesh):
    placed = (
        P(("dp", "shard"), None),
        P(("dp", "shard"), None),
        P(("dp", "shard")),
        P("shard", None),
        P(),
        P(),
        P(),
        P("section", None, "shard"),
        P(("dp", "shard"), None, None),
    )
    return jax.shard_map(
        body,
        mesh=mesh,
        in_specs=placed,
        out_specs=(
            P(("section", "shard"), None),
            P(("section", "shard"), None),
            P(),
            P("section", None, "shard"),
        ),
        check_vma=False,
    )
```

```python
import jax
import jax.numpy as jnp
from jax import lax
from jax.experimental import pallas as pl
from jax.experimental.pallas import tpu as pltpu
from jax.sharding import PartitionSpec as P

BOARD = 19
PITCH = 20
ROWS = 384
FRONT = 24
NORM_EPS = 1e-05
TAP_SHIFTS = [(a - 1) * PITCH + (b - 1) for a in range(3) for b in range(3)]
VMEM_BYTES = 34 * 1024 * 1024
F32 = jnp.float32
BF16 = jnp.bfloat16


def swap(block, axis, bits):
    return lax.ppermute(block, axis, [(i, i ^ bits) for i in range(lax.axis_size(axis))])


def turned(block, axis, distance):
    size = lax.axis_size(axis)
    return lax.ppermute(block, axis, [(i, (i + distance) % size) for i in range(size)])


def turned(block, axis, distance):
    size = lax.axis_size(axis)
    return lax.ppermute(block, axis, [(i, (i + distance) % size) for i in range(size)])


def exchange(blocks, axis):
    return lax.all_to_all(blocks, axis, 0, 0, tiled=True)


def nn(left, right):
    return lax.dot_general(left, right, (((1,), (0,)), ((), ())), preferred_element_type=F32)


def nt(left, right):
    return lax.dot_general(left, right, (((1,), (1,)), ((), ())), preferred_element_type=F32)


def tn(left, right):
    return lax.dot_general(left, right, (((0,), (0,)), ((), ())), preferred_element_type=F32)


def vmem_call(kernel, outs, scratch, name, flops, moved):
    spec = pl.BlockSpec(memory_space=pltpu.VMEM)

    def call(scalars, *arrays):
        return pl.pallas_call(
            kernel,
            out_shape=outs,
            in_specs=[pl.BlockSpec(memory_space=pltpu.SMEM)]
            + [spec] * len(arrays),
            out_specs=tuple(spec for _ in outs),
            scratch_shapes=scratch,
            compiler_params=pltpu.CompilerParams(vmem_limit_bytes=VMEM_BYTES),
            cost_estimate=pl.CostEstimate(flops=flops, bytes_accessed=moved, transcendentals=0),
            name=name,
        )(scalars, *arrays)

    return call


def encoder_kernel(where, context, w_first, w_second, preact, hidden, encoded):
    value = nn(context[...], w_first[...])
    preact[...] = value
    rounded = (value * (0.5 * (1.0 + lax.erf(value * 0.7071067811865476)))).astype(BF16)
    hidden[...] = rounded
    encoded[...] = nn(rounded, w_second[...])


def trunk_kernel(
    where, context, preact_in, hidden_in, encoded_in, w_second, embed, code_col, code_row, cotangent,
    mine, theirs,
    own, other,
    wt, patches, gt, normed, rscales, buf, grad, vectors,
):
    c = where[2]

    def block_rows(outer, inner, core):
        block = jnp.where(core == 0, inner, outer)
        shard = jnp.where(core == 0, outer, inner)
        return block, pl.ds(pl.multiple_of(shard * 64 + core * 32, 32), 32)

    for core, pieces in ((c, mine), (1 - c, theirs)):
        for outer in range(4):
            for inner in range(4):
                block, rows = block_rows(inner, outer, core)
                wt[block, rows, :] = pieces[outer, inner]

    point = lax.broadcasted_iota(jnp.int32, (ROWS, 1), 0)
    column = point - ((point * 3277) >> 16) * PITCH
    mask = jnp.where((column < BOARD) & (point < BOARD * PITCH), 1.0, 0.0).astype(F32)

    preact, hidden, encoded = preact_in[...], hidden_in[...], encoded_in[...]
    code = code_col[...]
    stone = embed[...].astype(F32)
    stones = jnp.where(code == 0, stone[0:1], jnp.where(code == 1, stone[1:2], stone[2:3]))
    start = (stones + encoded[0:1]).astype(BF16).astype(F32) * mask

    buf[0:FRONT, :] = jnp.zeros((FRONT, buf.shape[1]), F32)
    buf[FRONT + ROWS :, :] = jnp.zeros((FRONT, buf.shape[1]), F32)
    buf[FRONT : FRONT + ROWS, :] = start
    channels = start.shape[1]
    taps = wt.shape[2]

    def forward(block, carry):
        for tap, shift in enumerate(TAP_SHIFTS):
            patches[block, :, tap * channels : (tap + 1) * channels] = buf[
                FRONT + shift : FRONT + shift + ROWS, :
            ].astype(BF16)
        zconv = nt(patches[block], wt[block])
        rscale = lax.rsqrt(jnp.mean(zconv * zconv, axis=-1, keepdims=True) + NORM_EPS)
        value = zconv * rscale
        normed[block] = value
        rscales[block] = rscale
        stream = buf[FRONT : FRONT + ROWS, :] + value * jax.nn.sigmoid(value)
        buf[FRONT : FRONT + ROWS, :] = stream.astype(BF16).astype(F32) * mask
        return carry

    lax.fori_loop(0, 4, forward, 0, unroll=True)
    grad[...] = cotangent[...].astype(F32)

    def backward(step, carry):
        block = 3 - step
        value = normed[block]
        upper = grad[...]
        sigma = jax.nn.sigmoid(value)
        dnorm = upper * (sigma * (1.0 + value * (1.0 - sigma)))
        inner = jnp.mean(dnorm * value, axis=-1, keepdims=True)
        dconv = rscales[block] * (dnorm - value * inner)
        gt[block] = nn(dconv.T.astype(BF16), patches[block]).astype(BF16)
        buf[FRONT : FRONT + ROWS, :] = dconv.astype(BF16).astype(F32)
        total = upper
        for tap, shift in enumerate(TAP_SHIFTS):
            total += nn(
                buf[FRONT - shift : FRONT - shift + ROWS, :].astype(BF16),
                wt[block, :, tap * channels : (tap + 1) * channels],
            )
        grad[...] = total.astype(BF16).astype(F32) * mask
        return carry

    lax.fori_loop(0, 4, backward, 0, unroll=True)

    kind = lax.broadcasted_iota(jnp.int32, (16, ROWS), 0)
    codes = code_row[...]
    picked = ((kind < 3) & (codes == kind)) | ((kind == 3) & (codes < 3))
    sums = nn(jnp.where(picked, 1.0, 0.0).astype(BF16), grad[...].astype(BF16))
    rounded = sums.astype(BF16)
    cdf = 0.5 * (1.0 + lax.erf(preact * 0.7071067811865476))
    density = jnp.exp(-0.5 * preact * preact) * 0.3989422804014327
    pre_grad = (nt(rounded, w_second[...]) * (cdf + preact * density)).astype(BF16)
    parts = ((context[...], 0, 8), (hidden, 0, 8), (pre_grad, 3, 8))
    parts += tuple((rounded, row, 2) for row in (3, 0, 1, 2))
    place = 0
    for array, row, count in parts:
        for piece in range(count):
            vectors[place : place + 1, :] = array.astype(F32)[
                row : row + 1, piece * 128 : (piece + 1) * 128
            ]
            place += 1
    tail = vectors[...].astype(BF16)
    empty = jnp.zeros(tail.shape, BF16)
    for core, pieces, first, second in ((c, own, tail, empty), (1 - c, other, empty, tail)):
        for outer in range(4):
            for inner in range(4):
                block, rows = block_rows(outer, inner, core)
                pieces[outer, inner, :, 0:taps] = gt[block, rows, :]
                pieces[outer, inner, :, taps : taps + 128] = first
                pieces[outer, inner, :, taps + 128 :] = second


def fold_kernel(where, pieces, out):
    taps = pieces.shape[3] - 256
    for inner in range(4):
        total = pieces[0, inner, :, 0:taps].astype(F32)
        for source in range(1, 4):
            total += pieces[source, inner, :, 0:taps].astype(F32)
        out[inner, :, 0:taps] = total.astype(BF16)
        for source in range(4):
            lane = taps + source * 256
            out[inner, :, lane : lane + 256] = pieces[source, inner, :, taps:]


def pack_kernel(where, pieces, out, vectors, product, stones):
    first = where[0] * 256 + where[1] * 64 + where[2] * 32
    row = first // 128
    rows = pl.ds(pl.multiple_of(first - row * 128, 32), 32)
    taps = pieces.shape[2] - 1024
    for state in range(32):
        lane = taps + state % 8 * 128
        vectors[state * 32 : (state + 1) * 32, :] = pieces[state // 8, :, lane : lane + 128].astype(F32)

    def of_states(place):
        return vectors[pl.ds(place, 32, stride=32), :]

    context = of_states(row).astype(BF16)
    hidden = of_states(row + 8).astype(BF16)
    for piece in range(8):
        lanes = slice(piece * 128, (piece + 1) * 128)
        product[:, lanes] = tn(context, of_states(16 + piece).astype(BF16))
    for piece in range(2):
        lanes = slice(1024 + piece * 128, 1024 + (piece + 1) * 128)
        product[:, lanes] = tn(hidden, of_states(24 + piece).astype(BF16))
    stones[...] = jnp.zeros(stones.shape, F32)
    for piece in range(6):
        v, half = divmod(piece, 2)
        stones[v : v + 1, half * 128 : (half + 1) * 128] = jnp.sum(
            of_states(26 + piece), axis=0, keepdims=True
        )
    for column in range(taps // 256):
        lanes = slice(column * 256, (column + 1) * 256)
        block = pieces[0, :, lanes].astype(F32)
        for piece in range(1, 4):
            block += pieces[piece, :, lanes].astype(F32)
        out[2 * column] = block[0:16].astype(BF16)
        out[2 * column + 1] = block[16:32].astype(BF16)
    for column in range(5):
        block = product[rows, column * 256 : (column + 1) * 256]
        place = 2 * (taps // 256 + column)
        out[place] = block[0:16].astype(BF16)
        out[place + 1] = block[16:32].astype(BF16)
    out[28] = stones[...].astype(BF16)
    for place in (29, 30, 31):
        out[place] = jnp.zeros(out.shape[1:], BF16)


def finish_kernel(where, mine, theirs, conv, first, second, stones):
    c = where[2]
    for out, start in ((conv, 0), (first, conv.shape[1]), (second, conv.shape[1] + first.shape[1])):
        for column in range(out.shape[1] // 256):
            for half in range(2):
                for core, pieces in ((c, mine), (1 - c, theirs)):
                    rows = pl.ds(pl.multiple_of(core * 32 + half * 16, 16), 16)
                    out[rows, column * 256 : (column + 1) * 256] = (
                        pieces[2 * (start // 256 + column) + half].astype(F32) * (1.0 / 512.0)
                    ).astype(BF16)
    stones[...] = (mine[28].astype(F32) * (1.0 / 512.0))[0:3].astype(BF16)


def body(boards, neighbours, counts, database, w_first, w_second, embed, conv_weight, cotangent):
    h = lax.axis_index("shard")
    s = lax.axis_index("section")
    dp = lax.axis_index("dp")
    c = dp % 2
    where = jnp.stack([s, h, c]).astype(jnp.int32)
    channels = embed.shape[1]
    taps = conv_weight.shape[1]

    along_x, along_y = [], []
    for place in range(lax.axis_size("dp")):
        lines = ([[place * 16 + i * 4 + j for j in range(4)] for i in range(4)],
                 [[place * 16 + i * 4 + j for i in range(4)] for j in range(4)])
        along_x += lines[place % 2]
        along_y += lines[1 - place % 2]

    def ring(blocks, groups):
        return lax.all_to_all(
            blocks, ("dp", "section", "shard"), 0, 0, axis_index_groups=groups, tiled=True
        )

    slots = neighbours.shape[1]
    asked = jnp.concatenate([neighbours, counts[:, None]], axis=1)
    state = lax.broadcasted_iota(jnp.int32, asked.shape, 0)
    asked = jnp.sum(jnp.where(state == s, asked, 0), axis=0, keepdims=True)
    count = asked[:, slots]
    asked = jnp.broadcast_to(jnp.pad(asked, ((0, 0), (0, 127 - slots))), (8, 128))
    asked = lax.all_gather(asked[None], "shard", axis=0, tiled=True)[:, 0, : slots + 1]

    unit = lax.dynamic_slice_in_dim(conv_weight[0].T, c * 32, 32, 0)
    unit = jnp.broadcast_to(unit[None], (4,) + unit.shape)
    mine = ring(unit, along_x)
    asked, mine = lax.optimization_barrier((asked, mine))
    mine = ring(jnp.broadcast_to(mine[None], (4,) + mine.shape), along_y)

    live = lax.broadcasted_iota(jnp.int32, (4, slots), 1) < asked[:, slots:]
    stored = database.shape[0]
    positions = lax.broadcasted_iota(jnp.int32, (1, 1, stored), 2) + h * stored
    hits = (asked[:, :slots, None] == positions) & live[:, :, None]
    picks = jnp.sum(hits.astype(F32), axis=1).astype(BF16)
    partial = jnp.dot(picks, database, preferred_element_type=F32)
    summed = lax.dynamic_slice_in_dim(partial, h, 1, 0)
    for d in (1, 2, 3):
        piece = lax.dynamic_slice_in_dim(partial, (h + 4 - d) % 4, 1, 0)
        summed = summed + turned(piece, "shard", -d)
    context = (summed / jnp.maximum(count, 1).astype(F32)[:, None]).astype(BF16)
    context = jnp.broadcast_to(context, (16, context.shape[1]))

    board = lax.dynamic_index_in_dim(boards, s, 0, keepdims=False).reshape(BOARD, BOARD)
    code = jnp.pad(board, ((0, 0), (0, 1)), constant_values=3).reshape(-1)
    code = jnp.pad(code, (0, ROWS - BOARD * PITCH), constant_values=3)
    upper = lax.dynamic_index_in_dim(cotangent, s, 0, keepdims=False)
    upper = jnp.pad(upper.reshape(BOARD, BOARD, channels), ((0, 0), (0, 1), (0, 0)))
    upper = jnp.pad(upper.reshape(-1, channels), ((0, ROWS - BOARD * PITCH), (0, 0)))

    mine, context, upper = lax.optimization_barrier((mine, context, upper))
    theirs = swap(mine, "dp", 1)
    width = context.shape[1]
    preact, hidden, encoded = vmem_call(
        encoder_kernel,
        (
            jax.ShapeDtypeStruct((16, width), F32),
            jax.ShapeDtypeStruct((16, width), BF16),
            jax.ShapeDtypeStruct((16, channels), F32),
        ),
        [],
        "encoder",
        2 * 16 * width * (width + channels),
        3 << 20,
    )(where, context, w_first, w_second)
    part = jax.ShapeDtypeStruct((4, 4, 32, taps + 256), BF16)
    own, other = vmem_call(
        trunk_kernel,
        (part, part),
        [
            pltpu.VMEM((4, channels, taps), BF16),
            pltpu.VMEM((4, ROWS, taps), BF16),
            pltpu.VMEM((4, channels, taps), BF16),
            pltpu.VMEM((4, ROWS, channels), F32),
            pltpu.VMEM((4, ROWS, 1), F32),
            pltpu.VMEM((2 * FRONT + ROWS, channels), F32),
            pltpu.VMEM((ROWS, channels), F32),
            pltpu.VMEM((32, 128), F32),
        ],
        "trunk",
        12 * 2 * ROWS * taps * channels,
        16 << 20,
    )(
        where, context, preact, hidden, encoded, w_second, embed,
        code[:, None], code[None, :], upper, mine, theirs,
    )

    pieces = ring((own.astype(F32) + swap(other, "dp", 1).astype(F32)).astype(BF16), along_x)
    (pieces,) = vmem_call(
        fold_kernel,
        (jax.ShapeDtypeStruct((4, 32, taps + 1024), BF16),),
        [],
        "fold",
        pieces.size,
        3 << 20,
    )(where, pieces)
    pieces = ring(pieces, along_y)
    (chunks,) = vmem_call(
        pack_kernel,
        (jax.ShapeDtypeStruct((32, 16, 256), BF16),),
        [
            pltpu.VMEM((1024, 128), F32),
            pltpu.VMEM((128, 1280), F32),
            pltpu.VMEM((16, 256), F32),
        ],
        "pack",
        4 * 32 * 128 * 1280,
        3 << 20,
    )(where, pieces)

    line = [[2 * i + core for i in range(lax.axis_size("dp") // 2)] for core in (0, 1)]

    def along_z(blocks):
        return lax.all_to_all(blocks, "dp", 0, 0, axis_index_groups=line, tiled=True)

    total = along_z(chunks.reshape(16, 2, 16, 256))
    total = jnp.sum(total.astype(F32), axis=0, keepdims=True).astype(BF16)
    chunks = along_z(jnp.broadcast_to(total, (16,) + total.shape[1:])).reshape(32, 16, 256)
    conv, w1_grad, w2_grad, embed_grad = vmem_call(
        finish_kernel,
        (
            jax.ShapeDtypeStruct((64, taps), BF16),
            jax.ShapeDtypeStruct((64, 1024), BF16),
            jax.ShapeDtypeStruct((64, channels), BF16),
            jax.ShapeDtypeStruct((3, channels), BF16),
        ),
        [],
        "finish",
        1 << 18,
        1 << 20,
    )(where, chunks, swap(chunks, "dp", 1))
    return (w1_grad, w2_grad, embed_grad, conv.T[None])


def solution(mesh):
    placed = (
        P(("dp", "shard"), None),
        P(("dp", "shard"), None),
        P(("dp", "shard")),
        P("shard", None),
        P(),
        P(),
        P(),
        P("section", None, "shard"),
        P(("dp", "shard"), None, None),
    )
    return jax.shard_map(
        body,
        mesh=mesh,
        in_specs=placed,
        out_specs=(
            P(("section", "shard"), None),
            P(("section", "shard"), None),
            P(),
            P("section", None, "shard"),
        ),
        check_vma=False,
    )
```

```python
import jax
import jax.numpy as jnp
from jax import lax
from jax.experimental import pallas as pl
from jax.experimental.pallas import tpu as pltpu
from jax.sharding import PartitionSpec as P

BOARD = 19
PITCH = 20
ROWS = 384
FRONT = 24
NORM_EPS = 1e-05
TAP_SHIFTS = [(a - 1) * PITCH + (b - 1) for a in range(3) for b in range(3)]
VMEM_BYTES = 34 * 1024 * 1024
F32 = jnp.float32
BF16 = jnp.bfloat16


def swap(block, axis, bits):
    return lax.ppermute(block, axis, [(i, i ^ bits) for i in range(lax.axis_size(axis))])


def turned(block, axis, distance):
    size = lax.axis_size(axis)
    return lax.ppermute(block, axis, [(i, (i + distance) % size) for i in range(size)])


def turned(block, axis, distance):
    size = lax.axis_size(axis)
    return lax.ppermute(block, axis, [(i, (i + distance) % size) for i in range(size)])


def exchange(blocks, axis):
    return lax.all_to_all(blocks, axis, 0, 0, tiled=True)


def nn(left, right):
    return lax.dot_general(left, right, (((1,), (0,)), ((), ())), preferred_element_type=F32)


def nt(left, right):
    return lax.dot_general(left, right, (((1,), (1,)), ((), ())), preferred_element_type=F32)


def tn(left, right):
    return lax.dot_general(left, right, (((0,), (0,)), ((), ())), preferred_element_type=F32)


def vmem_call(kernel, outs, scratch, name, flops, moved):
    spec = pl.BlockSpec(memory_space=pltpu.VMEM)

    def call(scalars, *arrays):
        return pl.pallas_call(
            kernel,
            out_shape=outs,
            in_specs=[pl.BlockSpec(memory_space=pltpu.SMEM)]
            + [spec] * len(arrays),
            out_specs=tuple(spec for _ in outs),
            scratch_shapes=scratch,
            compiler_params=pltpu.CompilerParams(vmem_limit_bytes=VMEM_BYTES),
            cost_estimate=pl.CostEstimate(flops=flops, bytes_accessed=moved, transcendentals=0),
            name=name,
        )(scalars, *arrays)

    return call


def encoder_kernel(where, context, w_first, w_second, preact, hidden, encoded):
    value = nn(context[...], w_first[...])
    preact[...] = value
    rounded = (value * (0.5 * (1.0 + lax.erf(value * 0.7071067811865476)))).astype(BF16)
    hidden[...] = rounded
    encoded[...] = nn(rounded, w_second[...])


def trunk_kernel(
    where, context, preact_in, hidden_in, encoded_in, w_second, embed, code_col, code_row, cotangent,
    mine, theirs,
    own, other,
    wt, patches, gt, normed, rscales, buf, grad, vectors,
):
    c = where[2]

    def block_rows(outer, inner, core):
        block = jnp.where(core == 0, inner, outer)
        shard = jnp.where(core == 0, outer, inner)
        return block, pl.ds(pl.multiple_of(shard * 64 + core * 32, 32), 32)

    def assemble(place, carry):
        outer, inner = place >> 2, place & 3
        for core, pieces in ((c, mine), (1 - c, theirs)):
            block, rows = block_rows(inner, outer, core)
            wt[block, rows, :] = pieces[outer, inner]
        return carry

    lax.fori_loop(0, 16, assemble, 0)

    point = lax.broadcasted_iota(jnp.int32, (ROWS, 1), 0)
    column = point - ((point * 3277) >> 16) * PITCH
    mask = jnp.where((column < BOARD) & (point < BOARD * PITCH), 1.0, 0.0).astype(F32)

    preact, hidden, encoded = preact_in[...], hidden_in[...], encoded_in[...]
    code = code_col[...]
    stone = embed[...].astype(F32)
    stones = jnp.where(code == 0, stone[0:1], jnp.where(code == 1, stone[1:2], stone[2:3]))
    start = (stones + encoded[0:1]).astype(BF16).astype(F32) * mask

    buf[0:FRONT, :] = jnp.zeros((FRONT, buf.shape[1]), F32)
    buf[FRONT + ROWS :, :] = jnp.zeros((FRONT, buf.shape[1]), F32)
    buf[FRONT : FRONT + ROWS, :] = start
    channels = start.shape[1]
    taps = wt.shape[2]

    def forward(block, carry):
        for tap, shift in enumerate(TAP_SHIFTS):
            patches[block, :, tap * channels : (tap + 1) * channels] = buf[
                FRONT + shift : FRONT + shift + ROWS, :
            ].astype(BF16)
        zconv = nt(patches[block], wt[block])
        rscale = lax.rsqrt(jnp.mean(zconv * zconv, axis=-1, keepdims=True) + NORM_EPS)
        value = zconv * rscale
        normed[block] = value
        rscales[block] = rscale
        stream = buf[FRONT : FRONT + ROWS, :] + value * jax.nn.sigmoid(value)
        buf[FRONT : FRONT + ROWS, :] = stream.astype(BF16).astype(F32) * mask
        return carry

    lax.fori_loop(0, 4, forward, 0)
    grad[...] = cotangent[...].astype(F32)

    def backward(step, carry):
        block = 3 - step
        value = normed[block]
        upper = grad[...]
        sigma = jax.nn.sigmoid(value)
        dnorm = upper * (sigma * (1.0 + value * (1.0 - sigma)))
        inner = jnp.mean(dnorm * value, axis=-1, keepdims=True)
        dconv = rscales[block] * (dnorm - value * inner)
        gt[block] = nn(dconv.T.astype(BF16), patches[block]).astype(BF16)
        buf[FRONT : FRONT + ROWS, :] = dconv.astype(BF16).astype(F32)
        total = upper
        for tap, shift in enumerate(TAP_SHIFTS):
            total += nn(
                buf[FRONT - shift : FRONT - shift + ROWS, :].astype(BF16),
                wt[block, :, tap * channels : (tap + 1) * channels],
            )
        grad[...] = total.astype(BF16).astype(F32) * mask
        return carry

    lax.fori_loop(0, 4, backward, 0)

    kind = lax.broadcasted_iota(jnp.int32, (16, ROWS), 0)
    codes = code_row[...]
    picked = ((kind < 3) & (codes == kind)) | ((kind == 3) & (codes < 3))
    sums = nn(jnp.where(picked, 1.0, 0.0).astype(BF16), grad[...].astype(BF16))
    rounded = sums.astype(BF16)
    cdf = 0.5 * (1.0 + lax.erf(preact * 0.7071067811865476))
    density = jnp.exp(-0.5 * preact * preact) * 0.3989422804014327
    pre_grad = (nt(rounded, w_second[...]) * (cdf + preact * density)).astype(BF16)
    parts = ((context[...], 0, 8), (hidden, 0, 8), (pre_grad, 3, 8))
    parts += tuple((rounded, row, 2) for row in (3, 0, 1, 2))
    place = 0
    for array, row, count in parts:
        for piece in range(count):
            vectors[place : place + 1, :] = array.astype(F32)[
                row : row + 1, piece * 128 : (piece + 1) * 128
            ]
            place += 1
    tail = vectors[...].astype(BF16)
    empty = jnp.zeros(tail.shape, BF16)

    def hand_out(place, carry):
        outer, inner = place >> 2, place & 3
        for core, pieces, first, second in ((c, own, tail, empty), (1 - c, other, empty, tail)):
            block, rows = block_rows(outer, inner, core)
            pieces[outer, inner, :, 0:taps] = gt[block, rows, :]
            pieces[outer, inner, :, taps : taps + 128] = first
            pieces[outer, inner, :, taps + 128 :] = second
        return carry

    lax.fori_loop(0, 16, hand_out, 0)


def fold_kernel(where, pieces, out):
    taps = pieces.shape[3] - 256
    for inner in range(4):
        total = pieces[0, inner, :, 0:taps].astype(F32)
        for source in range(1, 4):
            total += pieces[source, inner, :, 0:taps].astype(F32)
        out[inner, :, 0:taps] = total.astype(BF16)
        for source in range(4):
            lane = taps + source * 256
            out[inner, :, lane : lane + 256] = pieces[source, inner, :, taps:]


def pack_kernel(where, pieces, out, vectors, product, stones):
    first = where[0] * 256 + where[1] * 64 + where[2] * 32
    row = first // 128
    rows = pl.ds(pl.multiple_of(first - row * 128, 32), 32)
    taps = pieces.shape[2] - 1024
    for state in range(32):
        lane = taps + state % 8 * 128
        vectors[state * 32 : (state + 1) * 32, :] = pieces[state // 8, :, lane : lane + 128].astype(F32)

    def of_states(place):
        return vectors[pl.ds(place, 32, stride=32), :]

    context = of_states(row).astype(BF16)
    hidden = of_states(row + 8).astype(BF16)
    for piece in range(8):
        lanes = slice(piece * 128, (piece + 1) * 128)
        product[:, lanes] = tn(context, of_states(16 + piece).astype(BF16))
    for piece in range(2):
        lanes = slice(1024 + piece * 128, 1024 + (piece + 1) * 128)
        product[:, lanes] = tn(hidden, of_states(24 + piece).astype(BF16))
    stones[...] = jnp.zeros(stones.shape, F32)
    for piece in range(6):
        v, half = divmod(piece, 2)
        stones[v : v + 1, half * 128 : (half + 1) * 128] = jnp.sum(
            of_states(26 + piece), axis=0, keepdims=True
        )
    for column in range(taps // 256):
        lanes = slice(column * 256, (column + 1) * 256)
        block = pieces[0, :, lanes].astype(F32)
        for piece in range(1, 4):
            block += pieces[piece, :, lanes].astype(F32)
        out[2 * column] = block[0:16].astype(BF16)
        out[2 * column + 1] = block[16:32].astype(BF16)
    for column in range(5):
        block = product[rows, column * 256 : (column + 1) * 256]
        place = 2 * (taps // 256 + column)
        out[place] = block[0:16].astype(BF16)
        out[place + 1] = block[16:32].astype(BF16)
    out[28] = stones[...].astype(BF16)
    for place in (29, 30, 31):
        out[place] = jnp.zeros(out.shape[1:], BF16)


def finish_kernel(where, mine, theirs, conv, first, second, stones):
    c = where[2]
    for out, start in ((conv, 0), (first, conv.shape[1]), (second, conv.shape[1] + first.shape[1])):
        for column in range(out.shape[1] // 256):
            for half in range(2):
                for core, pieces in ((c, mine), (1 - c, theirs)):
                    rows = pl.ds(pl.multiple_of(core * 32 + half * 16, 16), 16)
                    out[rows, column * 256 : (column + 1) * 256] = (
                        pieces[2 * (start // 256 + column) + half].astype(F32) * (1.0 / 512.0)
                    ).astype(BF16)
    stones[...] = (mine[28].astype(F32) * (1.0 / 512.0))[0:3].astype(BF16)


def body(boards, neighbours, counts, database, w_first, w_second, embed, conv_weight, cotangent):
    h = lax.axis_index("shard")
    s = lax.axis_index("section")
    dp = lax.axis_index("dp")
    c = dp % 2
    where = jnp.stack([s, h, c]).astype(jnp.int32)
    channels = embed.shape[1]
    taps = conv_weight.shape[1]

    along_x, along_y = [], []
    for place in range(lax.axis_size("dp")):
        lines = ([[place * 16 + i * 4 + j for j in range(4)] for i in range(4)],
                 [[place * 16 + i * 4 + j for i in range(4)] for j in range(4)])
        along_x += lines[place % 2]
        along_y += lines[1 - place % 2]

    def ring(blocks, groups):
        return lax.all_to_all(
            blocks, ("dp", "section", "shard"), 0, 0, axis_index_groups=groups, tiled=True
        )

    slots = neighbours.shape[1]
    asked = jnp.concatenate([neighbours, counts[:, None]], axis=1)
    state = lax.broadcasted_iota(jnp.int32, asked.shape, 0)
    asked = jnp.sum(jnp.where(state == s, asked, 0), axis=0, keepdims=True)
    count = asked[:, slots]
    asked = jnp.broadcast_to(jnp.pad(asked, ((0, 0), (0, 127 - slots))), (8, 128))
    asked = lax.all_gather(asked[None], "shard", axis=0, tiled=True)[:, 0, : slots + 1]

    unit = lax.dynamic_slice_in_dim(conv_weight[0].T, c * 32, 32, 0)
    unit = jnp.broadcast_to(unit[None], (4,) + unit.shape)
    mine = ring(unit, along_x)
    asked, mine = lax.optimization_barrier((asked, mine))
    mine = ring(jnp.broadcast_to(mine[None], (4,) + mine.shape), along_y)

    live = lax.broadcasted_iota(jnp.int32, (4, slots), 1) < asked[:, slots:]
    stored = database.shape[0]
    positions = lax.broadcasted_iota(jnp.int32, (1, 1, stored), 2) + h * stored
    hits = (asked[:, :slots, None] == positions) & live[:, :, None]
    picks = jnp.sum(hits.astype(F32), axis=1).astype(BF16)
    partial = jnp.dot(picks, database, preferred_element_type=F32)
    summed = lax.dynamic_slice_in_dim(partial, h, 1, 0)
    for d in (1, 2, 3):
        piece = lax.dynamic_slice_in_dim(partial, (h + 4 - d) % 4, 1, 0)
        summed = summed + turned(piece, "shard", -d)
    context = (summed / jnp.maximum(count, 1).astype(F32)[:, None]).astype(BF16)
    context = jnp.broadcast_to(context, (16, context.shape[1]))

    board = lax.dynamic_index_in_dim(boards, s, 0, keepdims=False).reshape(BOARD, BOARD)
    code = jnp.pad(board, ((0, 0), (0, 1)), constant_values=3).reshape(-1)
    code = jnp.pad(code, (0, ROWS - BOARD * PITCH), constant_values=3)
    upper = lax.dynamic_index_in_dim(cotangent, s, 0, keepdims=False)
    upper = jnp.pad(upper.reshape(BOARD, BOARD, channels), ((0, 0), (0, 1), (0, 0)))
    upper = jnp.pad(upper.reshape(-1, channels), ((0, ROWS - BOARD * PITCH), (0, 0)))

    mine, context, upper = lax.optimization_barrier((mine, context, upper))
    theirs = swap(mine, "dp", 1)
    width = context.shape[1]
    preact, hidden, encoded = vmem_call(
        encoder_kernel,
        (
            jax.ShapeDtypeStruct((16, width), F32),
            jax.ShapeDtypeStruct((16, width), BF16),
            jax.ShapeDtypeStruct((16, channels), F32),
        ),
        [],
        "encoder",
        2 * 16 * width * (width + channels),
        3 << 20,
    )(where, context, w_first, w_second)
    part = jax.ShapeDtypeStruct((4, 4, 32, taps + 256), BF16)
    own, other = vmem_call(
        trunk_kernel,
        (part, part),
        [
            pltpu.VMEM((4, channels, taps), BF16),
            pltpu.VMEM((4, ROWS, taps), BF16),
            pltpu.VMEM((4, channels, taps), BF16),
            pltpu.VMEM((4, ROWS, channels), F32),
            pltpu.VMEM((4, ROWS, 1), F32),
            pltpu.VMEM((2 * FRONT + ROWS, channels), F32),
            pltpu.VMEM((ROWS, channels), F32),
            pltpu.VMEM((32, 128), F32),
        ],
        "trunk",
        12 * 2 * ROWS * taps * channels,
        16 << 20,
    )(
        where, context, preact, hidden, encoded, w_second, embed,
        code[:, None], code[None, :], upper, mine, theirs,
    )

    pieces = ring((own.astype(F32) + swap(other, "dp", 1).astype(F32)).astype(BF16), along_x)
    (pieces,) = vmem_call(
        fold_kernel,
        (jax.ShapeDtypeStruct((4, 32, taps + 1024), BF16),),
        [],
        "fold",
        pieces.size,
        3 << 20,
    )(where, pieces)
    pieces = ring(pieces, along_y)
    (chunks,) = vmem_call(
        pack_kernel,
        (jax.ShapeDtypeStruct((32, 16, 256), BF16),),
        [
            pltpu.VMEM((1024, 128), F32),
            pltpu.VMEM((128, 1280), F32),
            pltpu.VMEM((16, 256), F32),
        ],
        "pack",
        4 * 32 * 128 * 1280,
        3 << 20,
    )(where, pieces)

    line = [[2 * i + core for i in range(lax.axis_size("dp") // 2)] for core in (0, 1)]

    def along_z(blocks):
        return lax.all_to_all(blocks, "dp", 0, 0, axis_index_groups=line, tiled=True)

    total = along_z(chunks.reshape(16, 2, 16, 256))
    total = jnp.sum(total.astype(F32), axis=0, keepdims=True).astype(BF16)
    chunks = along_z(jnp.broadcast_to(total, (16,) + total.shape[1:])).reshape(32, 16, 256)
    conv, w1_grad, w2_grad, embed_grad = vmem_call(
        finish_kernel,
        (
            jax.ShapeDtypeStruct((64, taps), BF16),
            jax.ShapeDtypeStruct((64, 1024), BF16),
            jax.ShapeDtypeStruct((64, channels), BF16),
            jax.ShapeDtypeStruct((3, channels), BF16),
        ),
        [],
        "finish",
        1 << 18,
        1 << 20,
    )(where, chunks, swap(chunks, "dp", 1))
    return (w1_grad, w2_grad, embed_grad, conv.T[None])


def solution(mesh):
    placed = (
        P(("dp", "shard"), None),
        P(("dp", "shard"), None),
        P(("dp", "shard")),
        P("shard", None),
        P(),
        P(),
        P(),
        P("section", None, "shard"),
        P(("dp", "shard"), None, None),
    )
    return jax.shard_map(
        body,
        mesh=mesh,
        in_specs=placed,
        out_specs=(
            P(("section", "shard"), None),
            P(("section", "shard"), None),
            P(),
            P("section", None, "shard"),
        ),
        check_vma=False,
    )
```

```python
import jax
import jax.numpy as jnp
from jax import lax
from jax.experimental import pallas as pl
from jax.experimental.pallas import tpu as pltpu
from jax.sharding import PartitionSpec as P

BOARD = 19
PITCH = 20
ROWS = 384
FRONT = 24
NORM_EPS = 1e-05
TAP_SHIFTS = [(a - 1) * PITCH + (b - 1) for a in range(3) for b in range(3)]
SMALL_VMEM = 8 * 1024 * 1024
TRUNK_VMEM = 24 * 1024 * 1024
F32 = jnp.float32
BF16 = jnp.bfloat16


def swap(block, axis, bits):
    return lax.ppermute(block, axis, [(i, i ^ bits) for i in range(lax.axis_size(axis))])


def turned(block, axis, distance):
    size = lax.axis_size(axis)
    return lax.ppermute(block, axis, [(i, (i + distance) % size) for i in range(size)])


def turned(block, axis, distance):
    size = lax.axis_size(axis)
    return lax.ppermute(block, axis, [(i, (i + distance) % size) for i in range(size)])


def exchange(blocks, axis):
    return lax.all_to_all(blocks, axis, 0, 0, tiled=True)


def nn(left, right):
    return lax.dot_general(left, right, (((1,), (0,)), ((), ())), preferred_element_type=F32)


def nt(left, right):
    return lax.dot_general(left, right, (((1,), (1,)), ((), ())), preferred_element_type=F32)


def tn(left, right):
    return lax.dot_general(left, right, (((0,), (0,)), ((), ())), preferred_element_type=F32)


def vmem_call(kernel, outs, scratch, name, flops, moved, vmem=SMALL_VMEM):
    spec = pl.BlockSpec(memory_space=pltpu.VMEM)

    def call(scalars, *arrays):
        return pl.pallas_call(
            kernel,
            out_shape=outs,
            in_specs=[pl.BlockSpec(memory_space=pltpu.SMEM)]
            + [spec] * len(arrays),
            out_specs=tuple(spec for _ in outs),
            scratch_shapes=scratch,
            compiler_params=pltpu.CompilerParams(vmem_limit_bytes=vmem),
            cost_estimate=pl.CostEstimate(flops=flops, bytes_accessed=moved, transcendentals=0),
            name=name,
        )(scalars, *arrays)

    return call


def encoder_kernel(where, context, w_first, w_second, preact, hidden, encoded):
    value = nn(context[...], w_first[...])
    preact[...] = value
    rounded = (value * (0.5 * (1.0 + lax.erf(value * 0.7071067811865476)))).astype(BF16)
    hidden[...] = rounded
    encoded[...] = nn(rounded, w_second[...])


def trunk_kernel(
    where, context, preact_in, hidden_in, encoded_in, w_second, embed, code_col, code_row, cotangent,
    mine, theirs,
    own, other,
    wt, patches, gt, normed, rscales, buf, grad, vectors,
):
    c = where[2]

    def block_rows(outer, inner, core):
        block = jnp.where(core == 0, inner, outer)
        shard = jnp.where(core == 0, outer, inner)
        return block, pl.ds(pl.multiple_of(shard * 64 + core * 32, 32), 32)

    def assemble(place, carry):
        outer, inner = place >> 2, place & 3
        for core, pieces in ((c, mine), (1 - c, theirs)):
            block, rows = block_rows(inner, outer, core)
            wt[block, rows, :] = pieces[outer, inner]
        return carry

    lax.fori_loop(0, 16, assemble, 0)

    point = lax.broadcasted_iota(jnp.int32, (ROWS, 1), 0)
    column = point - ((point * 3277) >> 16) * PITCH
    mask = jnp.where((column < BOARD) & (point < BOARD * PITCH), 1.0, 0.0).astype(F32)

    preact, hidden, encoded = preact_in[...], hidden_in[...], encoded_in[...]
    code = code_col[...]
    stone = embed[...].astype(F32)
    stones = jnp.where(code == 0, stone[0:1], jnp.where(code == 1, stone[1:2], stone[2:3]))
    start = (stones + encoded[0:1]).astype(BF16).astype(F32) * mask

    buf[0:FRONT, :] = jnp.zeros((FRONT, buf.shape[1]), F32)
    buf[FRONT + ROWS :, :] = jnp.zeros((FRONT, buf.shape[1]), F32)
    buf[FRONT : FRONT + ROWS, :] = start
    channels = start.shape[1]
    taps = wt.shape[2]

    def forward(block, carry):
        for tap, shift in enumerate(TAP_SHIFTS):
            patches[block, :, tap * channels : (tap + 1) * channels] = buf[
                FRONT + shift : FRONT + shift + ROWS, :
            ].astype(BF16)
        zconv = nt(patches[block], wt[block])
        rscale = lax.rsqrt(jnp.mean(zconv * zconv, axis=-1, keepdims=True) + NORM_EPS)
        value = zconv * rscale
        normed[block] = value
        rscales[block] = rscale
        stream = buf[FRONT : FRONT + ROWS, :] + value * jax.nn.sigmoid(value)
        buf[FRONT : FRONT + ROWS, :] = stream.astype(BF16).astype(F32) * mask
        return carry

    lax.fori_loop(0, 4, forward, 0)
    grad[...] = cotangent[...].astype(F32)

    def backward(step, carry):
        block = 3 - step
        value = normed[block]
        upper = grad[...]
        sigma = jax.nn.sigmoid(value)
        dnorm = upper * (sigma * (1.0 + value * (1.0 - sigma)))
        inner = jnp.mean(dnorm * value, axis=-1, keepdims=True)
        dconv = rscales[block] * (dnorm - value * inner)
        gt[block] = nn(dconv.T.astype(BF16), patches[block]).astype(BF16)
        buf[FRONT : FRONT + ROWS, :] = dconv.astype(BF16).astype(F32)
        total = upper
        for tap, shift in enumerate(TAP_SHIFTS):
            total += nn(
                buf[FRONT - shift : FRONT - shift + ROWS, :].astype(BF16),
                wt[block, :, tap * channels : (tap + 1) * channels],
            )
        grad[...] = total.astype(BF16).astype(F32) * mask
        return carry

    lax.fori_loop(0, 4, backward, 0)

    kind = lax.broadcasted_iota(jnp.int32, (16, ROWS), 0)
    codes = code_row[...]
    picked = ((kind < 3) & (codes == kind)) | ((kind == 3) & (codes < 3))
    sums = nn(jnp.where(picked, 1.0, 0.0).astype(BF16), grad[...].astype(BF16))
    rounded = sums.astype(BF16)
    cdf = 0.5 * (1.0 + lax.erf(preact * 0.7071067811865476))
    density = jnp.exp(-0.5 * preact * preact) * 0.3989422804014327
    pre_grad = (nt(rounded, w_second[...]) * (cdf + preact * density)).astype(BF16)
    parts = ((context[...], 0, 8), (hidden, 0, 8), (pre_grad, 3, 8))
    parts += tuple((rounded, row, 2) for row in (3, 0, 1, 2))
    place = 0
    for array, row, count in parts:
        for piece in range(count):
            vectors[place : place + 1, :] = array.astype(F32)[
                row : row + 1, piece * 128 : (piece + 1) * 128
            ]
            place += 1
    tail = vectors[...].astype(BF16)
    empty = jnp.zeros(tail.shape, BF16)

    def hand_out(place, carry):
        outer, inner = place >> 2, place & 3
        for core, pieces, first, second in ((c, own, tail, empty), (1 - c, other, empty, tail)):
            block, rows = block_rows(outer, inner, core)
            pieces[outer, inner, :, 0:taps] = gt[block, rows, :]
            pieces[outer, inner, :, taps : taps + 128] = first
            pieces[outer, inner, :, taps + 128 :] = second
        return carry

    lax.fori_loop(0, 16, hand_out, 0)


def fold_kernel(where, pieces, out):
    taps = pieces.shape[3] - 256
    for inner in range(4):
        total = pieces[0, inner, :, 0:taps].astype(F32)
        for source in range(1, 4):
            total += pieces[source, inner, :, 0:taps].astype(F32)
        out[inner, :, 0:taps] = total.astype(BF16)
        for source in range(4):
            lane = taps + source * 256
            out[inner, :, lane : lane + 256] = pieces[source, inner, :, taps:]


def pack_kernel(where, pieces, out, vectors, product, stones):
    first = where[0] * 256 + where[1] * 64 + where[2] * 32
    row = first // 128
    rows = pl.ds(pl.multiple_of(first - row * 128, 32), 32)
    taps = pieces.shape[2] - 1024
    for state in range(32):
        lane = taps + state % 8 * 128
        vectors[state * 32 : (state + 1) * 32, :] = pieces[state // 8, :, lane : lane + 128].astype(F32)

    def of_states(place):
        return vectors[pl.ds(place, 32, stride=32), :]

    context = of_states(row).astype(BF16)
    hidden = of_states(row + 8).astype(BF16)
    for piece in range(8):
        lanes = slice(piece * 128, (piece + 1) * 128)
        product[:, lanes] = tn(context, of_states(16 + piece).astype(BF16))
    for piece in range(2):
        lanes = slice(1024 + piece * 128, 1024 + (piece + 1) * 128)
        product[:, lanes] = tn(hidden, of_states(24 + piece).astype(BF16))
    stones[...] = jnp.zeros(stones.shape, F32)
    for piece in range(6):
        v, half = divmod(piece, 2)
        stones[v : v + 1, half * 128 : (half + 1) * 128] = jnp.sum(
            of_states(26 + piece), axis=0, keepdims=True
        )
    for column in range(taps // 256):
        lanes = slice(column * 256, (column + 1) * 256)
        block = pieces[0, :, lanes].astype(F32)
        for piece in range(1, 4):
            block += pieces[piece, :, lanes].astype(F32)
        out[2 * column] = block[0:16].astype(BF16)
        out[2 * column + 1] = block[16:32].astype(BF16)
    for column in range(5):
        block = product[rows, column * 256 : (column + 1) * 256]
        place = 2 * (taps // 256 + column)
        out[place] = block[0:16].astype(BF16)
        out[place + 1] = block[16:32].astype(BF16)
    out[28] = stones[...].astype(BF16)
    for place in (29, 30, 31):
        out[place] = jnp.zeros(out.shape[1:], BF16)


def finish_kernel(where, mine, theirs, conv, first, second, stones):
    c = where[2]
    for out, start in ((conv, 0), (first, conv.shape[1]), (second, conv.shape[1] + first.shape[1])):
        for column in range(out.shape[1] // 256):
            for half in range(2):
                for core, pieces in ((c, mine), (1 - c, theirs)):
                    rows = pl.ds(pl.multiple_of(core * 32 + half * 16, 16), 16)
                    out[rows, column * 256 : (column + 1) * 256] = (
                        pieces[2 * (start // 256 + column) + half].astype(F32) * (1.0 / 512.0)
                    ).astype(BF16)
    stones[...] = (mine[28].astype(F32) * (1.0 / 512.0))[0:3].astype(BF16)


def body(boards, neighbours, counts, database, w_first, w_second, embed, conv_weight, cotangent):
    h = lax.axis_index("shard")
    s = lax.axis_index("section")
    dp = lax.axis_index("dp")
    c = dp % 2
    where = jnp.stack([s, h, c]).astype(jnp.int32)
    channels = embed.shape[1]
    taps = conv_weight.shape[1]

    along_x, along_y = [], []
    for place in range(lax.axis_size("dp")):
        lines = ([[place * 16 + i * 4 + j for j in range(4)] for i in range(4)],
                 [[place * 16 + i * 4 + j for i in range(4)] for j in range(4)])
        along_x += lines[place % 2]
        along_y += lines[1 - place % 2]

    def ring(blocks, groups):
        return lax.all_to_all(
            blocks, ("dp", "section", "shard"), 0, 0, axis_index_groups=groups, tiled=True
        )

    slots = neighbours.shape[1]
    asked = jnp.concatenate([neighbours, counts[:, None]], axis=1)
    state = lax.broadcasted_iota(jnp.int32, asked.shape, 0)
    asked = jnp.sum(jnp.where(state == s, asked, 0), axis=0, keepdims=True)
    count = asked[:, slots]
    asked = jnp.broadcast_to(jnp.pad(asked, ((0, 0), (0, 127 - slots))), (8, 128))
    asked = lax.all_gather(asked[None], "shard", axis=0, tiled=True)[:, 0, : slots + 1]

    unit = lax.dynamic_slice_in_dim(conv_weight[0].T, c * 32, 32, 0)
    unit = jnp.broadcast_to(unit[None], (4,) + unit.shape)
    mine = ring(unit, along_x)
    asked, mine = lax.optimization_barrier((asked, mine))
    mine = ring(jnp.broadcast_to(mine[None], (4,) + mine.shape), along_y)

    live = lax.broadcasted_iota(jnp.int32, (4, slots), 1) < asked[:, slots:]
    stored = database.shape[0]
    positions = lax.broadcasted_iota(jnp.int32, (1, 1, stored), 2) + h * stored
    hits = (asked[:, :slots, None] == positions) & live[:, :, None]
    picks = jnp.sum(hits.astype(F32), axis=1).astype(BF16)
    partial = jnp.dot(picks, database, preferred_element_type=F32)
    summed = lax.dynamic_slice_in_dim(partial, h, 1, 0)
    for d in (1, 2, 3):
        piece = lax.dynamic_slice_in_dim(partial, (h + 4 - d) % 4, 1, 0)
        summed = summed + turned(piece, "shard", -d)
    context = (summed / jnp.maximum(count, 1).astype(F32)[:, None]).astype(BF16)
    context = jnp.broadcast_to(context, (16, context.shape[1]))

    board = lax.dynamic_index_in_dim(boards, s, 0, keepdims=False).reshape(BOARD, BOARD)
    code = jnp.pad(board, ((0, 0), (0, 1)), constant_values=3).reshape(-1)
    code = jnp.pad(code, (0, ROWS - BOARD * PITCH), constant_values=3)
    upper = lax.dynamic_index_in_dim(cotangent, s, 0, keepdims=False)
    upper = jnp.pad(upper.reshape(BOARD, BOARD, channels), ((0, 0), (0, 1), (0, 0)))
    upper = jnp.pad(upper.reshape(-1, channels), ((0, ROWS - BOARD * PITCH), (0, 0)))

    mine, context, upper = lax.optimization_barrier((mine, context, upper))
    theirs = swap(mine, "dp", 1)
    width = context.shape[1]
    preact, hidden, encoded = vmem_call(
        encoder_kernel,
        (
            jax.ShapeDtypeStruct((16, width), F32),
            jax.ShapeDtypeStruct((16, width), BF16),
            jax.ShapeDtypeStruct((16, channels), F32),
        ),
        [],
        "encoder",
        2 * 16 * width * (width + channels),
        3 << 20,
    )(where, context, w_first, w_second)
    part = jax.ShapeDtypeStruct((4, 4, 32, taps + 256), BF16)
    own, other = vmem_call(
        trunk_kernel,
        (part, part),
        [
            pltpu.VMEM((4, channels, taps), BF16),
            pltpu.VMEM((4, ROWS, taps), BF16),
            pltpu.VMEM((4, channels, taps), BF16),
            pltpu.VMEM((4, ROWS, channels), F32),
            pltpu.VMEM((4, ROWS, 1), F32),
            pltpu.VMEM((2 * FRONT + ROWS, channels), F32),
            pltpu.VMEM((ROWS, channels), F32),
            pltpu.VMEM((32, 128), F32),
        ],
        "trunk",
        12 * 2 * ROWS * taps * channels,
        16 << 20,
        vmem=TRUNK_VMEM,
    )(
        where, context, preact, hidden, encoded, w_second, embed,
        code[:, None], code[None, :], upper, mine, theirs,
    )

    pieces = ring((own.astype(F32) + swap(other, "dp", 1).astype(F32)).astype(BF16), along_x)
    (pieces,) = vmem_call(
        fold_kernel,
        (jax.ShapeDtypeStruct((4, 32, taps + 1024), BF16),),
        [],
        "fold",
        pieces.size,
        3 << 20,
    )(where, pieces)
    pieces = ring(pieces, along_y)
    (chunks,) = vmem_call(
        pack_kernel,
        (jax.ShapeDtypeStruct((32, 16, 256), BF16),),
        [
            pltpu.VMEM((1024, 128), F32),
            pltpu.VMEM((128, 1280), F32),
            pltpu.VMEM((16, 256), F32),
        ],
        "pack",
        4 * 32 * 128 * 1280,
        3 << 20,
    )(where, pieces)

    line = [[2 * i + core for i in range(lax.axis_size("dp") // 2)] for core in (0, 1)]

    def along_z(blocks):
        return lax.all_to_all(blocks, "dp", 0, 0, axis_index_groups=line, tiled=True)

    total = along_z(chunks.reshape(16, 2, 16, 256))
    total = jnp.sum(total.astype(F32), axis=0, keepdims=True).astype(BF16)
    chunks = along_z(jnp.broadcast_to(total, (16,) + total.shape[1:])).reshape(32, 16, 256)
    conv, w1_grad, w2_grad, embed_grad = vmem_call(
        finish_kernel,
        (
            jax.ShapeDtypeStruct((64, taps), BF16),
            jax.ShapeDtypeStruct((64, 1024), BF16),
            jax.ShapeDtypeStruct((64, channels), BF16),
            jax.ShapeDtypeStruct((3, channels), BF16),
        ),
        [],
        "finish",
        1 << 18,
        1 << 20,
    )(where, chunks, swap(chunks, "dp", 1))
    return (w1_grad, w2_grad, embed_grad, conv.T[None])


def solution(mesh):
    placed = (
        P(("dp", "shard"), None),
        P(("dp", "shard"), None),
        P(("dp", "shard")),
        P("shard", None),
        P(),
        P(),
        P(),
        P("section", None, "shard"),
        P(("dp", "shard"), None, None),
    )
    return jax.shard_map(
        body,
        mesh=mesh,
        in_specs=placed,
        out_specs=(
            P(("section", "shard"), None),
            P(("section", "shard"), None),
            P(),
            P("section", None, "shard"),
        ),
        check_vma=False,
    )
```

```python
import jax
import jax.numpy as jnp
from jax import lax
from jax.experimental import pallas as pl
from jax.experimental.pallas import tpu as pltpu
from jax.sharding import PartitionSpec as P

BOARD = 19
PITCH = 20
ROWS = 384
FRONT = 24
NORM_EPS = 1e-05
TAP_SHIFTS = [(a - 1) * PITCH + (b - 1) for a in range(3) for b in range(3)]
VMEM_BYTES = 34 * 1024 * 1024
F32 = jnp.float32
BF16 = jnp.bfloat16


def swap(block, axis, bits):
    return lax.ppermute(block, axis, [(i, i ^ bits) for i in range(lax.axis_size(axis))])


def nn(left, right):
    return lax.dot_general(left, right, (((1,), (0,)), ((), ())), preferred_element_type=F32)


def nt(left, right):
    return lax.dot_general(left, right, (((1,), (1,)), ((), ())), preferred_element_type=F32)


def tn(left, right):
    return lax.dot_general(left, right, (((0,), (0,)), ((), ())), preferred_element_type=F32)


def vmem_call(kernel, outs, scratch, name, flops, moved):
    spec = pl.BlockSpec(memory_space=pltpu.VMEM)

    def call(scalars, *arrays):
        return pl.pallas_call(
            kernel,
            out_shape=outs,
            in_specs=[pl.BlockSpec(memory_space=pltpu.SMEM)]
            + [spec] * len(arrays),
            out_specs=tuple(spec for _ in outs),
            scratch_shapes=scratch,
            compiler_params=pltpu.CompilerParams(vmem_limit_bytes=VMEM_BYTES),
            cost_estimate=pl.CostEstimate(flops=flops, bytes_accessed=moved, transcendentals=0),
            name=name,
        )(scalars, *arrays)

    return call


def encoder_kernel(where, context, w_first, w_second, preact, hidden, encoded):
    value = nn(context[...], w_first[...])
    preact[...] = value
    rounded = (value * (0.5 * (1.0 + lax.erf(value * 0.7071067811865476)))).astype(BF16)
    hidden[...] = rounded
    encoded[...] = nn(rounded, w_second[...])


def trunk_kernel(
    where, context, preact_in, hidden_in, encoded_in, w_second, embed, code_col, code_row, cotangent,
    mine, theirs,
    own, other,
    wt, patches, gt, normed, rscales, buf, grad, vectors,
):
    c = where[2]

    def block_rows(outer, inner, core):
        block = jnp.where(core == 0, inner, outer)
        shard = jnp.where(core == 0, outer, inner)
        return block, pl.ds(pl.multiple_of(shard * 64 + core * 32, 32), 32)

    def assemble(place, carry):
        outer, inner = place >> 2, place & 3
        for core, pieces in ((c, mine), (1 - c, theirs)):
            block, rows = block_rows(inner, outer, core)
            wt[block, rows, :] = pieces[outer, inner]
        return carry

    lax.fori_loop(0, 16, assemble, 0)

    point = lax.broadcasted_iota(jnp.int32, (ROWS, 1), 0)
    column = point - ((point * 3277) >> 16) * PITCH
    mask = jnp.where((column < BOARD) & (point < BOARD * PITCH), 1.0, 0.0).astype(F32)

    preact, hidden, encoded = preact_in[...], hidden_in[...], encoded_in[...]
    code = code_col[...]
    stone = embed[...].astype(F32)
    stones = jnp.where(code == 0, stone[0:1], jnp.where(code == 1, stone[1:2], stone[2:3]))
    start = (stones + encoded[0:1]).astype(BF16).astype(F32) * mask

    buf[0:FRONT, :] = jnp.zeros((FRONT, buf.shape[1]), F32)
    buf[FRONT + ROWS :, :] = jnp.zeros((FRONT, buf.shape[1]), F32)
    buf[FRONT : FRONT + ROWS, :] = start
    channels = start.shape[1]
    taps = wt.shape[2]

    def forward(block, carry):
        for tap, shift in enumerate(TAP_SHIFTS):
            patches[block, :, tap * channels : (tap + 1) * channels] = buf[
                FRONT + shift : FRONT + shift + ROWS, :
            ].astype(BF16)
        zconv = nt(patches[block], wt[block])
        rscale = lax.rsqrt(jnp.mean(zconv * zconv, axis=-1, keepdims=True) + NORM_EPS)
        value = zconv * rscale
        normed[block] = value
        rscales[block] = rscale
        stream = buf[FRONT : FRONT + ROWS, :] + value * jax.nn.sigmoid(value)
        buf[FRONT : FRONT + ROWS, :] = stream.astype(BF16).astype(F32) * mask
        return carry

    lax.fori_loop(0, 4, forward, 0)
    grad[...] = cotangent[...].astype(F32)

    def backward(step, carry):
        block = 3 - step
        value = normed[block]
        upper = grad[...]
        sigma = jax.nn.sigmoid(value)
        dnorm = upper * (sigma * (1.0 + value * (1.0 - sigma)))
        inner = jnp.mean(dnorm * value, axis=-1, keepdims=True)
        dconv = rscales[block] * (dnorm - value * inner)
        gt[block] = nn(dconv.T.astype(BF16), patches[block]).astype(BF16)
        buf[FRONT : FRONT + ROWS, :] = dconv.astype(BF16).astype(F32)
        total = upper
        for tap, shift in enumerate(TAP_SHIFTS):
            total += nn(
                buf[FRONT - shift : FRONT - shift + ROWS, :].astype(BF16),
                wt[block, :, tap * channels : (tap + 1) * channels],
            )
        grad[...] = total.astype(BF16).astype(F32) * mask
        return carry

    lax.fori_loop(0, 4, backward, 0)

    kind = lax.broadcasted_iota(jnp.int32, (16, ROWS), 0)
    codes = code_row[...]
    picked = ((kind < 3) & (codes == kind)) | ((kind == 3) & (codes < 3))
    sums = nn(jnp.where(picked, 1.0, 0.0).astype(BF16), grad[...].astype(BF16))
    rounded = sums.astype(BF16)
    cdf = 0.5 * (1.0 + lax.erf(preact * 0.7071067811865476))
    density = jnp.exp(-0.5 * preact * preact) * 0.3989422804014327
    pre_grad = (nt(rounded, w_second[...]) * (cdf + preact * density)).astype(BF16)
    parts = ((context[...], 0, 8), (hidden, 0, 8), (pre_grad, 3, 8))
    parts += tuple((rounded, row, 2) for row in (3, 0, 1, 2))
    place = 0
    for array, row, count in parts:
        for piece in range(count):
            vectors[place : place + 1, :] = array.astype(F32)[
                row : row + 1, piece * 128 : (piece + 1) * 128
            ]
            place += 1
    tail = vectors[...].astype(BF16)
    empty = jnp.zeros(tail.shape, BF16)

    def hand_out(place, carry):
        outer, inner = place >> 2, place & 3
        for core, pieces, first, second in ((c, own, tail, empty), (1 - c, other, empty, tail)):
            block, rows = block_rows(outer, inner, core)
            pieces[outer, inner, :, 0:taps] = gt[block, rows, :]
            pieces[outer, inner, :, taps : taps + 128] = first
            pieces[outer, inner, :, taps + 128 :] = second
        return carry

    lax.fori_loop(0, 16, hand_out, 0)


def fold_kernel(where, pieces, out):
    taps = pieces.shape[3] - 256
    for inner in range(4):
        total = pieces[0, inner, :, 0:taps].astype(F32)
        for source in range(1, 4):
            total += pieces[source, inner, :, 0:taps].astype(F32)
        out[inner, :, 0:taps] = total.astype(BF16)
        for source in range(4):
            lane = taps + source * 256
            out[inner, :, lane : lane + 256] = pieces[source, inner, :, taps:]


def pack_kernel(where, pieces, out, vectors, product, stones):
    first = where[0] * 256 + where[1] * 64 + where[2] * 32
    row = first // 128
    rows = pl.ds(pl.multiple_of(first - row * 128, 32), 32)
    taps = pieces.shape[2] - 1024
    for state in range(32):
        lane = taps + state % 8 * 128
        vectors[state * 32 : (state + 1) * 32, :] = pieces[state // 8, :, lane : lane + 128].astype(F32)

    def of_states(place):
        return vectors[pl.ds(place, 32, stride=32), :]

    context = of_states(row).astype(BF16)
    hidden = of_states(row + 8).astype(BF16)
    for piece in range(8):
        lanes = slice(piece * 128, (piece + 1) * 128)
        product[:, lanes] = tn(context, of_states(16 + piece).astype(BF16))
    for piece in range(2):
        lanes = slice(1024 + piece * 128, 1024 + (piece + 1) * 128)
        product[:, lanes] = tn(hidden, of_states(24 + piece).astype(BF16))
    stones[...] = jnp.zeros(stones.shape, F32)
    for piece in range(6):
        v, half = divmod(piece, 2)
        stones[v : v + 1, half * 128 : (half + 1) * 128] = jnp.sum(
            of_states(26 + piece), axis=0, keepdims=True
        )
    for column in range(taps // 256):
        lanes = slice(column * 256, (column + 1) * 256)
        block = pieces[0, :, lanes].astype(F32)
        for piece in range(1, 4):
            block += pieces[piece, :, lanes].astype(F32)
        out[2 * column] = block[0:16].astype(BF16)
        out[2 * column + 1] = block[16:32].astype(BF16)
    for column in range(5):
        block = product[rows, column * 256 : (column + 1) * 256]
        place = 2 * (taps // 256 + column)
        out[place] = block[0:16].astype(BF16)
        out[place + 1] = block[16:32].astype(BF16)
    out[28] = stones[...].astype(BF16)
    for place in (29, 30, 31):
        out[place] = jnp.zeros(out.shape[1:], BF16)


def finish_kernel(where, mine, theirs, conv, first, second, stones):
    c = where[2]
    for out, start in ((conv, 0), (first, conv.shape[1]), (second, conv.shape[1] + first.shape[1])):
        for column in range(out.shape[1] // 256):
            for half in range(2):
                for core, pieces in ((c, mine), (1 - c, theirs)):
                    rows = pl.ds(pl.multiple_of(core * 32 + half * 16, 16), 16)
                    out[rows, column * 256 : (column + 1) * 256] = (
                        pieces[2 * (start // 256 + column) + half].astype(F32) * (1.0 / 512.0)
                    ).astype(BF16)
    stones[...] = (mine[28].astype(F32) * (1.0 / 512.0))[0:3].astype(BF16)


def body(boards, neighbours, counts, database, w_first, w_second, embed, conv_weight, cotangent):
    h = lax.axis_index("shard")
    s = lax.axis_index("section")
    dp = lax.axis_index("dp")
    c = dp % 2
    where = jnp.stack([s, h, c]).astype(jnp.int32)
    channels = embed.shape[1]
    taps = conv_weight.shape[1]

    along_x, along_y = [], []
    for place in range(lax.axis_size("dp")):
        lines = ([[place * 16 + i * 4 + j for j in range(4)] for i in range(4)],
                 [[place * 16 + i * 4 + j for i in range(4)] for j in range(4)])
        along_x += lines[place % 2]
        along_y += lines[1 - place % 2]

    def ring(blocks, groups):
        return lax.all_to_all(
            blocks, ("dp", "section", "shard"), 0, 0, axis_index_groups=groups, tiled=True
        )

    slots = neighbours.shape[1]
    asked = jnp.concatenate([neighbours, counts[:, None]], axis=1)
    state = lax.broadcasted_iota(jnp.int32, asked.shape, 0)
    asked = jnp.sum(jnp.where(state == s, asked, 0), axis=0, keepdims=True)
    count = asked[:, slots]
    asked = jnp.concatenate([asked, swap(asked, "shard", 1)])
    asked = jnp.concatenate([asked, swap(asked, "shard", 3)])

    unit = lax.dynamic_slice_in_dim(conv_weight[0].T, c * 32, 32, 0)
    unit = jnp.broadcast_to(unit[None], (4,) + unit.shape)
    mine = ring(unit, along_x)
    asked, mine = lax.optimization_barrier((asked, mine))
    mine = ring(jnp.broadcast_to(mine[None], (4,) + mine.shape), along_y)

    live = lax.broadcasted_iota(jnp.int32, (4, slots), 1) < asked[:, slots:]
    stored = database.shape[0]
    positions = lax.broadcasted_iota(jnp.int32, (1, 1, stored), 2) + h * stored
    hits = (asked[:, :slots, None] == positions) & live[:, :, None]
    picks = jnp.sum(hits.astype(F32), axis=1).astype(BF16)
    partial = jnp.dot(picks, database, preferred_element_type=F32)
    summed = partial[0:1]
    for place, bits in ((1, 1), (2, 3), (3, 2)):
        summed = summed + swap(partial[place : place + 1], "shard", bits)
    context = (summed / jnp.maximum(count, 1).astype(F32)[:, None]).astype(BF16)
    context = jnp.broadcast_to(context, (16, context.shape[1]))

    board = lax.dynamic_index_in_dim(boards, s, 0, keepdims=False).reshape(BOARD, BOARD)
    code = jnp.pad(board, ((0, 0), (0, 1)), constant_values=3).reshape(-1)
    code = jnp.pad(code, (0, ROWS - BOARD * PITCH), constant_values=3)
    upper = lax.dynamic_index_in_dim(cotangent, s, 0, keepdims=False)
    upper = jnp.pad(upper.reshape(BOARD, BOARD, channels), ((0, 0), (0, 1), (0, 0)))
    upper = jnp.pad(upper.reshape(-1, channels), ((0, ROWS - BOARD * PITCH), (0, 0)))

    mine, context, upper = lax.optimization_barrier((mine, context, upper))
    theirs = swap(mine, "dp", 1)
    width = context.shape[1]
    preact, hidden, encoded = vmem_call(
        encoder_kernel,
        (
            jax.ShapeDtypeStruct((16, width), F32),
            jax.ShapeDtypeStruct((16, width), BF16),
            jax.ShapeDtypeStruct((16, channels), F32),
        ),
        [],
        "encoder",
        2 * 16 * width * (width + channels),
        3 << 20,
    )(where, context, w_first, w_second)
    part = jax.ShapeDtypeStruct((4, 4, 32, taps + 256), BF16)
    own, other = vmem_call(
        trunk_kernel,
        (part, part),
        [
            pltpu.VMEM((4, channels, taps), BF16),
            pltpu.VMEM((4, ROWS, taps), BF16),
            pltpu.VMEM((4, channels, taps), BF16),
            pltpu.VMEM((4, ROWS, channels), F32),
            pltpu.VMEM((4, ROWS, 1), F32),
            pltpu.VMEM((2 * FRONT + ROWS, channels), F32),
            pltpu.VMEM((ROWS, channels), F32),
            pltpu.VMEM((32, 128), F32),
        ],
        "trunk",
        12 * 2 * ROWS * taps * channels,
        16 << 20,
    )(
        where, context, preact, hidden, encoded, w_second, embed,
        code[:, None], code[None, :], upper, mine, theirs,
    )

    pieces = ring((own.astype(F32) + swap(other, "dp", 1).astype(F32)).astype(BF16), along_x)
    (pieces,) = vmem_call(
        fold_kernel,
        (jax.ShapeDtypeStruct((4, 32, taps + 1024), BF16),),
        [],
        "fold",
        pieces.size,
        3 << 20,
    )(where, pieces)
    pieces = ring(pieces, along_y)
    (chunks,) = vmem_call(
        pack_kernel,
        (jax.ShapeDtypeStruct((32, 16, 256), BF16),),
        [
            pltpu.VMEM((1024, 128), F32),
            pltpu.VMEM((128, 1280), F32),
            pltpu.VMEM((16, 256), F32),
        ],
        "pack",
        4 * 32 * 128 * 1280,
        3 << 20,
    )(where, pieces)

    line = [[2 * i + core for i in range(lax.axis_size("dp") // 2)] for core in (0, 1)]

    def along_z(blocks):
        return lax.all_to_all(blocks, "dp", 0, 0, axis_index_groups=line, tiled=True)

    total = along_z(chunks.reshape(16, 2, 16, 256))
    total = jnp.sum(total.astype(F32), axis=0, keepdims=True).astype(BF16)
    chunks = along_z(jnp.broadcast_to(total, (16,) + total.shape[1:])).reshape(32, 16, 256)
    conv, w1_grad, w2_grad, embed_grad = vmem_call(
        finish_kernel,
        (
            jax.ShapeDtypeStruct((64, taps), BF16),
            jax.ShapeDtypeStruct((64, 1024), BF16),
            jax.ShapeDtypeStruct((64, channels), BF16),
            jax.ShapeDtypeStruct((3, channels), BF16),
        ),
        [],
        "finish",
        1 << 18,
        1 << 20,
    )(where, chunks, swap(chunks, "dp", 1))
    return (w1_grad, w2_grad, embed_grad, conv.T[None])


def solution(mesh):
    placed = (
        P(("dp", "shard"), None),
        P(("dp", "shard"), None),
        P(("dp", "shard")),
        P("shard", None),
        P(),
        P(),
        P(),
        P("section", None, "shard"),
        P(("dp", "shard"), None, None),
    )
    return jax.shard_map(
        body,
        mesh=mesh,
        in_specs=placed,
        out_specs=(
            P(("section", "shard"), None),
            P(("section", "shard"), None),
            P(),
            P("section", None, "shard"),
        ),
        check_vma=False,
    )
```
